32 devices in a mesh: parts: 2 (over x), blk: 16 (over z, y, core).
Axes of the slice: x: 2, y: 2, z: 4, core: 2. Of those that a mesh axis runs over, the one named last changes fastest.
Arguments:
- embeddings: float32 [32768, 768], P(('parts', 'blk')), parts along dimension 0
- cluster_id: int32 [32768], P(('parts', 'blk')), parts along dimension 0, may hold values from -1 to 15, as said below
Outputs:
- dup_score: float32 [32768], P(('parts', 'blk')), parts along dimension 0
The draws below stay inside these ranges and needn't reach their ends.
There are 2 independent parts, one for each index of `parts`. The reference program is written for one: setup_inputs(seed, part) draws one part's arguments, and reference() takes and returns one part's arrays. A program takes and returns all parts, laid end to end along the dimension named above; each array names one. Nothing has to cross between parts.
Inputs may be any that keep to these rules, and one draw needn't show every extreme that they name: `cluster_id`: row slots are laid out as 16 consecutive blocks of 1024. A row of cluster c lies in block (c + o) modulo 16 for some o in 0 to 7. Each block holds live rows first and padding slots (-1) after them; at least 64 rows of each block are live.
All inputs are finite; a program needn't handle non-finite values.
Results may differ from the reference program's by a relative error of at most 0.0003.
Values may be sent and summed in bfloat16 or wider, within the bound.
No kernel may reach another device: no remote copies, remote signals or barrier semaphores. Data moves between devices by JAX's collectives and lax.ppermute only.
A program may use at most 64 MiB of HBM per device.

```python
import jax
import jax.numpy as jnp
from jax import lax

W = 768
TILE = 256
TILES_DEV = 4
CL_DEV = 1
SPAN = 8
ROWS_DEV = 1024
ROWS = 16384
CLUSTERS = 16


def layout_ids(key):
    key = jax.random.fold_in(key, 101)
    key_offset, key_slot, key_tiles, key_fill = jax.random.split(key, 4)
    blocks_count = ROWS // ROWS_DEV
    rows = jnp.arange(ROWS, dtype=jnp.int32)
    block = rows // ROWS_DEV
    local = rows % ROWS_DEV
    offset = jax.random.randint(key_offset, (ROWS,), 0, SPAN, dtype=jnp.int32)
    slot = jax.random.randint(key_slot, (ROWS,), 0, CL_DEV, dtype=jnp.int32)
    home = (block - offset) % blocks_count
    ids = home * CL_DEV + slot
    live_tiles = jax.random.randint(key_tiles, (blocks_count,), 1, TILES_DEV + 1, dtype=jnp.int32)
    fill = jax.random.randint(key_fill, (blocks_count,), TILE // 4, TILE + 1, dtype=jnp.int32)
    tile = local // TILE
    within = local % TILE
    last = live_tiles[block] - 1
    live = (tile < last) | (tile == last) & (within < fill[block])
    return jnp.where(live, ids, -1).astype(jnp.int32)


def draw_cluster_id(key, part):
    return layout_ids(key)


def draw_embeddings(key, part):
    ids = layout_ids(key)
    key = jax.random.fold_in(key, 7)
    key_centre = jax.random.fold_in(key, 0)
    key_weight = jax.random.fold_in(key, 1)
    key_noise = jax.random.fold_in(key, 2)
    key_twin = jax.random.fold_in(key, 4)
    key_own = jax.random.fold_in(key, 5)
    centres = jax.random.normal(key_centre, (CLUSTERS, W), jnp.float32)
    weight = jax.random.uniform(key_weight, (ROWS, 1), jnp.float32, 0.3, 1.6)
    picked = centres[jnp.maximum(ids, 0)]
    groups = max(SPAN * ROWS_DEV // (4 * CL_DEV), 1)
    member = jax.random.randint(key_twin, (ROWS,), 0, groups, dtype=jnp.int32)
    tag = (jnp.maximum(ids, 0) * groups + member).astype(jnp.int32)
    shared = jax.vmap(lambda t: jax.random.normal(jax.random.fold_in(key_noise, t), (W,), jnp.float32))(tag)
    own = 0.3 * jax.random.normal(key_own, (ROWS, W), jnp.float32)
    return (weight * picked + shared + own).astype(jnp.float32)


def setup_inputs(seed: int = 0, part: int = 0) -> dict:
    seeds = jax.random.split(jax.random.key(seed), 3)
    part_splits = jax.random.split(jax.random.fold_in(seeds[2], part), 3)
    embeddings = draw_embeddings(jax.random.fold_in(jax.random.fold_in(seeds[2], part), 71), part)
    cluster_id = draw_cluster_id(jax.random.fold_in(jax.random.fold_in(seeds[2], part), 71), part)
    return {"embeddings": embeddings, "cluster_id": cluster_id}


def block_max(left, left_id, right, right_id, same_block):
    scores = lax.dot_general(left, right, (((1,), (1,)), ((), ())), preferred_element_type=jnp.float32)
    match = (left_id[:, None] == right_id[None, :]) & (left_id[:, None] >= 0)
    if same_block:
        count = left.shape[0]
        match = match & (jnp.arange(count)[:, None] != jnp.arange(count)[None, :])
    masked = jnp.where(match, scores, jnp.float32(-1.0))
    return (lax.optimization_barrier(jnp.max(masked, axis=1)), lax.optimization_barrier(jnp.max(masked, axis=0)))

def reference(embeddings, cluster_id):
    scale = lax.rsqrt(lax.optimization_barrier(jnp.sum(embeddings * embeddings, axis=1, keepdims=True)) + 1e-06)
    normed = (embeddings * scale).astype(jnp.bfloat16)
    blocks_count = ROWS // ROWS_DEV
    blocks = normed.reshape(blocks_count, ROWS_DEV, W)
    block_ids = cluster_id.reshape(blocks_count, ROWS_DEV)
    best = jnp.full((blocks_count, ROWS_DEV), -1.0, jnp.float32)

    def one_block(index, best):
        home = jnp.asarray(index).astype(jnp.int32)
        mine = lax.dynamic_index_in_dim(blocks, home, 0, False)
        mine_id = lax.dynamic_index_in_dim(block_ids, home, 0, False)
        for offset in range(SPAN):
            other = ((home + offset) % blocks_count).astype(jnp.int32)
            theirs = lax.dynamic_index_in_dim(blocks, other, 0, False)
            theirs_id = lax.dynamic_index_in_dim(block_ids, other, 0, False)
            row_best, col_best = block_max(mine, mine_id, theirs, theirs_id, offset == 0)
            current = lax.dynamic_index_in_dim(best, home, 0, False)
            best = lax.dynamic_update_index_in_dim(best, jnp.maximum(current, row_best), home, 0)
            current = lax.dynamic_index_in_dim(best, other, 0, False)
            best = lax.dynamic_update_index_in_dim(best, jnp.maximum(current, col_best), other, 0)
        return best
    best = lax.fori_loop(0, blocks_count, one_block, best)
    return best.reshape(ROWS)
```

```python
import functools

import jax
import jax.numpy as jnp
from jax import lax
from jax.experimental import pallas as pl
from jax.experimental.pallas import tpu as pltpu
from jax.sharding import PartitionSpec as P

SPAN = 8
HOME = 4
ROOM = 176
LANES = 128
EMPTY = 2.0
VMEM_BYTES = 48 * 1024 * 1024


def shifted(block, axis, distance):
    size = lax.axis_size(axis)
    route = [(i, (i + distance) % size) for i in range(size)]
    return lax.ppermute(block, axis, route)


def block_max(left, left_id, right, right_id, same_block):
    scores = lax.dot_general(
        left, right, (((1,), (1,)), ((), ())), preferred_element_type=jnp.float32
    )
    match = (left_id[:, None] == right_id[None, :]) & (left_id[:, None] >= 0)
    if same_block:
        count = left.shape[0]
        match = match & (jnp.arange(count)[:, None] != jnp.arange(count)[None, :])
    masked = jnp.where(match, scores, jnp.float32(-1.0))
    return (jnp.max(masked, axis=1), jnp.max(masked, axis=0))


def by_ring(embeddings, cluster_id):
    scale = lax.rsqrt(jnp.sum(embeddings * embeddings, axis=1, keepdims=True) + 1e-06)
    normed = (embeddings * scale).astype(jnp.bfloat16)
    best, unused_cols = block_max(normed, cluster_id, normed, cluster_id, True)
    visitor = (normed, cluster_id)
    for offset in range(1, SPAN):
        visitor = (shifted(visitor[0], "blk", 1), shifted(visitor[1], "blk", 1))
        row_best, col_best = block_max(normed, cluster_id, visitor[0], visitor[1], False)
        returned = shifted(col_best, "blk", -offset)
        best = jnp.maximum(best, jnp.maximum(row_best, returned))
    return best


def pack_kernel(blocks, emb_ref, id_ref, *refs):
    out_refs, (offset_ref, rank_ref, over_ref) = refs[:SPAN], refs[SPAN : SPAN + 3]
    raw, normed, arrived = refs[SPAN + 3 :]
    rows, width = normed.shape
    segments = rows // LANES
    copies = []
    for s in range(segments):
        part = pl.ds(s * LANES, LANES)
        copies.append(pltpu.make_async_copy(emb_ref.at[part], raw.at[part], arrived.at[s]))
        copies[-1].start()

    me = lax.axis_index("blk")
    ids = id_ref[...]
    offset = lax.rem(me - ids + 2 * blocks, blocks)
    offset = jnp.where(ids >= 0, offset, SPAN)
    member = [jnp.where(offset == o, 1.0, 0.0) for o in range(SPAN)]
    stacked = jnp.concatenate(member, axis=0).astype(jnp.bfloat16)
    before = lax.broadcasted_iota(jnp.int32, (LANES, LANES), 0) < lax.broadcasted_iota(
        jnp.int32, (LANES, LANES), 1
    )
    before = jnp.where(before, 1.0, 0.0).astype(jnp.bfloat16)
    ones = jnp.ones((LANES, LANES), jnp.bfloat16)
    count = SPAN * segments
    r = lax.broadcasted_iota(jnp.int32, (count, count), 0)
    c = lax.broadcasted_iota(jnp.int32, (count, count), 1)
    earlier = (lax.div(r, segments) == lax.div(c, segments)) & (c < r)
    same = lax.div(r, segments) == lax.div(c, segments)
    earlier = jnp.where(earlier, 1.0, 0.0).astype(jnp.bfloat16)
    same = jnp.where(same, 1.0, 0.0).astype(jnp.bfloat16)

    def dot(a, b):
        return jnp.dot(a, b, preferred_element_type=jnp.float32)

    within = dot(stacked, before)
    start = dot(dot(earlier, stacked).astype(jnp.bfloat16), ones)
    total = dot(dot(same, stacked).astype(jnp.bfloat16), ones)
    place = (within + start).astype(jnp.int32)
    rank = jnp.zeros_like(ids)
    for o in range(SPAN):
        rank = jnp.where(offset == o, place[o * segments : (o + 1) * segments], rank)
    offset_ref[...] = offset
    rank_ref[...] = rank
    over_ref[...] = jnp.max(jnp.where(total > ROOM, 1.0, 0.0), axis=0, keepdims=True)

    for s in range(segments):
        part = pl.ds(s * LANES, LANES)
        copies[s].wait()
        x = raw[part]
        scale = lax.rsqrt(jnp.sum(x * x, axis=1, keepdims=True) + 1e-06)
        normed[part] = (x * scale).astype(jnp.bfloat16)

    slot = lax.broadcasted_iota(jnp.int32, (ROOM, LANES), 0)
    lane = lax.broadcasted_iota(jnp.int32, (ROOM, LANES), 1)
    for o in range(SPAN):
        key = jnp.where(offset == o, rank, -1)
        pick = [
            jnp.where(slot == key[s : s + 1], 1.0, 0.0).astype(jnp.bfloat16)
            for s in range(segments)
        ]
        picked = dot(jnp.concatenate(pick, axis=1), normed[...])
        held = total[o * segments : o * segments + 1].astype(jnp.int32)
        empty = (slot >= held) & (lane == 0)
        first = jnp.where(empty, EMPTY, picked[:, :LANES])
        out_refs[o][:, :LANES] = first.astype(jnp.bfloat16)
        out_refs[o][:, LANES:] = picked[:, LANES:].astype(jnp.bfloat16)


def pack(embeddings, ids, blocks):
    rows, width = embeddings.shape
    segments = rows // LANES
    vmem = pl.BlockSpec(memory_space=pltpu.VMEM)
    shapes = [jax.ShapeDtypeStruct((ROOM, width), jnp.bfloat16)] * SPAN
    shapes += [jax.ShapeDtypeStruct((segments, LANES), jnp.int32)] * 2
    shapes += [jax.ShapeDtypeStruct((1, LANES), jnp.float32)]
    return pl.pallas_call(
        functools.partial(pack_kernel, blocks),
        out_shape=shapes,
        in_specs=[pl.BlockSpec(memory_space=pl.ANY), vmem],
        out_specs=[vmem] * len(shapes),
        scratch_shapes=[
            pltpu.VMEM((rows, width), jnp.float32),
            pltpu.VMEM((rows, width), jnp.bfloat16),
            pltpu.SemaphoreType.DMA((segments,)),
        ],
        compiler_params=pltpu.CompilerParams(vmem_limit_bytes=VMEM_BYTES),
        name="pack",
    )(embeddings, ids)


def score_kernel(*refs):
    message, best, (held, arrived) = refs[:SPAN], refs[SPAN : 2 * SPAN], refs[2 * SPAN :]
    copies = []
    for o in range(SPAN):
        part = pl.ds(o * ROOM, ROOM)
        copies.append(pltpu.make_async_copy(message[o], held.at[part], arrived.at[o]))
        copies[-1].start()
    for o in range(SPAN):
        copies[o].wait()
    penalty = []
    for o in range(SPAN):
        first = held[o * ROOM : (o + 1) * ROOM, :LANES].astype(jnp.float32)[:, :1]
        penalty.append(jnp.where(first > 1.5, -4.0, 0.0))
    row = lax.broadcasted_iota(jnp.int32, (ROOM, ROOM), 0)
    column = lax.broadcasted_iota(jnp.int32, (ROOM, ROOM), 1)
    for o in range(SPAN):
        mine = held[o * ROOM : (o + 1) * ROOM]
        top = jnp.full((1, ROOM), -1.0, jnp.float32)
        for p in range(SPAN):
            scores = lax.dot_general(
                held[p * ROOM : (p + 1) * ROOM],
                mine,
                (((1,), (1,)), ((), ())),
                preferred_element_type=jnp.float32,
            )
            scores = scores + penalty[p]
            if p == o:
                scores = jnp.where(row == column, -1.0, scores)
            top = jnp.maximum(top, jnp.max(scores, axis=0, keepdims=True))
        best[o][:, :ROOM] = top


def score(messages):
    room, width = messages[0].shape
    padded = pl.cdiv(room, LANES) * LANES
    return pl.pallas_call(
        score_kernel,
        out_shape=[jax.ShapeDtypeStruct((1, padded), jnp.float32)] * SPAN,
        in_specs=[pl.BlockSpec(memory_space=pl.ANY)] * SPAN,
        out_specs=[pl.BlockSpec(memory_space=pltpu.VMEM)] * SPAN,
        scratch_shapes=[
            pltpu.VMEM((SPAN * room, width), jnp.bfloat16),
            pltpu.SemaphoreType.DMA((SPAN,)),
        ],
        compiler_params=pltpu.CompilerParams(vmem_limit_bytes=VMEM_BYTES),
        name="score",
    )(*messages)


def unpack_kernel(*refs):
    best, (offset_ref, rank_ref, out_ref) = refs[:SPAN], refs[SPAN:]
    offset, rank = offset_ref[...], rank_ref[...]
    inner = lax.bitwise_and(rank, LANES - 1)
    result = jnp.full(offset.shape, -1.0, jnp.float32)
    for o in range(SPAN):
        for start in range(0, best[o].shape[1], LANES):
            table = jnp.broadcast_to(best[o][:, start : start + LANES], offset.shape)
            value = jnp.take_along_axis(table, inner, axis=1)
            here = (offset == o) & (rank >= start) & (rank < start + LANES)
            result = jnp.where(here, value, result)
    out_ref[...] = result


def unpack(best, offset, rank):
    vmem = pl.BlockSpec(memory_space=pltpu.VMEM)
    return pl.pallas_call(
        unpack_kernel,
        out_shape=jax.ShapeDtypeStruct(offset.shape, jnp.float32),
        in_specs=[vmem] * (SPAN + 2),
        out_specs=vmem,
        name="unpack",
    )(*best, offset, rank)


def local(embeddings, cluster_id):
    blocks = lax.axis_size("blk")
    ids = cluster_id.reshape(-1, LANES)
    *messages, offset, rank, over = pack(embeddings, ids, blocks)
    over = lax.pmax(over, ("parts", "blk"))
    arrived = [shifted(messages[o], "blk", HOME - o) if o != HOME else messages[o] for o in range(SPAN)]
    best = score(arrived)
    returned = [shifted(best[o], "blk", o - HOME) if o != HOME else best[o] for o in range(SPAN)]
    packed = unpack(returned, offset, rank).reshape(-1)
    return lax.cond(
        over[0, 0] > 0, lambda: by_ring(embeddings, cluster_id), lambda: packed
    )


def solution(mesh):
    in_specs = (P(("parts", "blk"), None), P(("parts", "blk")))
    out_specs = P(("parts", "blk"))
    return jax.shard_map(local, mesh=mesh, in_specs=in_specs, out_specs=out_specs, check_vma=False)
```

```python
import functools

import jax
import jax.numpy as jnp
from jax import lax
from jax.experimental import pallas as pl
from jax.experimental.pallas import tpu as pltpu
from jax.sharding import PartitionSpec as P

SPAN = 8
HOME = 4
ORDER = (0, 7, 1, 6, 2, 5, 3, 4)
ROOM = 176
LANES = 128
EMPTY = 2.0
VMEM_BYTES = 32 * 1024 * 1024
SCORE_VMEM = 16 * 1024 * 1024


def shifted(block, axis, distance):
    if distance == 0:
        return block
    size = lax.axis_size(axis)
    route = [(i, (i + distance) % size) for i in range(size)]
    return lax.ppermute(block, axis, route)


def block_max(left, left_id, right, right_id, same_block):
    scores = lax.dot_general(
        left, right, (((1,), (1,)), ((), ())), preferred_element_type=jnp.float32
    )
    match = (left_id[:, None] == right_id[None, :]) & (left_id[:, None] >= 0)
    if same_block:
        count = left.shape[0]
        match = match & (jnp.arange(count)[:, None] != jnp.arange(count)[None, :])
    masked = jnp.where(match, scores, jnp.float32(-1.0))
    return (jnp.max(masked, axis=1), jnp.max(masked, axis=0))


def by_ring(embeddings, cluster_id):
    scale = lax.rsqrt(jnp.sum(embeddings * embeddings, axis=1, keepdims=True) + 1e-06)
    normed = (embeddings * scale).astype(jnp.bfloat16)
    best, unused_cols = block_max(normed, cluster_id, normed, cluster_id, True)
    visitor = (normed, cluster_id)
    for offset in range(1, SPAN):
        visitor = (shifted(visitor[0], "blk", 1), shifted(visitor[1], "blk", 1))
        row_best, col_best = block_max(normed, cluster_id, visitor[0], visitor[1], False)
        returned = shifted(col_best, "blk", -offset)
        best = jnp.maximum(best, jnp.maximum(row_best, returned))
    return best


def pack_kernel(blocks, emb_ref, id_ref, *refs):
    out_refs, (offset_ref, rank_ref, over_ref) = refs[:SPAN], refs[SPAN : SPAN + 3]
    raw, normed, arrived = refs[SPAN + 3 :]
    rows, width = normed.shape
    segments = rows // LANES
    copies = []
    for s in range(segments):
        part = pl.ds(s * LANES, LANES)
        copies.append(pltpu.make_async_copy(emb_ref.at[part], raw.at[part], arrived.at[s]))
        copies[-1].start()

    me = lax.axis_index("blk")
    ids = id_ref[...]
    offset = lax.rem(me - ids + 2 * blocks, blocks)
    offset = jnp.where(ids >= 0, offset, SPAN)
    member = [jnp.where(offset == o, 1.0, 0.0) for o in range(SPAN)]
    stacked = jnp.concatenate(member, axis=0).astype(jnp.bfloat16)
    before = lax.broadcasted_iota(jnp.int32, (LANES, LANES), 0) < lax.broadcasted_iota(
        jnp.int32, (LANES, LANES), 1
    )
    before = jnp.where(before, 1.0, 0.0).astype(jnp.bfloat16)
    ones = jnp.ones((LANES, LANES), jnp.bfloat16)
    count = SPAN * segments
    r = lax.broadcasted_iota(jnp.int32, (count, count), 0)
    c = lax.broadcasted_iota(jnp.int32, (count, count), 1)
    earlier = (lax.div(r, segments) == lax.div(c, segments)) & (c < r)
    same = lax.div(r, segments) == lax.div(c, segments)
    earlier = jnp.where(earlier, 1.0, 0.0).astype(jnp.bfloat16)
    same = jnp.where(same, 1.0, 0.0).astype(jnp.bfloat16)

    def dot(a, b):
        return jnp.dot(a, b, preferred_element_type=jnp.float32)

    within = dot(stacked, before)
    start = dot(dot(earlier, stacked).astype(jnp.bfloat16), ones)
    total = dot(dot(same, stacked).astype(jnp.bfloat16), ones)
    place = (within + start).astype(jnp.int32)
    rank = jnp.zeros_like(ids)
    for o in range(SPAN):
        rank = jnp.where(offset == o, place[o * segments : (o + 1) * segments], rank)
    offset_ref[...] = offset
    rank_ref[...] = rank
    over_ref[...] = jnp.max(jnp.where(total > ROOM, 1.0, 0.0), axis=0, keepdims=True)

    for s in range(segments):
        part = pl.ds(s * LANES, LANES)
        copies[s].wait()
        x = raw[part]
        scale = lax.rsqrt(jnp.sum(x * x, axis=1, keepdims=True) + 1e-06)
        normed[part] = (x * scale).astype(jnp.bfloat16)

    slot = lax.broadcasted_iota(jnp.int32, (ROOM, LANES), 0)
    lane = lax.broadcasted_iota(jnp.int32, (ROOM, LANES), 1)
    for o, out_ref in zip(ORDER, out_refs):
        key = jnp.where(offset == o, rank, -1)
        pick = [
            jnp.where(slot == key[s : s + 1], 1.0, 0.0).astype(jnp.bfloat16)
            for s in range(segments)
        ]
        picked = dot(jnp.concatenate(pick, axis=1), normed[...])
        held = total[o * segments : o * segments + 1].astype(jnp.int32)
        empty = (slot >= held) & (lane == 0)
        first = jnp.where(empty, EMPTY, picked[:, :LANES])
        out_ref[:, :LANES] = first.astype(jnp.bfloat16)
        out_ref[:, LANES:] = picked[:, LANES:].astype(jnp.bfloat16)


def pack(embeddings, ids, blocks):
    rows, width = embeddings.shape
    segments = rows // LANES
    vmem = pl.BlockSpec(memory_space=pltpu.VMEM)
    shapes = [jax.ShapeDtypeStruct((ROOM, width), jnp.bfloat16)] * SPAN
    shapes += [jax.ShapeDtypeStruct((segments, LANES), jnp.int32)] * 2
    shapes += [jax.ShapeDtypeStruct((1, LANES), jnp.float32)]
    return pl.pallas_call(
        functools.partial(pack_kernel, blocks),
        out_shape=shapes,
        in_specs=[pl.BlockSpec(memory_space=pl.ANY), vmem],
        out_specs=[vmem] * len(shapes),
        scratch_shapes=[
            pltpu.VMEM((rows, width), jnp.float32),
            pltpu.VMEM((rows, width), jnp.bfloat16),
            pltpu.SemaphoreType.DMA((segments,)),
        ],
        compiler_params=pltpu.CompilerParams(vmem_limit_bytes=VMEM_BYTES),
        name="pack",
    )(embeddings, ids)


def score_kernel(*refs):
    message, best = refs[:SPAN], refs[SPAN:]
    penalty = []
    for o in range(SPAN):
        first = message[o][:, :LANES].astype(jnp.float32)[:, :1]
        penalty.append(jnp.where(first > 1.5, -4.0, 0.0))
    row = lax.broadcasted_iota(jnp.int32, (ROOM, ROOM), 0)
    column = lax.broadcasted_iota(jnp.int32, (ROOM, ROOM), 1)
    for o in range(SPAN):
        top = jnp.full((1, ROOM), -1.0, jnp.float32)
        for p in range(SPAN):
            scores = lax.dot_general(
                message[p][...],
                message[o][...],
                (((1,), (1,)), ((), ())),
                preferred_element_type=jnp.float32,
            )
            scores = scores + penalty[p]
            if p == o:
                scores = jnp.where(row == column, -1.0, scores)
            top = jnp.maximum(top, jnp.max(scores, axis=0, keepdims=True))
        best[o][:, :ROOM] = top


def score(messages):
    room, width = messages[0].shape
    padded = pl.cdiv(room, LANES) * LANES
    return pl.pallas_call(
        score_kernel,
        out_shape=[jax.ShapeDtypeStruct((1, padded), jnp.float32)] * SPAN,
        in_specs=[pl.BlockSpec(memory_space=pltpu.VMEM)] * SPAN,
        out_specs=[pl.BlockSpec(memory_space=pltpu.VMEM)] * SPAN,
        compiler_params=pltpu.CompilerParams(vmem_limit_bytes=SCORE_VMEM),
        name="score",
    )(*messages)


def unpack_kernel(*refs):
    best, (offset_ref, rank_ref, out_ref) = refs[:SPAN], refs[SPAN:]
    offset, rank = offset_ref[...], rank_ref[...]
    inner = lax.bitwise_and(rank, LANES - 1)
    result = jnp.full(offset.shape, -1.0, jnp.float32)
    for o, best_ref in zip(ORDER, best):
        for start in range(0, best_ref.shape[1], LANES):
            table = jnp.broadcast_to(best_ref[:, start : start + LANES], offset.shape)
            value = jnp.take_along_axis(table, inner, axis=1)
            here = (offset == o) & (rank >= start) & (rank < start + LANES)
            result = jnp.where(here, value, result)
    out_ref[...] = result


def unpack(best, offset, rank):
    vmem = pl.BlockSpec(memory_space=pltpu.VMEM)
    return pl.pallas_call(
        unpack_kernel,
        out_shape=jax.ShapeDtypeStruct(offset.shape, jnp.float32),
        in_specs=[vmem] * (SPAN + 2),
        out_specs=vmem,
        compiler_params=pltpu.CompilerParams(vmem_limit_bytes=1024 * 1024),
        name="unpack",
    )(*best, offset, rank)


def local(embeddings, cluster_id):
    blocks = lax.axis_size("blk")
    ids = cluster_id.reshape(-1, LANES)
    *messages, offset, rank, over = pack(embeddings, ids, blocks)
    flags = lax.all_gather(over, ("parts", "blk"), axis=0, tiled=True)
    arrived = [shifted(m, "blk", HOME - o) for o, m in zip(ORDER, messages)]
    best = score(arrived)
    returned = [shifted(b, "blk", o - HOME) for o, b in zip(ORDER, best)]
    packed = unpack(returned, offset, rank).reshape(-1)
    return lax.cond(
        jnp.max(flags) > 0, lambda: by_ring(embeddings, cluster_id), lambda: packed
    )


def solution(mesh):
    in_specs = (P(("parts", "blk"), None), P(("parts", "blk")))
    out_specs = P(("parts", "blk"))
    return jax.shard_map(local, mesh=mesh, in_specs=in_specs, out_specs=out_specs, check_vma=False)
```

```python
import functools

import jax
import jax.numpy as jnp
from jax import lax
from jax.experimental import pallas as pl
from jax.experimental.pallas import tpu as pltpu
from jax.sharding import PartitionSpec as P

SPAN = 8
HOME = 4
ORDER = (0, 7, 1, 6, 2, 5, 3, 4)
ROOM = 176
LANES = 128
EMPTY = 2.0
VMEM_BYTES = 32 * 1024 * 1024
SCORE_VMEM = 16 * 1024 * 1024


def shifted(block, axis, distance):
    if distance == 0:
        return block
    size = lax.axis_size(axis)
    route = [(i, (i + distance) % size) for i in range(size)]
    return lax.ppermute(block, axis, route)


def block_max(left, left_id, right, right_id, same_block):
    scores = lax.dot_general(
        left, right, (((1,), (1,)), ((), ())), preferred_element_type=jnp.float32
    )
    match = (left_id[:, None] == right_id[None, :]) & (left_id[:, None] >= 0)
    if same_block:
        count = left.shape[0]
        match = match & (jnp.arange(count)[:, None] != jnp.arange(count)[None, :])
    masked = jnp.where(match, scores, jnp.float32(-1.0))
    return (jnp.max(masked, axis=1), jnp.max(masked, axis=0))


def by_ring(embeddings, cluster_id):
    scale = lax.rsqrt(jnp.sum(embeddings * embeddings, axis=1, keepdims=True) + 1e-06)
    normed = (embeddings * scale).astype(jnp.bfloat16)
    best, unused_cols = block_max(normed, cluster_id, normed, cluster_id, True)
    visitor = (normed, cluster_id)
    for offset in range(1, SPAN):
        visitor = (shifted(visitor[0], "blk", 1), shifted(visitor[1], "blk", 1))
        row_best, col_best = block_max(normed, cluster_id, visitor[0], visitor[1], False)
        returned = shifted(col_best, "blk", -offset)
        best = jnp.maximum(best, jnp.maximum(row_best, returned))
    return best


def pack_kernel(blocks, emb_ref, id_ref, *refs):
    out_refs, (offset_ref, rank_ref, over_ref) = refs[:SPAN], refs[SPAN : SPAN + 3]
    raw, normed, arrived = refs[SPAN + 3 :]
    rows, width = normed.shape
    segments = rows // LANES
    copies = []
    for s in range(segments):
        part = pl.ds(s * LANES, LANES)
        copies.append(pltpu.make_async_copy(emb_ref.at[part], raw.at[part], arrived.at[s]))
        copies[-1].start()

    me = lax.axis_index("blk")
    ids = id_ref[...]
    offset = lax.rem(me - ids + 2 * blocks, blocks)
    offset = jnp.where(ids >= 0, offset, SPAN)
    member = [jnp.where(offset == o, 1.0, 0.0) for o in range(SPAN)]
    stacked = jnp.concatenate(member, axis=0).astype(jnp.bfloat16)
    before = lax.broadcasted_iota(jnp.int32, (LANES, LANES), 0) < lax.broadcasted_iota(
        jnp.int32, (LANES, LANES), 1
    )
    before = jnp.where(before, 1.0, 0.0).astype(jnp.bfloat16)
    ones = jnp.ones((LANES, LANES), jnp.bfloat16)
    count = SPAN * segments
    r = lax.broadcasted_iota(jnp.int32, (count, count), 0)
    c = lax.broadcasted_iota(jnp.int32, (count, count), 1)
    earlier = (lax.div(r, segments) == lax.div(c, segments)) & (c < r)
    same = lax.div(r, segments) == lax.div(c, segments)
    earlier = jnp.where(earlier, 1.0, 0.0).astype(jnp.bfloat16)
    same = jnp.where(same, 1.0, 0.0).astype(jnp.bfloat16)

    def dot(a, b):
        return jnp.dot(a, b, preferred_element_type=jnp.float32)

    within = dot(stacked, before)
    start = dot(dot(earlier, stacked).astype(jnp.bfloat16), ones)
    total = dot(dot(same, stacked).astype(jnp.bfloat16), ones)
    place = (within + start).astype(jnp.int32)
    rank = jnp.zeros_like(ids)
    for o in range(SPAN):
        rank = jnp.where(offset == o, place[o * segments : (o + 1) * segments], rank)
    offset_ref[...] = offset
    rank_ref[...] = rank
    over_ref[...] = jnp.max(jnp.where(total > ROOM, 1.0, 0.0), axis=0, keepdims=True)

    for s in range(segments):
        part = pl.ds(s * LANES, LANES)
        copies[s].wait()
        x = raw[part]
        scale = lax.rsqrt(jnp.sum(x * x, axis=1, keepdims=True) + 1e-06)
        normed[part] = (x * scale).astype(jnp.bfloat16)

    slot = lax.broadcasted_iota(jnp.int32, (ROOM, LANES), 0)
    lane = lax.broadcasted_iota(jnp.int32, (ROOM, LANES), 1)
    for o, out_ref in zip(ORDER, out_refs):
        key = jnp.where(offset == o, rank, -1)
        pick = [
            jnp.where(slot == key[s : s + 1], 1.0, 0.0).astype(jnp.bfloat16)
            for s in range(segments)
        ]
        picked = dot(jnp.concatenate(pick, axis=1), normed[...])
        held = total[o * segments : o * segments + 1].astype(jnp.int32)
        empty = (slot >= held) & (lane == 0)
        first = jnp.where(empty, EMPTY, picked[:, :LANES])
        out_ref[:, :LANES] = first.astype(jnp.bfloat16)
        out_ref[:, LANES:] = picked[:, LANES:].astype(jnp.bfloat16)


def pack(embeddings, ids, blocks):
    rows, width = embeddings.shape
    segments = rows // LANES
    vmem = pl.BlockSpec(memory_space=pltpu.VMEM)
    shapes = [jax.ShapeDtypeStruct((ROOM, width), jnp.bfloat16)] * SPAN
    shapes += [jax.ShapeDtypeStruct((segments, LANES), jnp.int32)] * 2
    shapes += [jax.ShapeDtypeStruct((1, LANES), jnp.float32)]
    return pl.pallas_call(
        functools.partial(pack_kernel, blocks),
        out_shape=shapes,
        in_specs=[pl.BlockSpec(memory_space=pl.ANY), vmem],
        out_specs=[vmem] * len(shapes),
        scratch_shapes=[
            pltpu.VMEM((rows, width), jnp.float32),
            pltpu.VMEM((rows, width), jnp.bfloat16),
            pltpu.SemaphoreType.DMA((segments,)),
        ],
        compiler_params=pltpu.CompilerParams(vmem_limit_bytes=VMEM_BYTES),
        name="pack",
    )(embeddings, ids)


def score_kernel(blocks, *refs):
    message, (over_ref, other_ref, best_ref) = refs[:SPAN], refs[SPAN:]
    room = message[0].shape[0]
    padded = best_ref.shape[2]
    me = lax.axis_index("blk")
    flag = jnp.maximum(over_ref[...], other_ref[...])
    best_ref[...] = jnp.concatenate([flag[None]] * (padded // LANES), axis=2) + jnp.zeros_like(best_ref)
    penalty = []
    for k in range(SPAN):
        first = message[k][:, :LANES].astype(jnp.float32)[:, :1]
        penalty.append(jnp.where(first > 1.5, -4.0, 0.0))
    row = lax.broadcasted_iota(jnp.int32, (room, room), 0)
    column = lax.broadcasted_iota(jnp.int32, (room, room), 1)
    for k in range(SPAN):
        top = jnp.full((1, room), -1.0, jnp.float32)
        for p in range(SPAN):
            scores = lax.dot_general(
                message[p][...],
                message[k][...],
                (((1,), (1,)), ((), ())),
                preferred_element_type=jnp.float32,
            )
            scores = scores + penalty[p]
            if p == k:
                scores = jnp.where(row == column, -1.0, scores)
            top = jnp.maximum(top, jnp.max(scores, axis=0, keepdims=True))
        source = lax.rem(me + ORDER[k] - HOME + blocks, blocks)
        best_ref[source, :, :room] = top


def score(messages, over, other, blocks):
    room, width = messages[0].shape
    padded = (pl.cdiv(room, LANES) if room % LANES else room // LANES + 1) * LANES
    vmem = pl.BlockSpec(memory_space=pltpu.VMEM)
    return pl.pallas_call(
        functools.partial(score_kernel, blocks),
        out_shape=jax.ShapeDtypeStruct((blocks, 1, padded), jnp.float32),
        in_specs=[vmem] * (SPAN + 2),
        out_specs=vmem,
        compiler_params=pltpu.CompilerParams(vmem_limit_bytes=SCORE_VMEM),
        name="score",
    )(*messages, over, other)


def unpack_kernel(blocks, best_ref, offset_ref, rank_ref, out_ref, over_ref):
    offset, rank = offset_ref[...], rank_ref[...]
    padded = best_ref.shape[2]
    me = lax.axis_index("blk")
    inner = lax.bitwise_and(rank, LANES - 1)
    result = jnp.full(offset.shape, -1.0, jnp.float32)
    for o in range(SPAN):
        home = lax.rem(me + HOME - o + blocks, blocks)
        best = best_ref[home]
        for start in range(0, padded, LANES):
            table = jnp.broadcast_to(best[:, start : start + LANES], offset.shape)
            value = jnp.take_along_axis(table, inner, axis=1)
            here = (offset == o) & (rank >= start) & (rank < start + LANES)
            result = jnp.where(here, value, result)
    out_ref[...] = result
    flags = jnp.max(best_ref[:, :, padded - LANES :], axis=0)
    lane = lax.broadcasted_iota(jnp.int32, flags.shape, 1)
    over_ref[0, 0] = jnp.max(jnp.where(lane == LANES - 1, flags, 0.0))


def unpack(best, offset, rank):
    vmem = pl.BlockSpec(memory_space=pltpu.VMEM)
    return pl.pallas_call(
        functools.partial(unpack_kernel, best.shape[0]),
        out_shape=[
            jax.ShapeDtypeStruct(offset.shape, jnp.float32),
            jax.ShapeDtypeStruct((1, 1), jnp.float32),
        ],
        in_specs=[vmem] * 3,
        out_specs=[vmem, pl.BlockSpec(memory_space=pltpu.SMEM)],
        compiler_params=pltpu.CompilerParams(vmem_limit_bytes=4 * 1024 * 1024),
        name="unpack",
    )(best, offset, rank)


def local(embeddings, cluster_id):
    blocks = lax.axis_size("blk")
    ids = cluster_id.reshape(-1, LANES)
    *messages, offset, rank, over = pack(embeddings, ids, blocks)
    arrived = [shifted(m, "blk", HOME - o) for o, m in zip(ORDER, messages)]
    other = over
    for distance in range(1, lax.axis_size("parts")):
        other = jnp.maximum(other, shifted(over, "parts", distance))
    best = score(arrived, over, other, blocks)
    returned = lax.all_to_all(best, "blk", 0, 0, tiled=True)
    packed, flag = unpack(returned, offset, rank)
    return lax.cond(
        flag[0, 0] > 0, lambda: by_ring(embeddings, cluster_id), lambda: packed.reshape(-1)
    )


def solution(mesh):
    in_specs = (P(("parts", "blk"), None), P(("parts", "blk")))
    out_specs = P(("parts", "blk"))
    return jax.shard_map(local, mesh=mesh, in_specs=in_specs, out_specs=out_specs, check_vma=False)
```

```python
import functools

import jax
import jax.numpy as jnp
from jax import lax
from jax.experimental import pallas as pl
from jax.experimental.pallas import tpu as pltpu
from jax.sharding import PartitionSpec as P

SPAN = 8
HOME = 4
GROUP = 4
ROOM = 176
LANES = 128
EMPTY = 2.0
VMEM_BYTES = 32 * 1024 * 1024
SCORE_VMEM = 16 * 1024 * 1024


def shifted(block, axis, distance):
    if distance == 0:
        return block
    size = lax.axis_size(axis)
    route = [(i, (i + distance) % size) for i in range(size)]
    return lax.ppermute(block, axis, route)


def block_max(left, left_id, right, right_id, same_block):
    scores = lax.dot_general(
        left, right, (((1,), (1,)), ((), ())), preferred_element_type=jnp.float32
    )
    match = (left_id[:, None] == right_id[None, :]) & (left_id[:, None] >= 0)
    if same_block:
        count = left.shape[0]
        match = match & (jnp.arange(count)[:, None] != jnp.arange(count)[None, :])
    masked = jnp.where(match, scores, jnp.float32(-1.0))
    return (jnp.max(masked, axis=1), jnp.max(masked, axis=0))


def by_ring(embeddings, cluster_id):
    scale = lax.rsqrt(jnp.sum(embeddings * embeddings, axis=1, keepdims=True) + 1e-06)
    normed = (embeddings * scale).astype(jnp.bfloat16)
    best, unused_cols = block_max(normed, cluster_id, normed, cluster_id, True)
    visitor = (normed, cluster_id)
    for offset in range(1, SPAN):
        visitor = (shifted(visitor[0], "blk", 1), shifted(visitor[1], "blk", 1))
        row_best, col_best = block_max(normed, cluster_id, visitor[0], visitor[1], False)
        returned = shifted(col_best, "blk", -offset)
        best = jnp.maximum(best, jnp.maximum(row_best, returned))
    return best


def outside(block, k, blocks):
    q = block % GROUP
    r = q ^ k
    return (block - q + r + (GROUP if r <= q else -GROUP)) % blocks


def partner(me, m, blocks, sender):
    q = lax.rem(me, GROUP)
    if m >= GROUP:
        return me - q + m - GROUP
    r = lax.bitwise_xor(q, m)
    after = (q <= r) if sender else (r > q)
    step = jnp.where(after, blocks - GROUP, GROUP)
    return lax.rem(me - q + r + step, blocks)


def pack_kernel(blocks, emb_ref, id_ref, *refs):
    out_refs, refs = refs[:GROUP], refs[GROUP:]
    near_ref, label_ref, rank_ref, over_ref, raw, normed, arrived = refs
    rows, width = normed.shape
    segments = rows // LANES
    copies = []
    for s in range(segments):
        part = pl.ds(s * LANES, LANES)
        copies.append(pltpu.make_async_copy(emb_ref.at[part], raw.at[part], arrived.at[s]))
        copies[-1].start()

    me = lax.axis_index("blk")
    ids = id_ref[...]
    q = lax.rem(me, GROUP)
    offset = lax.rem(me - ids + 2 * blocks, blocks)
    turn = lax.bitwise_and(q - offset + SPAN, SPAN - 1)
    label = jnp.where(turn < GROUP, lax.bitwise_xor(turn, q), turn)
    label = jnp.where(ids >= 0, label, SPAN)
    member = [jnp.where(label == m, 1.0, 0.0) for m in range(SPAN)]
    stacked = jnp.concatenate(member, axis=0).astype(jnp.bfloat16)
    before = lax.broadcasted_iota(jnp.int32, (LANES, LANES), 0) < lax.broadcasted_iota(
        jnp.int32, (LANES, LANES), 1
    )
    before = jnp.where(before, 1.0, 0.0).astype(jnp.bfloat16)
    ones = jnp.ones((LANES, LANES), jnp.bfloat16)
    count = SPAN * segments
    r = lax.broadcasted_iota(jnp.int32, (count, count), 0)
    c = lax.broadcasted_iota(jnp.int32, (count, count), 1)
    earlier = (lax.div(r, segments) == lax.div(c, segments)) & (c < r)
    same = lax.div(r, segments) == lax.div(c, segments)
    earlier = jnp.where(earlier, 1.0, 0.0).astype(jnp.bfloat16)
    same = jnp.where(same, 1.0, 0.0).astype(jnp.bfloat16)

    def dot(a, b):
        return jnp.dot(a, b, preferred_element_type=jnp.float32)

    within = dot(stacked, before)
    start = dot(dot(earlier, stacked).astype(jnp.bfloat16), ones)
    total = dot(dot(same, stacked).astype(jnp.bfloat16), ones)
    place = (within + start).astype(jnp.int32)
    rank = jnp.zeros_like(ids)
    for m in range(SPAN):
        rank = jnp.where(label == m, place[m * segments : (m + 1) * segments], rank)
    label_ref[...] = label
    rank_ref[...] = rank
    over_ref[...] = jnp.max(jnp.where(total > ROOM, 1.0, 0.0), axis=0, keepdims=True)

    for s in range(segments):
        part = pl.ds(s * LANES, LANES)
        copies[s].wait()
        x = raw[part]
        scale = lax.rsqrt(jnp.sum(x * x, axis=1, keepdims=True) + 1e-06)
        normed[part] = (x * scale).astype(jnp.bfloat16)

    slot = lax.broadcasted_iota(jnp.int32, (ROOM, LANES), 0)
    lane = lax.broadcasted_iota(jnp.int32, (ROOM, LANES), 1)
    for m in range(SPAN):
        key = jnp.where(label == m, rank, -1)
        pick = [
            jnp.where(slot == key[s : s + 1], 1.0, 0.0).astype(jnp.bfloat16)
            for s in range(segments)
        ]
        picked = dot(jnp.concatenate(pick, axis=1), normed[...])
        held = total[m * segments : m * segments + 1].astype(jnp.int32)
        empty = (slot >= held) & (lane == 0)
        first = jnp.where(empty, EMPTY, picked[:, :LANES])
        out_ref = out_refs[m] if m < GROUP else near_ref.at[pl.ds((m - GROUP) * ROOM, ROOM)]
        out_ref[:, :LANES] = first.astype(jnp.bfloat16)
        out_ref[:, LANES:] = picked[:, LANES:].astype(jnp.bfloat16)


def pack(embeddings, ids, blocks):
    rows, width = embeddings.shape
    segments = rows // LANES
    vmem = pl.BlockSpec(memory_space=pltpu.VMEM)
    shapes = [jax.ShapeDtypeStruct((ROOM, width), jnp.bfloat16)] * GROUP
    shapes += [jax.ShapeDtypeStruct((GROUP * ROOM, width), jnp.bfloat16)]
    shapes += [jax.ShapeDtypeStruct((segments, LANES), jnp.int32)] * 2
    shapes += [jax.ShapeDtypeStruct((1, LANES), jnp.float32)]
    return pl.pallas_call(
        functools.partial(pack_kernel, blocks),
        out_shape=shapes,
        in_specs=[pl.BlockSpec(memory_space=pl.ANY), vmem],
        out_specs=[vmem] * len(shapes),
        scratch_shapes=[
            pltpu.VMEM((rows, width), jnp.float32),
            pltpu.VMEM((rows, width), jnp.bfloat16),
            pltpu.SemaphoreType.DMA((segments,)),
        ],
        compiler_params=pltpu.CompilerParams(vmem_limit_bytes=VMEM_BYTES),
        name="pack",
    )(embeddings, ids)


def score_kernel(blocks, *refs):
    far, (near_ref, over_ref, other_ref, best_ref) = refs[:GROUP], refs[GROUP:]
    room = far[0].shape[0]
    message = list(far) + [near_ref.at[pl.ds(r * room, room)] for r in range(GROUP)]
    padded = best_ref.shape[2]
    me = lax.axis_index("blk")
    flag = jnp.maximum(over_ref[...], other_ref[...])
    best_ref[...] = jnp.concatenate([flag[None]] * (padded // LANES), axis=2) + jnp.zeros_like(best_ref)
    penalty = []
    for k in range(SPAN):
        first = message[k][:, :LANES].astype(jnp.float32)[:, :1]
        penalty.append(jnp.where(first > 1.5, -4.0, 0.0))
    row = lax.broadcasted_iota(jnp.int32, (room, room), 0)
    column = lax.broadcasted_iota(jnp.int32, (room, room), 1)
    for k in range(SPAN):
        top = jnp.full((1, room), -1.0, jnp.float32)
        for p in range(SPAN):
            scores = lax.dot_general(
                message[p][...],
                message[k][...],
                (((1,), (1,)), ((), ())),
                preferred_element_type=jnp.float32,
            )
            scores = scores + penalty[p]
            if p == k:
                scores = jnp.where(row == column, -1.0, scores)
            top = jnp.maximum(top, jnp.max(scores, axis=0, keepdims=True))
        best_ref[partner(me, k, blocks, True), :, :room] = top


def score(far, near, over, other, blocks):
    room, width = far[0].shape
    padded = (pl.cdiv(room, LANES) if room % LANES else room // LANES + 1) * LANES
    vmem = pl.BlockSpec(memory_space=pltpu.VMEM)
    return pl.pallas_call(
        functools.partial(score_kernel, blocks),
        out_shape=jax.ShapeDtypeStruct((blocks, 1, padded), jnp.float32),
        in_specs=[vmem] * (GROUP + 3),
        out_specs=vmem,
        compiler_params=pltpu.CompilerParams(vmem_limit_bytes=SCORE_VMEM),
        name="score",
    )(*far, near, over, other)


def unpack_kernel(blocks, best_ref, label_ref, rank_ref, out_ref, over_ref):
    label, rank = label_ref[...], rank_ref[...]
    padded = best_ref.shape[2]
    me = lax.axis_index("blk")
    inner = lax.bitwise_and(rank, LANES - 1)
    result = jnp.full(label.shape, -1.0, jnp.float32)
    for m in range(SPAN):
        best = best_ref[partner(me, m, blocks, False)]
        for start in range(0, padded, LANES):
            table = jnp.broadcast_to(best[:, start : start + LANES], label.shape)
            value = jnp.take_along_axis(table, inner, axis=1)
            here = (label == m) & (rank >= start) & (rank < start + LANES)
            result = jnp.where(here, value, result)
    out_ref[...] = result
    flags = jnp.max(best_ref[:, :, padded - LANES :], axis=0)
    lane = lax.broadcasted_iota(jnp.int32, flags.shape, 1)
    over_ref[0, 0] = jnp.max(jnp.where(lane == LANES - 1, flags, 0.0))


def unpack(best, label, rank):
    vmem = pl.BlockSpec(memory_space=pltpu.VMEM)
    return pl.pallas_call(
        functools.partial(unpack_kernel, best.shape[0]),
        out_shape=[
            jax.ShapeDtypeStruct(label.shape, jnp.float32),
            jax.ShapeDtypeStruct((1, 1), jnp.float32),
        ],
        in_specs=[vmem] * 3,
        out_specs=[vmem, pl.BlockSpec(memory_space=pltpu.SMEM)],
        compiler_params=pltpu.CompilerParams(vmem_limit_bytes=4 * 1024 * 1024),
        name="unpack",
    )(best, label, rank)


def local(embeddings, cluster_id):
    blocks = lax.axis_size("blk")
    ids = cluster_id.reshape(-1, LANES)
    *far, near, label, rank, over = pack(embeddings, ids, blocks)
    for k in range(GROUP):
        route = [(i, outside(i, k, blocks)) for i in range(blocks)]
        far[k] = lax.ppermute(far[k], "blk", route)
    groups = [list(range(i, i + GROUP)) for i in range(0, blocks, GROUP)]
    near = lax.all_to_all(near, "blk", 0, 0, axis_index_groups=groups, tiled=True)
    other = over
    for distance in range(1, lax.axis_size("parts")):
        other = jnp.maximum(other, shifted(over, "parts", distance))
    best = score(far, near, over, other, blocks)
    returned = lax.all_to_all(best, "blk", 0, 0, tiled=True)
    packed, flag = unpack(returned, label, rank)
    return lax.cond(
        flag[0, 0] > 0, lambda: by_ring(embeddings, cluster_id), lambda: packed.reshape(-1)
    )


def solution(mesh):
    in_specs = (P(("parts", "blk"), None), P(("parts", "blk")))
    out_specs = P(("parts", "blk"))
    return jax.shard_map(local, mesh=mesh, in_specs=in_specs, out_specs=out_specs, check_vma=False)
```

```python
import functools

import jax
import jax.numpy as jnp
from jax import lax
from jax.experimental import pallas as pl
from jax.experimental.pallas import tpu as pltpu
from jax.sharding import PartitionSpec as P

SPAN = 8
HOME = 4
GROUP = 4
ROOM = 176
LANES = 128
EMPTY = 2.0
PACK_VMEM = 24 * 1024 * 1024
SCORE_VMEM = 20 * 1024 * 1024


def shifted(block, axis, distance):
    if distance == 0:
        return block
    size = lax.axis_size(axis)
    route = [(i, (i + distance) % size) for i in range(size)]
    return lax.ppermute(block, axis, route)


def block_max(left, left_id, right, right_id, same_block):
    scores = lax.dot_general(
        left, right, (((1,), (1,)), ((), ())), preferred_element_type=jnp.float32
    )
    match = (left_id[:, None] == right_id[None, :]) & (left_id[:, None] >= 0)
    if same_block:
        count = left.shape[0]
        match = match & (jnp.arange(count)[:, None] != jnp.arange(count)[None, :])
    masked = jnp.where(match, scores, jnp.float32(-1.0))
    return (jnp.max(masked, axis=1), jnp.max(masked, axis=0))


def by_ring(embeddings, cluster_id):
    scale = lax.rsqrt(jnp.sum(embeddings * embeddings, axis=1, keepdims=True) + 1e-06)
    normed = (embeddings * scale).astype(jnp.bfloat16)
    best, unused_cols = block_max(normed, cluster_id, normed, cluster_id, True)
    visitor = (normed, cluster_id)
    for offset in range(1, SPAN):
        visitor = (shifted(visitor[0], "blk", 1), shifted(visitor[1], "blk", 1))
        row_best, col_best = block_max(normed, cluster_id, visitor[0], visitor[1], False)
        returned = shifted(col_best, "blk", -offset)
        best = jnp.maximum(best, jnp.maximum(row_best, returned))
    return best


def outside(block, k, blocks):
    q = block % GROUP
    r = q ^ k
    return (block - q + r + (GROUP if r <= q else -GROUP)) % blocks


def partner(me, m, blocks, sender):
    q = lax.rem(me, GROUP)
    if m >= GROUP:
        return me - q + m - GROUP
    r = lax.bitwise_xor(q, m)
    after = (q <= r) if sender else (r > q)
    step = jnp.where(after, blocks - GROUP, GROUP)
    return lax.rem(me - q + r + step, blocks)


def dot(a, b):
    return jnp.dot(a, b, preferred_element_type=jnp.float32)


def dot_rows(a, b):
    return lax.dot_general(a, b, (((1,), (1,)), ((), ())), preferred_element_type=jnp.float32)


def pick_rows(messages, label, rank, count, normed, out_refs):
    segments = label.shape[0]
    slot = lax.broadcasted_iota(jnp.int32, (ROOM, LANES), 0)
    lane = lax.broadcasted_iota(jnp.int32, (ROOM, LANES), 1)
    pick = []
    for m in messages:
        key = jnp.where(label == m, rank, -1)
        here = [jnp.where(slot == key[s : s + 1], 1.0, 0.0) for s in range(segments)]
        pick.append(jnp.concatenate([h.astype(jnp.bfloat16) for h in here], axis=1))
    picked = dot(jnp.concatenate(pick, axis=0), normed)
    for i, (m, out_ref) in enumerate(zip(messages, out_refs)):
        rows = picked[i * ROOM : (i + 1) * ROOM]
        empty = (slot >= count[m : m + 1]) & (lane == 0)
        first = jnp.where(empty, EMPTY, rows[:, :LANES])
        out_ref[:, :LANES] = first.astype(jnp.bfloat16)
        out_ref[:, LANES:] = rows[:, LANES:].astype(jnp.bfloat16)


def pack_far_kernel(blocks, emb_ref, id_ref, *refs):
    far, refs = refs[:GROUP], refs[GROUP:]
    normed, label_ref, rank_ref, count_ref, over_ref, raw, arrived = refs
    rows, width = normed.shape
    segments = rows // LANES
    copies = []
    for s in range(segments):
        part = pl.ds(s * LANES, LANES)
        copies.append(pltpu.make_async_copy(emb_ref.at[part], raw.at[part], arrived.at[s]))
        copies[-1].start()

    me = lax.axis_index("blk")
    ids = id_ref[...]
    q = lax.rem(me, GROUP)
    offset = lax.rem(me - ids + 2 * blocks, blocks)
    turn = lax.bitwise_and(q - offset + SPAN, SPAN - 1)
    label = jnp.where(turn < GROUP, lax.bitwise_xor(turn, q), turn)
    label = jnp.where(ids >= 0, label, SPAN)
    member = [jnp.where(label == m, 1.0, 0.0) for m in range(SPAN)]
    stacked = jnp.concatenate(member, axis=0).astype(jnp.bfloat16)
    before = lax.broadcasted_iota(jnp.int32, (LANES, LANES), 0) < lax.broadcasted_iota(
        jnp.int32, (LANES, LANES), 1
    )
    before = jnp.where(before, 1.0, 0.0).astype(jnp.bfloat16)
    ones = jnp.ones((LANES, LANES), jnp.bfloat16)
    size = SPAN * segments
    r = lax.broadcasted_iota(jnp.int32, (size, size), 0)
    c = lax.broadcasted_iota(jnp.int32, (size, size), 1)
    earlier = (lax.div(r, segments) == lax.div(c, segments)) & (c < r)
    earlier = jnp.where(earlier, 1.0, 0.0).astype(jnp.bfloat16)
    r = lax.broadcasted_iota(jnp.int32, (SPAN, size), 0)
    c = lax.broadcasted_iota(jnp.int32, (SPAN, size), 1)
    same = jnp.where(r == lax.div(c, segments), 1.0, 0.0).astype(jnp.bfloat16)
    within = dot(stacked, before)
    start = dot(dot(earlier, stacked).astype(jnp.bfloat16), ones)
    count = dot(dot(same, stacked).astype(jnp.bfloat16), ones).astype(jnp.int32)
    place = (within + start).astype(jnp.int32)
    rank = jnp.zeros_like(ids)
    for m in range(SPAN):
        rank = jnp.where(label == m, place[m * segments : (m + 1) * segments], rank)
    label_ref[...] = label
    rank_ref[...] = rank
    count_ref[...] = count
    over_ref[...] = jnp.max(jnp.where(count > ROOM, 1.0, 0.0), axis=0, keepdims=True)

    for s in range(segments):
        part = pl.ds(s * LANES, LANES)
        copies[s].wait()
        x = raw[part]
        scale = lax.rsqrt(jnp.sum(x * x, axis=1, keepdims=True) + 1e-06)
        normed[part] = (x * scale).astype(jnp.bfloat16)

    pick_rows(range(GROUP), label, rank, count, normed[...], far)


def pack_far(embeddings, ids, blocks):
    rows, width = embeddings.shape
    segments = rows // LANES
    vmem = pl.BlockSpec(memory_space=pltpu.VMEM)
    shapes = [jax.ShapeDtypeStruct((ROOM, width), jnp.bfloat16)] * GROUP
    shapes += [jax.ShapeDtypeStruct((rows, width), jnp.bfloat16)]
    shapes += [jax.ShapeDtypeStruct((segments, LANES), jnp.int32)] * 2
    shapes += [jax.ShapeDtypeStruct((SPAN, LANES), jnp.int32)]
    shapes += [jax.ShapeDtypeStruct((1, LANES), jnp.float32)]
    return pl.pallas_call(
        functools.partial(pack_far_kernel, blocks),
        out_shape=shapes,
        in_specs=[pl.BlockSpec(memory_space=pl.ANY), vmem],
        out_specs=[vmem] * len(shapes),
        scratch_shapes=[
            pltpu.VMEM((rows, width), jnp.float32),
            pltpu.SemaphoreType.DMA((segments,)),
        ],
        compiler_params=pltpu.CompilerParams(vmem_limit_bytes=PACK_VMEM),
        cost_estimate=pl.CostEstimate(
            flops=2 * GROUP * ROOM * rows * width, bytes_accessed=rows * width * 4, transcendentals=rows
        ),
        name="pack_far",
    )(embeddings, ids)


def pack_near_kernel(normed, label_ref, rank_ref, count_ref, near_ref):
    out_refs = [near_ref.at[pl.ds(r * ROOM, ROOM)] for r in range(GROUP)]
    label, rank, count = label_ref[...], rank_ref[...], count_ref[...]
    pick_rows(range(GROUP, SPAN), label, rank, count, normed[...], out_refs)


def pack_near(normed, label, rank, count):
    rows, width = normed.shape
    vmem = pl.BlockSpec(memory_space=pltpu.VMEM)
    return pl.pallas_call(
        pack_near_kernel,
        out_shape=jax.ShapeDtypeStruct((GROUP * ROOM, width), jnp.bfloat16),
        in_specs=[vmem] * 4,
        out_specs=vmem,
        compiler_params=pltpu.CompilerParams(vmem_limit_bytes=PACK_VMEM),
        cost_estimate=pl.CostEstimate(
            flops=2 * GROUP * ROOM * rows * width, bytes_accessed=rows * width * 4, transcendentals=0
        ),
        name="pack_near",
    )(normed, label, rank, count)


def penalty(rows):
    return jnp.where(rows[:, :LANES].astype(jnp.float32)[:, :1] > 1.5, -4.0, 0.0)


def best_within(rows):
    scores = dot_rows(rows, rows) + penalty(rows)
    i = lax.broadcasted_iota(jnp.int32, scores.shape, 0)
    j = lax.broadcasted_iota(jnp.int32, scores.shape, 1)
    return jnp.max(jnp.where(i == j, -1.0, scores), axis=0, keepdims=True)


def best_across(rows, columns):
    return jnp.max(dot_rows(rows, columns) + penalty(rows), axis=0, keepdims=True)


def score_near_kernel(near_ref, best_ref):
    best_ref[...] = best_within(near_ref[...])


def score_near(near):
    rows, width = near.shape
    vmem = pl.BlockSpec(memory_space=pltpu.VMEM)
    return pl.pallas_call(
        score_near_kernel,
        out_shape=jax.ShapeDtypeStruct((1, rows), jnp.float32),
        in_specs=[vmem],
        out_specs=vmem,
        compiler_params=pltpu.CompilerParams(vmem_limit_bytes=SCORE_VMEM),
        cost_estimate=pl.CostEstimate(
            flops=2 * rows * rows * width, bytes_accessed=rows * width * 2, transcendentals=0
        ),
        name="score_near",
    )(near)


def score_kernel(blocks, *refs):
    far, (near_ref, before_ref, over_ref, other_ref, best_ref, far_ref) = refs[:GROUP], refs[GROUP:]
    room = far[0].shape[0]
    me = lax.axis_index("blk")
    flag = jnp.maximum(over_ref[...], other_ref[...])
    padded = best_ref.shape[2]
    best_ref[...] = jnp.concatenate([flag[None]] * (padded // LANES), axis=2) + jnp.zeros_like(best_ref)
    for k in range(GROUP):
        far_ref[k * room : (k + 1) * room] = far[k][...]
    far_rows, near_rows = far_ref[...], near_ref[...]
    best_far = jnp.maximum(best_within(far_rows), best_across(near_rows, far_rows))
    best_near = jnp.maximum(before_ref[...], best_across(far_rows, near_rows))
    for m in range(SPAN):
        best = best_far if m < GROUP else best_near
        first = m % GROUP * room
        top = jnp.maximum(best[:, first : first + room], -1.0)
        best_ref[partner(me, m, blocks, True), :, :room] = top


def score(far, near, before, over, other, blocks):
    room, width = far[0].shape
    padded = (pl.cdiv(room, LANES) if room % LANES else room // LANES + 1) * LANES
    vmem = pl.BlockSpec(memory_space=pltpu.VMEM)
    return pl.pallas_call(
        functools.partial(score_kernel, blocks),
        out_shape=jax.ShapeDtypeStruct((blocks, 1, padded), jnp.float32),
        in_specs=[vmem] * (GROUP + 4),
        out_specs=vmem,
        scratch_shapes=[pltpu.VMEM((GROUP * room, width), jnp.bfloat16)],
        compiler_params=pltpu.CompilerParams(vmem_limit_bytes=SCORE_VMEM),
        name="score",
    )(*far, near, before, over, other)


def unpack_kernel(blocks, best_ref, label_ref, rank_ref, out_ref, over_ref):
    label, rank = label_ref[...], rank_ref[...]
    padded = best_ref.shape[2]
    me = lax.axis_index("blk")
    inner = lax.bitwise_and(rank, LANES - 1)
    result = jnp.full(label.shape, -1.0, jnp.float32)
    for m in range(SPAN):
        best = best_ref[partner(me, m, blocks, False)]
        for start in range(0, padded, LANES):
            table = jnp.broadcast_to(best[:, start : start + LANES], label.shape)
            value = jnp.take_along_axis(table, inner, axis=1)
            here = (label == m) & (rank >= start) & (rank < start + LANES)
            result = jnp.where(here, value, result)
    out_ref[...] = result
    flags = jnp.max(best_ref[:, :, padded - LANES :], axis=0)
    lane = lax.broadcasted_iota(jnp.int32, flags.shape, 1)
    over_ref[0, 0] = jnp.max(jnp.where(lane == LANES - 1, flags, 0.0))


def unpack(best, label, rank):
    vmem = pl.BlockSpec(memory_space=pltpu.VMEM)
    return pl.pallas_call(
        functools.partial(unpack_kernel, best.shape[0]),
        out_shape=[
            jax.ShapeDtypeStruct(label.shape, jnp.float32),
            jax.ShapeDtypeStruct((1, 1), jnp.float32),
        ],
        in_specs=[vmem] * 3,
        out_specs=[vmem, pl.BlockSpec(memory_space=pltpu.SMEM)],
        compiler_params=pltpu.CompilerParams(vmem_limit_bytes=4 * 1024 * 1024),
        name="unpack",
    )(best, label, rank)


def local(embeddings, cluster_id):
    blocks = lax.axis_size("blk")
    ids = cluster_id.reshape(-1, LANES)
    *far, normed, label, rank, count, over = pack_far(embeddings, ids, blocks)
    for k in range(GROUP):
        route = [(i, outside(i, k, blocks)) for i in range(blocks)]
        far[k] = lax.ppermute(far[k], "blk", route)
    groups = [list(range(i, i + GROUP)) for i in range(0, blocks, GROUP)]
    near = pack_near(normed, label, rank, count)
    near = lax.all_to_all(near, "blk", 0, 0, axis_index_groups=groups, tiled=True)
    other = over
    for distance in range(1, lax.axis_size("parts")):
        other = jnp.maximum(other, shifted(over, "parts", distance))
    before = score_near(near)
    best = score(far, near, before, over, other, blocks)
    returned = lax.all_to_all(best, "blk", 0, 0, tiled=True)
    packed, flag = unpack(returned, label, rank)
    return lax.cond(
        flag[0, 0] > 0, lambda: by_ring(embeddings, cluster_id), lambda: packed.reshape(-1)
    )


def solution(mesh):
    in_specs = (P(("parts", "blk"), None), P(("parts", "blk")))
    out_specs = P(("parts", "blk"))
    return jax.shard_map(local, mesh=mesh, in_specs=in_specs, out_specs=out_specs, check_vma=False)
```

```python
import functools

import jax
import jax.numpy as jnp
from jax import lax
from jax.experimental import pallas as pl
from jax.experimental.pallas import tpu as pltpu
from jax.sharding import PartitionSpec as P

SPAN = 8
HOME = 4
GROUP = 4
ROOM = 176
LANES = 128
EMPTY = 2.0
PACK_VMEM = 24 * 1024 * 1024
SCORE_VMEM = 20 * 1024 * 1024


def shifted(block, axis, distance):
    if distance == 0:
        return block
    size = lax.axis_size(axis)
    route = [(i, (i + distance) % size) for i in range(size)]
    return lax.ppermute(block, axis, route)


def block_max(left, left_id, right, right_id, same_block):
    scores = lax.dot_general(
        left, right, (((1,), (1,)), ((), ())), preferred_element_type=jnp.float32
    )
    match = (left_id[:, None] == right_id[None, :]) & (left_id[:, None] >= 0)
    if same_block:
        count = left.shape[0]
        match = match & (jnp.arange(count)[:, None] != jnp.arange(count)[None, :])
    masked = jnp.where(match, scores, jnp.float32(-1.0))
    return (jnp.max(masked, axis=1), jnp.max(masked, axis=0))


def by_ring(embeddings, cluster_id):
    scale = lax.rsqrt(jnp.sum(embeddings * embeddings, axis=1, keepdims=True) + 1e-06)
    normed = (embeddings * scale).astype(jnp.bfloat16)
    best, unused_cols = block_max(normed, cluster_id, normed, cluster_id, True)
    visitor = (normed, cluster_id)
    for offset in range(1, SPAN):
        visitor = (shifted(visitor[0], "blk", 1), shifted(visitor[1], "blk", 1))
        row_best, col_best = block_max(normed, cluster_id, visitor[0], visitor[1], False)
        returned = shifted(col_best, "blk", -offset)
        best = jnp.maximum(best, jnp.maximum(row_best, returned))
    return best


def outside(block, k, blocks):
    q = block % GROUP
    r = q ^ k
    return (block - q + r + (GROUP if r <= q else -GROUP)) % blocks


def partner(me, m, blocks, sender):
    q = lax.rem(me, GROUP)
    if m >= GROUP:
        return me - q + m - GROUP
    r = lax.bitwise_xor(q, m)
    after = (q <= r) if sender else (r > q)
    step = jnp.where(after, blocks - GROUP, GROUP)
    return lax.rem(me - q + r + step, blocks)


def dot(a, b):
    return jnp.dot(a, b, preferred_element_type=jnp.float32)


def dot_rows(a, b):
    return lax.dot_general(a, b, (((1,), (1,)), ((), ())), preferred_element_type=jnp.float32)


def pick_rows(messages, label, rank, count, normed, out_refs):
    segments = label.shape[0]
    slot = lax.broadcasted_iota(jnp.int32, (ROOM, LANES), 0)
    lane = lax.broadcasted_iota(jnp.int32, (ROOM, LANES), 1)
    pick = []
    for m in messages:
        key = jnp.where(label == m, rank, -1)
        here = [jnp.where(slot == key[s : s + 1], 1.0, 0.0) for s in range(segments)]
        pick.append(jnp.concatenate([h.astype(jnp.bfloat16) for h in here], axis=1))
    picked = dot(jnp.concatenate(pick, axis=0), normed)
    for i, (m, out_ref) in enumerate(zip(messages, out_refs)):
        rows = picked[i * ROOM : (i + 1) * ROOM]
        empty = (slot >= count[m : m + 1]) & (lane == 0)
        first = jnp.where(empty, EMPTY, rows[:, :LANES])
        out_ref[:, :LANES] = first.astype(jnp.bfloat16)
        out_ref[:, LANES:] = rows[:, LANES:].astype(jnp.bfloat16)


def pack_far_kernel(blocks, emb_ref, id_ref, *refs):
    far, refs = refs[:GROUP], refs[GROUP:]
    normed, label_ref, rank_ref, count_ref, over_ref, raw, arrived = refs
    rows, width = normed.shape
    segments = rows // LANES
    copies = []
    for s in range(segments):
        part = pl.ds(s * LANES, LANES)
        copies.append(pltpu.make_async_copy(emb_ref.at[part], raw.at[part], arrived.at[s]))
        copies[-1].start()

    me = lax.axis_index("blk")
    ids = id_ref[...]
    q = lax.rem(me, GROUP)
    offset = lax.rem(me - ids + 2 * blocks, blocks)
    turn = lax.bitwise_and(q - offset + SPAN, SPAN - 1)
    label = jnp.where(turn < GROUP, lax.bitwise_xor(turn, q), turn)
    label = jnp.where(ids >= 0, label, SPAN)
    member = [jnp.where(label == m, 1.0, 0.0) for m in range(SPAN)]
    stacked = jnp.concatenate(member, axis=0).astype(jnp.bfloat16)
    before = lax.broadcasted_iota(jnp.int32, (LANES, LANES), 0) < lax.broadcasted_iota(
        jnp.int32, (LANES, LANES), 1
    )
    before = jnp.where(before, 1.0, 0.0).astype(jnp.bfloat16)
    ones = jnp.ones((LANES, LANES), jnp.bfloat16)
    size = SPAN * segments
    r = lax.broadcasted_iota(jnp.int32, (size, size), 0)
    c = lax.broadcasted_iota(jnp.int32, (size, size), 1)
    earlier = (lax.div(r, segments) == lax.div(c, segments)) & (c < r)
    earlier = jnp.where(earlier, 1.0, 0.0).astype(jnp.bfloat16)
    r = lax.broadcasted_iota(jnp.int32, (SPAN, size), 0)
    c = lax.broadcasted_iota(jnp.int32, (SPAN, size), 1)
    same = jnp.where(r == lax.div(c, segments), 1.0, 0.0).astype(jnp.bfloat16)
    within = dot(stacked, before)
    start = dot(dot(earlier, stacked).astype(jnp.bfloat16), ones)
    count = dot(dot(same, stacked).astype(jnp.bfloat16), ones).astype(jnp.int32)
    place = (within + start).astype(jnp.int32)
    rank = jnp.zeros_like(ids)
    for m in range(SPAN):
        rank = jnp.where(label == m, place[m * segments : (m + 1) * segments], rank)
    label_ref[...] = label
    rank_ref[...] = rank
    count_ref[...] = count
    over_ref[...] = jnp.max(jnp.where(count > ROOM, 1.0, 0.0), axis=0, keepdims=True)

    for s in range(segments):
        part = pl.ds(s * LANES, LANES)
        copies[s].wait()
        x = raw[part]
        scale = lax.rsqrt(jnp.sum(x * x, axis=1, keepdims=True) + 1e-06)
        normed[part] = (x * scale).astype(jnp.bfloat16)

    pick_rows(range(GROUP), label, rank, count, normed[...], far)


def pack_far(embeddings, ids, blocks):
    rows, width = embeddings.shape
    segments = rows // LANES
    vmem = pl.BlockSpec(memory_space=pltpu.VMEM)
    shapes = [jax.ShapeDtypeStruct((ROOM, width), jnp.bfloat16)] * GROUP
    shapes += [jax.ShapeDtypeStruct((rows, width), jnp.bfloat16)]
    shapes += [jax.ShapeDtypeStruct((segments, LANES), jnp.int32)] * 2
    shapes += [jax.ShapeDtypeStruct((SPAN, LANES), jnp.int32)]
    shapes += [jax.ShapeDtypeStruct((1, LANES), jnp.float32)]
    return pl.pallas_call(
        functools.partial(pack_far_kernel, blocks),
        out_shape=shapes,
        in_specs=[pl.BlockSpec(memory_space=pl.ANY), vmem],
        out_specs=[vmem] * len(shapes),
        scratch_shapes=[
            pltpu.VMEM((rows, width), jnp.float32),
            pltpu.SemaphoreType.DMA((segments,)),
        ],
        compiler_params=pltpu.CompilerParams(vmem_limit_bytes=PACK_VMEM),
        cost_estimate=pl.CostEstimate(
            flops=2 * GROUP * ROOM * rows * width, bytes_accessed=rows * width * 4, transcendentals=rows
        ),
        name="pack_far",
    )(embeddings, ids)


def pack_near_kernel(normed, label_ref, rank_ref, count_ref, after_ref, near_ref):
    out_refs = [near_ref.at[pl.ds(r * ROOM, ROOM)] for r in range(GROUP)]
    label, rank, count = label_ref[...], rank_ref[...], count_ref[...]
    pick_rows(range(GROUP, SPAN), label, rank, count, normed[...], out_refs)


def pack_near(normed, label, rank, count, after):
    rows, width = normed.shape
    vmem = pl.BlockSpec(memory_space=pltpu.VMEM)
    return pl.pallas_call(
        pack_near_kernel,
        out_shape=jax.ShapeDtypeStruct((GROUP * ROOM, width), jnp.bfloat16),
        in_specs=[vmem] * 5,
        out_specs=vmem,
        compiler_params=pltpu.CompilerParams(vmem_limit_bytes=PACK_VMEM),
        cost_estimate=pl.CostEstimate(
            flops=2 * GROUP * ROOM * rows * width, bytes_accessed=rows * width * 4, transcendentals=0
        ),
        name="pack_near",
    )(normed, label, rank, count, after)


def penalty(rows):
    return jnp.where(rows[:, :LANES].astype(jnp.float32)[:, :1] > 1.5, -4.0, 0.0)


def best_within(rows):
    scores = dot_rows(rows, rows) + penalty(rows)
    i = lax.broadcasted_iota(jnp.int32, scores.shape, 0)
    j = lax.broadcasted_iota(jnp.int32, scores.shape, 1)
    return jnp.max(jnp.where(i == j, -1.0, scores), axis=0, keepdims=True)


def best_across(rows, columns):
    return jnp.max(dot_rows(rows, columns) + penalty(rows), axis=0, keepdims=True)


def score_near_kernel(near_ref, best_ref):
    best_ref[...] = best_within(near_ref[...])


def score_near(near):
    rows, width = near.shape
    vmem = pl.BlockSpec(memory_space=pltpu.VMEM)
    return pl.pallas_call(
        score_near_kernel,
        out_shape=jax.ShapeDtypeStruct((1, rows), jnp.float32),
        in_specs=[vmem],
        out_specs=vmem,
        compiler_params=pltpu.CompilerParams(vmem_limit_bytes=SCORE_VMEM),
        cost_estimate=pl.CostEstimate(
            flops=2 * rows * rows * width, bytes_accessed=rows * width * 2, transcendentals=0
        ),
        name="score_near",
    )(near)


def join(far, near_ref, before):
    last = far[-1][...]
    best_last = best_within(last)
    best_near = jnp.maximum(before[0], best_across(last, near_ref[...]))
    best_last = jnp.maximum(best_last, best_across(near_ref[...], last))
    bests = [best_near]
    for other, best in zip(far[:-1], before[1:]):
        bests.append(jnp.maximum(best, best_across(last, other[...])))
        best_last = jnp.maximum(best_last, best_across(other[...], last))
    return bests + [best_last]


def score_step_kernel(count, *refs):
    far, near_ref, before, after = refs[:count], refs[count], refs[count + 1 : 2 * count + 1], refs[2 * count + 1 :]
    for ref, best in zip(after, join(far, near_ref, [b[...] for b in before])):
        ref[...] = best


def score_step(far, near, before):
    room, width = far[0].shape
    vmem = pl.BlockSpec(memory_space=pltpu.VMEM)
    count = len(far)
    shapes = [jax.ShapeDtypeStruct(near.shape[:1], jnp.float32)] + [jax.ShapeDtypeStruct((room,), jnp.float32)] * count
    shapes = [jax.ShapeDtypeStruct((1,) + s.shape, s.dtype) for s in shapes]
    return pl.pallas_call(
        functools.partial(score_step_kernel, count),
        out_shape=shapes,
        in_specs=[vmem] * (2 * count + 1),
        out_specs=[vmem] * (count + 1),
        compiler_params=pltpu.CompilerParams(vmem_limit_bytes=SCORE_VMEM),
        cost_estimate=pl.CostEstimate(
            flops=4 * room * (near.shape[0] + count * room) * width, bytes_accessed=near.shape[0] * width * 2, transcendentals=0
        ),
        name=f"score_step{count}",
    )(*far, near, *before)


def score_last_kernel(blocks, *refs):
    far, near_ref, refs = refs[:GROUP], refs[GROUP], refs[GROUP + 1 :]
    before, (over_ref, other_ref, best_ref) = refs[:GROUP], refs[GROUP:]
    room = far[0].shape[0]
    me = lax.axis_index("blk")
    flag = jnp.maximum(over_ref[...], other_ref[...])
    padded = best_ref.shape[2]
    best_ref[...] = jnp.concatenate([flag[None]] * (padded // LANES), axis=2) + jnp.zeros_like(best_ref)
    best_near, *bests = join(far, near_ref, [b[...] for b in before])
    bests += [best_near[:, r * room : (r + 1) * room] for r in range(GROUP)]
    for m, best in enumerate(bests):
        best_ref[partner(me, m, blocks, True), :, :room] = jnp.maximum(best, -1.0)


def score_last(far, near, before, over, other, blocks):
    room, width = far[0].shape
    padded = (pl.cdiv(room, LANES) if room % LANES else room // LANES + 1) * LANES
    vmem = pl.BlockSpec(memory_space=pltpu.VMEM)
    return pl.pallas_call(
        functools.partial(score_last_kernel, blocks),
        out_shape=jax.ShapeDtypeStruct((blocks, 1, padded), jnp.float32),
        in_specs=[vmem] * (2 * GROUP + 3),
        out_specs=vmem,
        compiler_params=pltpu.CompilerParams(vmem_limit_bytes=SCORE_VMEM),
        name="score_last",
    )(*far, near, *before, over, other)


def unpack_kernel(blocks, best_ref, label_ref, rank_ref, out_ref, over_ref):
    label, rank = label_ref[...], rank_ref[...]
    padded = best_ref.shape[2]
    me = lax.axis_index("blk")
    inner = lax.bitwise_and(rank, LANES - 1)
    result = jnp.full(label.shape, -1.0, jnp.float32)
    for m in range(SPAN):
        best = best_ref[partner(me, m, blocks, False)]
        for start in range(0, padded, LANES):
            table = jnp.broadcast_to(best[:, start : start + LANES], label.shape)
            value = jnp.take_along_axis(table, inner, axis=1)
            here = (label == m) & (rank >= start) & (rank < start + LANES)
            result = jnp.where(here, value, result)
    out_ref[...] = result
    flags = jnp.max(best_ref[:, :, padded - LANES :], axis=0)
    lane = lax.broadcasted_iota(jnp.int32, flags.shape, 1)
    over_ref[0, 0] = jnp.max(jnp.where(lane == LANES - 1, flags, 0.0))


def unpack(best, label, rank):
    vmem = pl.BlockSpec(memory_space=pltpu.VMEM)
    return pl.pallas_call(
        functools.partial(unpack_kernel, best.shape[0]),
        out_shape=[
            jax.ShapeDtypeStruct(label.shape, jnp.float32),
            jax.ShapeDtypeStruct((1, 1), jnp.float32),
        ],
        in_specs=[vmem] * 3,
        out_specs=[vmem, pl.BlockSpec(memory_space=pltpu.SMEM)],
        compiler_params=pltpu.CompilerParams(vmem_limit_bytes=4 * 1024 * 1024),
        name="unpack",
    )(best, label, rank)


def local(embeddings, cluster_id):
    blocks = lax.axis_size("blk")
    ids = cluster_id.reshape(-1, LANES)
    *far, normed, label, rank, count, over = pack_far(embeddings, ids, blocks)
    for k in range(GROUP):
        route = [(i, outside(i, k, blocks)) for i in range(blocks)]
        far[k] = lax.ppermute(far[k], "blk", route)
    groups = [list(range(i, i + GROUP)) for i in range(0, blocks, GROUP)]
    other = over
    for distance in range(1, lax.axis_size("parts")):
        other = jnp.maximum(other, shifted(over, "parts", distance))
    near = pack_near(normed, label, rank, count, other)
    near = lax.all_to_all(near, "blk", 0, 0, axis_index_groups=groups, tiled=True)
    bests = [score_near(near)]
    for k in range(1, GROUP):
        bests = score_step(far[:k], near, bests)
    best = score_last(far, near, bests, over, other, blocks)
    returned = lax.all_to_all(best, "blk", 0, 0, tiled=True)
    packed, flag = unpack(returned, label, rank)
    return lax.cond(
        flag[0, 0] > 0, lambda: by_ring(embeddings, cluster_id), lambda: packed.reshape(-1)
    )


def solution(mesh):
    in_specs = (P(("parts", "blk"), None), P(("parts", "blk")))
    out_specs = P(("parts", "blk"))
    return jax.shard_map(local, mesh=mesh, in_specs=in_specs, out_specs=out_specs, check_vma=False)
```

```python
import functools

import jax
import jax.numpy as jnp
from jax import lax
from jax.experimental import pallas as pl
from jax.experimental.pallas import tpu as pltpu
from jax.sharding import PartitionSpec as P

SPAN = 8
HOME = 4
GROUP = 4
ROOM = 176
LANES = 128
EMPTY = 2.0
PACK_VMEM = 24 * 1024 * 1024
SCORE_VMEM = 20 * 1024 * 1024


def shifted(block, axis, distance):
    if distance == 0:
        return block
    size = lax.axis_size(axis)
    route = [(i, (i + distance) % size) for i in range(size)]
    return lax.ppermute(block, axis, route)


def block_max(left, left_id, right, right_id, same_block):
    scores = lax.dot_general(
        left, right, (((1,), (1,)), ((), ())), preferred_element_type=jnp.float32
    )
    match = (left_id[:, None] == right_id[None, :]) & (left_id[:, None] >= 0)
    if same_block:
        count = left.shape[0]
        match = match & (jnp.arange(count)[:, None] != jnp.arange(count)[None, :])
    masked = jnp.where(match, scores, jnp.float32(-1.0))
    return (jnp.max(masked, axis=1), jnp.max(masked, axis=0))


def by_ring(embeddings, cluster_id):
    scale = lax.rsqrt(jnp.sum(embeddings * embeddings, axis=1, keepdims=True) + 1e-06)
    normed = (embeddings * scale).astype(jnp.bfloat16)
    best, unused_cols = block_max(normed, cluster_id, normed, cluster_id, True)
    visitor = (normed, cluster_id)
    for offset in range(1, SPAN):
        visitor = (shifted(visitor[0], "blk", 1), shifted(visitor[1], "blk", 1))
        row_best, col_best = block_max(normed, cluster_id, visitor[0], visitor[1], False)
        returned = shifted(col_best, "blk", -offset)
        best = jnp.maximum(best, jnp.maximum(row_best, returned))
    return best


OWN = GROUP
FAR = (0, 1, 2, 3)
NEAR = (6, 7, 5)
STEPS = ((OWN, 0, 1, 2), NEAR, (3,))


def target(block, m, blocks):
    q = block % GROUP
    r = q ^ (m % GROUP)
    step = 0 if m >= GROUP else GROUP if r <= q else -GROUP
    return (block - q + r + step) % blocks


def partner(me, m, blocks, sender):
    q = lax.rem(me, GROUP)
    r = lax.bitwise_xor(q, m % GROUP)
    if m >= GROUP:
        return me - q + r
    back = (q <= r) if sender else (r > q)
    step = jnp.where(back, blocks - GROUP, GROUP)
    return lax.rem(me - q + r + step, blocks)


def send(rows, m):
    blocks = lax.axis_size("blk")
    return lax.ppermute(rows, "blk", [(i, target(i, m, blocks)) for i in range(blocks)])


def dot(a, b):
    return jnp.dot(a, b, preferred_element_type=jnp.float32)


def dot_rows(a, b):
    return lax.dot_general(a, b, (((1,), (1,)), ((), ())), preferred_element_type=jnp.float32)


def pick_rows(messages, label, rank, count, normed, out_refs):
    segments = label.shape[0]
    slot = lax.broadcasted_iota(jnp.int32, (ROOM, LANES), 0)
    lane = lax.broadcasted_iota(jnp.int32, (ROOM, LANES), 1)
    pick = []
    for m in messages:
        key = jnp.where(label == m, rank, -1)
        here = [jnp.where(slot == key[s : s + 1], 1.0, 0.0) for s in range(segments)]
        pick.append(jnp.concatenate([h.astype(jnp.bfloat16) for h in here], axis=1))
    picked = dot(jnp.concatenate(pick, axis=0), normed)
    for i, (m, out_ref) in enumerate(zip(messages, out_refs)):
        rows = picked[i * ROOM : (i + 1) * ROOM]
        empty = (slot >= count[m : m + 1]) & (lane == 0)
        first = jnp.where(empty, EMPTY, rows[:, :LANES])
        out_ref[:, :LANES] = first.astype(jnp.bfloat16)
        out_ref[:, LANES:] = rows[:, LANES:].astype(jnp.bfloat16)


def pack_far_kernel(blocks, emb_ref, id_ref, *refs):
    far, refs = refs[:GROUP], refs[GROUP:]
    normed, label_ref, rank_ref, count_ref, over_ref, raw, arrived = refs
    rows, width = normed.shape
    segments = rows // LANES
    copies = []
    for s in range(segments):
        part = pl.ds(s * LANES, LANES)
        copies.append(pltpu.make_async_copy(emb_ref.at[part], raw.at[part], arrived.at[s]))
        copies[-1].start()

    me = lax.axis_index("blk")
    ids = id_ref[...]
    q = lax.rem(me, GROUP)
    offset = lax.rem(me - ids + 2 * blocks, blocks)
    turn = lax.bitwise_and(q - offset + SPAN, SPAN - 1)
    label = jnp.where(ids >= 0, lax.bitwise_xor(turn, q), SPAN)
    member = [jnp.where(label == m, 1.0, 0.0) for m in range(SPAN)]
    stacked = jnp.concatenate(member, axis=0).astype(jnp.bfloat16)
    before = lax.broadcasted_iota(jnp.int32, (LANES, LANES), 0) < lax.broadcasted_iota(
        jnp.int32, (LANES, LANES), 1
    )
    before = jnp.where(before, 1.0, 0.0).astype(jnp.bfloat16)
    ones = jnp.ones((LANES, LANES), jnp.bfloat16)
    size = SPAN * segments
    r = lax.broadcasted_iota(jnp.int32, (size, size), 0)
    c = lax.broadcasted_iota(jnp.int32, (size, size), 1)
    earlier = (lax.div(r, segments) == lax.div(c, segments)) & (c < r)
    earlier = jnp.where(earlier, 1.0, 0.0).astype(jnp.bfloat16)
    r = lax.broadcasted_iota(jnp.int32, (SPAN, size), 0)
    c = lax.broadcasted_iota(jnp.int32, (SPAN, size), 1)
    same = jnp.where(r == lax.div(c, segments), 1.0, 0.0).astype(jnp.bfloat16)
    within = dot(stacked, before)
    start = dot(dot(earlier, stacked).astype(jnp.bfloat16), ones)
    count = dot(dot(same, stacked).astype(jnp.bfloat16), ones).astype(jnp.int32)
    place = (within + start).astype(jnp.int32)
    rank = jnp.zeros_like(ids)
    for m in range(SPAN):
        rank = jnp.where(label == m, place[m * segments : (m + 1) * segments], rank)
    label_ref[...] = label
    rank_ref[...] = rank
    count_ref[...] = count
    over_ref[...] = jnp.max(jnp.where(count > ROOM, 1.0, 0.0), axis=0, keepdims=True)

    for s in range(segments):
        part = pl.ds(s * LANES, LANES)
        copies[s].wait()
        x = raw[part]
        scale = lax.rsqrt(jnp.sum(x * x, axis=1, keepdims=True) + 1e-06)
        normed[part] = (x * scale).astype(jnp.bfloat16)

    pick_rows(FAR, label, rank, count, normed[...], far)


def pack_far(embeddings, ids, blocks):
    rows, width = embeddings.shape
    segments = rows // LANES
    vmem = pl.BlockSpec(memory_space=pltpu.VMEM)
    shapes = [jax.ShapeDtypeStruct((ROOM, width), jnp.bfloat16)] * GROUP
    shapes += [jax.ShapeDtypeStruct((rows, width), jnp.bfloat16)]
    shapes += [jax.ShapeDtypeStruct((segments, LANES), jnp.int32)] * 2
    shapes += [jax.ShapeDtypeStruct((SPAN, LANES), jnp.int32)]
    shapes += [jax.ShapeDtypeStruct((1, LANES), jnp.float32)]
    return pl.pallas_call(
        functools.partial(pack_far_kernel, blocks),
        out_shape=shapes,
        in_specs=[pl.BlockSpec(memory_space=pl.ANY), vmem],
        out_specs=[vmem] * len(shapes),
        scratch_shapes=[
            pltpu.VMEM((rows, width), jnp.float32),
            pltpu.SemaphoreType.DMA((segments,)),
        ],
        compiler_params=pltpu.CompilerParams(vmem_limit_bytes=PACK_VMEM),
        cost_estimate=pl.CostEstimate(
            flops=2 * GROUP * ROOM * rows * width, bytes_accessed=rows * width * 4, transcendentals=rows
        ),
        name="pack_far",
    )(embeddings, ids)


def pack_near_kernel(normed, label_ref, rank_ref, count_ref, *out_refs):
    label, rank, count = label_ref[...], rank_ref[...], count_ref[...]
    pick_rows(NEAR + (OWN,), label, rank, count, normed[...], out_refs)


def pack_near(normed, label, rank, count):
    rows, width = normed.shape
    vmem = pl.BlockSpec(memory_space=pltpu.VMEM)
    return pl.pallas_call(
        pack_near_kernel,
        out_shape=[jax.ShapeDtypeStruct((ROOM, width), jnp.bfloat16)] * GROUP,
        in_specs=[vmem] * 4,
        out_specs=[vmem] * GROUP,
        compiler_params=pltpu.CompilerParams(vmem_limit_bytes=PACK_VMEM),
        cost_estimate=pl.CostEstimate(
            flops=2 * GROUP * ROOM * rows * width, bytes_accessed=rows * width * 4, transcendentals=0
        ),
        name="pack_near",
    )(normed, label, rank, count)


def penalty(rows):
    return jnp.where(rows[:, :LANES].astype(jnp.float32)[:, :1] > 1.5, -4.0, 0.0)


def best_within(rows):
    scores = dot_rows(rows, rows) + penalty(rows)
    i = lax.broadcasted_iota(jnp.int32, scores.shape, 0)
    j = lax.broadcasted_iota(jnp.int32, scores.shape, 1)
    return jnp.max(jnp.where(i == j, -1.0, scores), axis=0, keepdims=True)


def best_across(rows, columns):
    return jnp.max(dot_rows(rows, columns) + penalty(rows), axis=0, keepdims=True)


def stacked(refs):
    return jnp.concatenate([ref[...] for ref in refs], axis=0)


def join(old, new, before):
    rows = stacked(new)
    best = best_within(rows)
    if not old:
        return [best]
    others = stacked(old)
    best_old = jnp.maximum(before, best_across(rows, others))
    return [best_old, jnp.maximum(best, best_across(others, rows))]


def score_step_kernel(olds, news, *refs):
    old, new, refs = refs[:olds], refs[olds : olds + news], refs[olds + news :]
    before = refs[0][...] if olds else None
    refs[-1][...] = jnp.concatenate(join(old, new, before), axis=1)


def score_step(old, new, before):
    room, width = new[0].shape
    vmem = pl.BlockSpec(memory_space=pltpu.VMEM)
    count = len(old) + len(new)
    args = (*old, *new, *before)
    return pl.pallas_call(
        functools.partial(score_step_kernel, len(old), len(new)),
        out_shape=jax.ShapeDtypeStruct((1, count * room), jnp.float32),
        in_specs=[vmem] * len(args),
        out_specs=vmem,
        compiler_params=pltpu.CompilerParams(vmem_limit_bytes=SCORE_VMEM),
        cost_estimate=pl.CostEstimate(
            flops=4 * len(new) * room * count * room * width, bytes_accessed=count * room * width * 2, transcendentals=0
        ),
        name=f"score_{count}",
    )(*args)


def score_last_kernel(blocks, order, olds, *refs):
    old, new, refs = refs[:olds], refs[olds:SPAN], refs[SPAN:]
    before_ref, over_ref, other_ref, best_ref = refs
    room = new[0].shape[0]
    me = lax.axis_index("blk")
    flag = jnp.maximum(over_ref[...], other_ref[...])
    padded = best_ref.shape[2]
    best_ref[...] = jnp.concatenate([flag[None]] * (padded // LANES), axis=2) + jnp.zeros_like(best_ref)
    bests = []
    for best in join(old, new, before_ref[...]):
        bests += [best[:, i : i + room] for i in range(0, best.shape[1], room)]
    for m, best in zip(order, bests):
        best_ref[partner(me, m, blocks, True), :, :room] = jnp.maximum(best, -1.0)


def score_last(order, old, new, before, over, other, blocks):
    room, width = new[0].shape
    padded = (pl.cdiv(room, LANES) if room % LANES else room // LANES + 1) * LANES
    vmem = pl.BlockSpec(memory_space=pltpu.VMEM)
    return pl.pallas_call(
        functools.partial(score_last_kernel, blocks, order, len(old)),
        out_shape=jax.ShapeDtypeStruct((blocks, 1, padded), jnp.float32),
        in_specs=[vmem] * (SPAN + 3),
        out_specs=vmem,
        compiler_params=pltpu.CompilerParams(vmem_limit_bytes=SCORE_VMEM),
        name="score_last",
    )(*old, *new, *before, over, other)


def unpack_kernel(blocks, best_ref, label_ref, rank_ref, out_ref, over_ref):
    label, rank = label_ref[...], rank_ref[...]
    padded = best_ref.shape[2]
    me = lax.axis_index("blk")
    inner = lax.bitwise_and(rank, LANES - 1)
    result = jnp.full(label.shape, -1.0, jnp.float32)
    for m in range(SPAN):
        best = best_ref[partner(me, m, blocks, False)]
        for start in range(0, padded, LANES):
            table = jnp.broadcast_to(best[:, start : start + LANES], label.shape)
            value = jnp.take_along_axis(table, inner, axis=1)
            here = (label == m) & (rank >= start) & (rank < start + LANES)
            result = jnp.where(here, value, result)
    out_ref[...] = result
    flags = jnp.max(best_ref[:, :, padded - LANES :], axis=0)
    lane = lax.broadcasted_iota(jnp.int32, flags.shape, 1)
    over_ref[0, 0] = jnp.max(jnp.where(lane == LANES - 1, flags, 0.0))


def unpack(best, label, rank):
    vmem = pl.BlockSpec(memory_space=pltpu.VMEM)
    return pl.pallas_call(
        functools.partial(unpack_kernel, best.shape[0]),
        out_shape=[
            jax.ShapeDtypeStruct(label.shape, jnp.float32),
            jax.ShapeDtypeStruct((1, 1), jnp.float32),
        ],
        in_specs=[vmem] * 3,
        out_specs=[vmem, pl.BlockSpec(memory_space=pltpu.SMEM)],
        compiler_params=pltpu.CompilerParams(vmem_limit_bytes=4 * 1024 * 1024),
        name="unpack",
    )(best, label, rank)


def local(embeddings, cluster_id):
    blocks = lax.axis_size("blk")
    ids = cluster_id.reshape(-1, LANES)
    *far, normed, label, rank, count, over = pack_far(embeddings, ids, blocks)
    rows = {m: send(packed, m) for m, packed in zip(FAR, far)}
    near = pack_near(normed, label, rank, count)
    rows |= {m: send(packed, m) for m, packed in zip(NEAR, near)}
    rows[OWN] = near[-1]
    other = over
    for distance in range(1, lax.axis_size("parts")):
        other = jnp.maximum(other, shifted(over, "parts", distance))
    done, best = (), []
    for step in STEPS[:-1]:
        best = [score_step([rows[m] for m in done], [rows[m] for m in step], best)]
        done += step
    order = done + STEPS[-1]
    old, new = [rows[m] for m in done], [rows[m] for m in STEPS[-1]]
    best = score_last(order, old, new, best, over, other, blocks)
    returned = lax.all_to_all(best, "blk", 0, 0, tiled=True)
    packed, flag = unpack(returned, label, rank)
    return lax.cond(
        flag[0, 0] > 0, lambda: by_ring(embeddings, cluster_id), lambda: packed.reshape(-1)
    )


def solution(mesh):
    in_specs = (P(("parts", "blk"), None), P(("parts", "blk")))
    out_specs = P(("parts", "blk"))
    return jax.shard_map(local, mesh=mesh, in_specs=in_specs, out_specs=out_specs, check_vma=False)
```

```python
import functools

import jax
import jax.numpy as jnp
from jax import lax
from jax.experimental import pallas as pl
from jax.experimental.pallas import tpu as pltpu
from jax.sharding import PartitionSpec as P

SPAN = 8
HOME = 4
GROUP = 4
ROOM = 176
LANES = 128
EMPTY = 2.0
PACK_VMEM = 24 * 1024 * 1024
SCORE_VMEM = 20 * 1024 * 1024


def shifted(block, axis, distance):
    if distance == 0:
        return block
    size = lax.axis_size(axis)
    route = [(i, (i + distance) % size) for i in range(size)]
    return lax.ppermute(block, axis, route)


def block_max(left, left_id, right, right_id, same_block):
    scores = lax.dot_general(
        left, right, (((1,), (1,)), ((), ())), preferred_element_type=jnp.float32
    )
    match = (left_id[:, None] == right_id[None, :]) & (left_id[:, None] >= 0)
    if same_block:
        count = left.shape[0]
        match = match & (jnp.arange(count)[:, None] != jnp.arange(count)[None, :])
    masked = jnp.where(match, scores, jnp.float32(-1.0))
    return (jnp.max(masked, axis=1), jnp.max(masked, axis=0))


def by_ring(embeddings, cluster_id):
    scale = lax.rsqrt(jnp.sum(embeddings * embeddings, axis=1, keepdims=True) + 1e-06)
    normed = (embeddings * scale).astype(jnp.bfloat16)
    best, unused_cols = block_max(normed, cluster_id, normed, cluster_id, True)
    visitor = (normed, cluster_id)
    for offset in range(1, SPAN):
        visitor = (shifted(visitor[0], "blk", 1), shifted(visitor[1], "blk", 1))
        row_best, col_best = block_max(normed, cluster_id, visitor[0], visitor[1], False)
        returned = shifted(col_best, "blk", -offset)
        best = jnp.maximum(best, jnp.maximum(row_best, returned))
    return best


OWN = GROUP
FIRST = (0, 1, 6, 7)
SECOND = (5, 2, 3, OWN)
STEPS = ((OWN, 0, 1), (6, 7, 5), (2,), (3,))


def target(block, m, blocks):
    q = block % GROUP
    r = q ^ (m % GROUP)
    step = 0 if m >= GROUP else GROUP if r <= q else -GROUP
    return (block - q + r + step) % blocks


def partner(me, m, blocks, sender):
    q = lax.rem(me, GROUP)
    r = lax.bitwise_xor(q, m % GROUP)
    if m >= GROUP:
        return me - q + r
    back = (q <= r) if sender else (r > q)
    step = jnp.where(back, blocks - GROUP, GROUP)
    return lax.rem(me - q + r + step, blocks)


def send(rows, m):
    if m == OWN:
        return rows
    blocks = lax.axis_size("blk")
    return lax.ppermute(rows, "blk", [(i, target(i, m, blocks)) for i in range(blocks)])


def dot(a, b):
    return jnp.dot(a, b, preferred_element_type=jnp.float32)


def dot_rows(a, b):
    return lax.dot_general(a, b, (((1,), (1,)), ((), ())), preferred_element_type=jnp.float32)


def pick_rows(messages, label, rank, count, normed, out_refs):
    segments = label.shape[0]
    slot = lax.broadcasted_iota(jnp.int32, (ROOM, LANES), 0)
    lane = lax.broadcasted_iota(jnp.int32, (ROOM, LANES), 1)
    pick = []
    for m in messages:
        key = jnp.where(label == m, rank, -1)
        here = [jnp.where(slot == key[s : s + 1], 1.0, 0.0) for s in range(segments)]
        pick.append(jnp.concatenate([h.astype(jnp.bfloat16) for h in here], axis=1))
    picked = dot(jnp.concatenate(pick, axis=0), normed)
    for i, (m, out_ref) in enumerate(zip(messages, out_refs)):
        rows = picked[i * ROOM : (i + 1) * ROOM]
        empty = (slot >= count[m : m + 1]) & (lane == 0)
        first = jnp.where(empty, EMPTY, rows[:, :LANES])
        out_ref[:, :LANES] = first.astype(jnp.bfloat16)
        out_ref[:, LANES:] = rows[:, LANES:].astype(jnp.bfloat16)


def pack_first_kernel(blocks, emb_ref, id_ref, *refs):
    first_refs, refs = refs[:GROUP], refs[GROUP:]
    normed, label_ref, rank_ref, count_ref, over_ref, raw, arrived = refs
    rows, width = normed.shape
    segments = rows // LANES
    copies = []
    for s in range(segments):
        part = pl.ds(s * LANES, LANES)
        copies.append(pltpu.make_async_copy(emb_ref.at[part], raw.at[part], arrived.at[s]))
        copies[-1].start()

    me = lax.axis_index("blk")
    ids = id_ref[...]
    q = lax.rem(me, GROUP)
    offset = lax.rem(me - ids + 2 * blocks, blocks)
    turn = lax.bitwise_and(q - offset + SPAN, SPAN - 1)
    label = jnp.where(ids >= 0, lax.bitwise_xor(turn, q), SPAN)
    member = [jnp.where(label == m, 1.0, 0.0) for m in range(SPAN)]
    stacked = jnp.concatenate(member, axis=0).astype(jnp.bfloat16)
    before = lax.broadcasted_iota(jnp.int32, (LANES, LANES), 0) < lax.broadcasted_iota(
        jnp.int32, (LANES, LANES), 1
    )
    before = jnp.where(before, 1.0, 0.0).astype(jnp.bfloat16)
    ones = jnp.ones((LANES, LANES), jnp.bfloat16)
    size = SPAN * segments
    r = lax.broadcasted_iota(jnp.int32, (size, size), 0)
    c = lax.broadcasted_iota(jnp.int32, (size, size), 1)
    earlier = (lax.div(r, segments) == lax.div(c, segments)) & (c < r)
    earlier = jnp.where(earlier, 1.0, 0.0).astype(jnp.bfloat16)
    r = lax.broadcasted_iota(jnp.int32, (SPAN, size), 0)
    c = lax.broadcasted_iota(jnp.int32, (SPAN, size), 1)
    same = jnp.where(r == lax.div(c, segments), 1.0, 0.0).astype(jnp.bfloat16)
    within = dot(stacked, before)
    start = dot(dot(earlier, stacked).astype(jnp.bfloat16), ones)
    count = dot(dot(same, stacked).astype(jnp.bfloat16), ones).astype(jnp.int32)
    place = (within + start).astype(jnp.int32)
    rank = jnp.zeros_like(ids)
    for m in range(SPAN):
        rank = jnp.where(label == m, place[m * segments : (m + 1) * segments], rank)
    label_ref[...] = label
    rank_ref[...] = rank
    count_ref[...] = count
    over_ref[...] = jnp.max(jnp.where(count > ROOM, 1.0, 0.0), axis=0, keepdims=True)

    for s in range(segments):
        part = pl.ds(s * LANES, LANES)
        copies[s].wait()
        x = raw[part]
        scale = lax.rsqrt(jnp.sum(x * x, axis=1, keepdims=True) + 1e-06)
        normed[part] = (x * scale).astype(jnp.bfloat16)

    pick_rows(FIRST, label, rank, count, normed[...], first_refs)


def pack_first(embeddings, ids, blocks):
    rows, width = embeddings.shape
    segments = rows // LANES
    vmem = pl.BlockSpec(memory_space=pltpu.VMEM)
    shapes = [jax.ShapeDtypeStruct((ROOM, width), jnp.bfloat16)] * GROUP
    shapes += [jax.ShapeDtypeStruct((rows, width), jnp.bfloat16)]
    shapes += [jax.ShapeDtypeStruct((segments, LANES), jnp.int32)] * 2
    shapes += [jax.ShapeDtypeStruct((SPAN, LANES), jnp.int32)]
    shapes += [jax.ShapeDtypeStruct((1, LANES), jnp.float32)]
    return pl.pallas_call(
        functools.partial(pack_first_kernel, blocks),
        out_shape=shapes,
        in_specs=[pl.BlockSpec(memory_space=pl.ANY), vmem],
        out_specs=[vmem] * len(shapes),
        scratch_shapes=[
            pltpu.VMEM((rows, width), jnp.float32),
            pltpu.SemaphoreType.DMA((segments,)),
        ],
        compiler_params=pltpu.CompilerParams(vmem_limit_bytes=PACK_VMEM),
        cost_estimate=pl.CostEstimate(
            flops=2 * GROUP * ROOM * rows * width, bytes_accessed=rows * width * 4, transcendentals=rows
        ),
        name="pack_first",
    )(embeddings, ids)


def pack_second_kernel(normed, label_ref, rank_ref, count_ref, *out_refs):
    label, rank, count = label_ref[...], rank_ref[...], count_ref[...]
    pick_rows(SECOND, label, rank, count, normed[...], out_refs)


def pack_second(normed, label, rank, count):
    rows, width = normed.shape
    vmem = pl.BlockSpec(memory_space=pltpu.VMEM)
    return pl.pallas_call(
        pack_second_kernel,
        out_shape=[jax.ShapeDtypeStruct((ROOM, width), jnp.bfloat16)] * GROUP,
        in_specs=[vmem] * 4,
        out_specs=[vmem] * GROUP,
        compiler_params=pltpu.CompilerParams(vmem_limit_bytes=PACK_VMEM),
        cost_estimate=pl.CostEstimate(
            flops=2 * GROUP * ROOM * rows * width, bytes_accessed=rows * width * 4, transcendentals=0
        ),
        name="pack_second",
    )(normed, label, rank, count)


def penalty(rows):
    return jnp.where(rows[:, :LANES].astype(jnp.float32)[:, :1] > 1.5, -4.0, 0.0)


def best_within(rows):
    scores = dot_rows(rows, rows) + penalty(rows)
    i = lax.broadcasted_iota(jnp.int32, scores.shape, 0)
    j = lax.broadcasted_iota(jnp.int32, scores.shape, 1)
    return jnp.max(jnp.where(i == j, -1.0, scores), axis=0, keepdims=True)


def best_across(rows, columns):
    return jnp.max(dot_rows(rows, columns) + penalty(rows), axis=0, keepdims=True)


def stacked(refs):
    return jnp.concatenate([ref[...] for ref in refs], axis=0)


def join(old, new, before):
    rows = stacked(new)
    best = best_within(rows)
    if not old:
        return [best]
    others = stacked(old)
    best_old = jnp.maximum(before, best_across(rows, others))
    return [best_old, jnp.maximum(best, best_across(others, rows))]


def score_step_kernel(olds, news, *refs):
    old, new, refs = refs[:olds], refs[olds : olds + news], refs[olds + news :]
    before = refs[0][...] if olds else None
    refs[-1][...] = jnp.concatenate(join(old, new, before), axis=1)


def score_step(old, new, before):
    room, width = new[0].shape
    vmem = pl.BlockSpec(memory_space=pltpu.VMEM)
    count = len(old) + len(new)
    args = (*old, *new, *before)
    return pl.pallas_call(
        functools.partial(score_step_kernel, len(old), len(new)),
        out_shape=jax.ShapeDtypeStruct((1, count * room), jnp.float32),
        in_specs=[vmem] * len(args),
        out_specs=vmem,
        compiler_params=pltpu.CompilerParams(vmem_limit_bytes=SCORE_VMEM),
        cost_estimate=pl.CostEstimate(
            flops=4 * len(new) * room * count * room * width, bytes_accessed=count * room * width * 2, transcendentals=0
        ),
        name=f"score_{count}",
    )(*args)


def score_last_kernel(blocks, order, olds, *refs):
    old, new, refs = refs[:olds], refs[olds:SPAN], refs[SPAN:]
    before_ref, over_ref, other_ref, best_ref = refs
    room = new[0].shape[0]
    me = lax.axis_index("blk")
    flag = jnp.maximum(over_ref[...], other_ref[...])
    padded = best_ref.shape[2]
    best_ref[...] = jnp.concatenate([flag[None]] * (padded // LANES), axis=2) + jnp.zeros_like(best_ref)
    bests = []
    for best in join(old, new, before_ref[...]):
        bests += [best[:, i : i + room] for i in range(0, best.shape[1], room)]
    for m, best in zip(order, bests):
        best_ref[partner(me, m, blocks, True), :, :room] = jnp.maximum(best, -1.0)


def score_last(order, old, new, before, over, other, blocks):
    room, width = new[0].shape
    padded = (pl.cdiv(room, LANES) if room % LANES else room // LANES + 1) * LANES
    vmem = pl.BlockSpec(memory_space=pltpu.VMEM)
    return pl.pallas_call(
        functools.partial(score_last_kernel, blocks, order, len(old)),
        out_shape=jax.ShapeDtypeStruct((blocks, 1, padded), jnp.float32),
        in_specs=[vmem] * (SPAN + 3),
        out_specs=vmem,
        compiler_params=pltpu.CompilerParams(vmem_limit_bytes=SCORE_VMEM),
        name="score_last",
    )(*old, *new, *before, over, other)


def unpack_kernel(blocks, best_ref, label_ref, rank_ref, out_ref, over_ref):
    label, rank = label_ref[...], rank_ref[...]
    padded = best_ref.shape[2]
    me = lax.axis_index("blk")
    inner = lax.bitwise_and(rank, LANES - 1)
    result = jnp.full(label.shape, -1.0, jnp.float32)
    for m in range(SPAN):
        best = best_ref[partner(me, m, blocks, False)]
        for start in range(0, padded, LANES):
            table = jnp.broadcast_to(best[:, start : start + LANES], label.shape)
            value = jnp.take_along_axis(table, inner, axis=1)
            here = (label == m) & (rank >= start) & (rank < start + LANES)
            result = jnp.where(here, value, result)
    out_ref[...] = result
    flags = jnp.max(best_ref[:, :, padded - LANES :], axis=0)
    lane = lax.broadcasted_iota(jnp.int32, flags.shape, 1)
    over_ref[0, 0] = jnp.max(jnp.where(lane == LANES - 1, flags, 0.0))


def unpack(best, label, rank):
    vmem = pl.BlockSpec(memory_space=pltpu.VMEM)
    return pl.pallas_call(
        functools.partial(unpack_kernel, best.shape[0]),
        out_shape=[
            jax.ShapeDtypeStruct(label.shape, jnp.float32),
            jax.ShapeDtypeStruct((1, 1), jnp.float32),
        ],
        in_specs=[vmem] * 3,
        out_specs=[vmem, pl.BlockSpec(memory_space=pltpu.SMEM)],
        compiler_params=pltpu.CompilerParams(vmem_limit_bytes=4 * 1024 * 1024),
        name="unpack",
    )(best, label, rank)


def local(embeddings, cluster_id):
    blocks = lax.axis_size("blk")
    ids = cluster_id.reshape(-1, LANES)
    *first, normed, label, rank, count, over = pack_first(embeddings, ids, blocks)
    rows = {m: send(packed, m) for m, packed in zip(FIRST, first)}
    second = pack_second(normed, label, rank, count)
    rows |= {m: send(packed, m) for m, packed in zip(SECOND, second)}
    other = over
    for distance in range(1, lax.axis_size("parts")):
        other = jnp.maximum(other, shifted(over, "parts", distance))
    done, best = (), []
    for step in STEPS[:-1]:
        best = [score_step([rows[m] for m in done], [rows[m] for m in step], best)]
        done += step
    order = done + STEPS[-1]
    old, new = [rows[m] for m in done], [rows[m] for m in STEPS[-1]]
    best = score_last(order, old, new, best, over, other, blocks)
    returned = lax.all_to_all(best, "blk", 0, 0, tiled=True)
    packed, flag = unpack(returned, label, rank)
    return lax.cond(
        flag[0, 0] > 0, lambda: by_ring(embeddings, cluster_id), lambda: packed.reshape(-1)
    )


def solution(mesh):
    in_specs = (P(("parts", "blk"), None), P(("parts", "blk")))
    out_specs = P(("parts", "blk"))
    return jax.shard_map(local, mesh=mesh, in_specs=in_specs, out_specs=out_specs, check_vma=False)
```

```python
import functools

import jax
import jax.numpy as jnp
from jax import lax
from jax.experimental import pallas as pl
from jax.experimental.pallas import tpu as pltpu
from jax.sharding import PartitionSpec as P

SPAN = 8
HOME = 4
GROUP = 4
ROOM = 176
LANES = 128
EMPTY = 2.0
PACK_VMEM = 24 * 1024 * 1024
SCORE_VMEM = 20 * 1024 * 1024


def shifted(block, axis, distance):
    if distance == 0:
        return block
    size = lax.axis_size(axis)
    route = [(i, (i + distance) % size) for i in range(size)]
    return lax.ppermute(block, axis, route)


def block_max(left, left_id, right, right_id, same_block):
    scores = lax.dot_general(
        left, right, (((1,), (1,)), ((), ())), preferred_element_type=jnp.float32
    )
    match = (left_id[:, None] == right_id[None, :]) & (left_id[:, None] >= 0)
    if same_block:
        count = left.shape[0]
        match = match & (jnp.arange(count)[:, None] != jnp.arange(count)[None, :])
    masked = jnp.where(match, scores, jnp.float32(-1.0))
    return (jnp.max(masked, axis=1), jnp.max(masked, axis=0))


def by_ring(embeddings, cluster_id):
    scale = lax.rsqrt(jnp.sum(embeddings * embeddings, axis=1, keepdims=True) + 1e-06)
    normed = (embeddings * scale).astype(jnp.bfloat16)
    best, unused_cols = block_max(normed, cluster_id, normed, cluster_id, True)
    visitor = (normed, cluster_id)
    for offset in range(1, SPAN):
        visitor = (shifted(visitor[0], "blk", 1), shifted(visitor[1], "blk", 1))
        row_best, col_best = block_max(normed, cluster_id, visitor[0], visitor[1], False)
        returned = shifted(col_best, "blk", -offset)
        best = jnp.maximum(best, jnp.maximum(row_best, returned))
    return best


OWN = GROUP
FIRST = (6, 0, 7, 1)
SECOND = (2, 5, 3, OWN)
STEPS = ((OWN, 6, 0), (7, 1), (2, 5), (3,))


def target(block, m, blocks):
    q = block % GROUP
    r = q ^ (m % GROUP)
    step = 0 if m >= GROUP else GROUP if r <= q else -GROUP
    return (block - q + r + step) % blocks


def partner(me, m, blocks, sender):
    q = lax.rem(me, GROUP)
    r = lax.bitwise_xor(q, m % GROUP)
    if m >= GROUP:
        return me - q + r
    back = (q <= r) if sender else (r > q)
    step = jnp.where(back, blocks - GROUP, GROUP)
    return lax.rem(me - q + r + step, blocks)


def send(rows, m):
    if m == OWN:
        return rows
    blocks = lax.axis_size("blk")
    return lax.ppermute(rows, "blk", [(i, target(i, m, blocks)) for i in range(blocks)])


def dot(a, b):
    return jnp.dot(a, b, preferred_element_type=jnp.float32)


def dot_rows(a, b):
    return lax.dot_general(a, b, (((1,), (1,)), ((), ())), preferred_element_type=jnp.float32)


def pick_rows(messages, label, rank, count, normed, out_refs):
    segments = label.shape[0]
    slot = lax.broadcasted_iota(jnp.int32, (ROOM, LANES), 0)
    lane = lax.broadcasted_iota(jnp.int32, (ROOM, LANES), 1)
    pick = []
    for m in messages:
        key = jnp.where(label == m, rank, -1)
        here = [jnp.where(slot == key[s : s + 1], 1.0, 0.0) for s in range(segments)]
        pick.append(jnp.concatenate([h.astype(jnp.bfloat16) for h in here], axis=1))
    picked = dot(jnp.concatenate(pick, axis=0), normed)
    for i, (m, out_ref) in enumerate(zip(messages, out_refs)):
        rows = picked[i * ROOM : (i + 1) * ROOM]
        empty = (slot >= count[m : m + 1]) & (lane == 0)
        first = jnp.where(empty, EMPTY, rows[:, :LANES])
        out_ref[:, :LANES] = first.astype(jnp.bfloat16)
        out_ref[:, LANES:] = rows[:, LANES:].astype(jnp.bfloat16)


def pack_first_kernel(blocks, emb_ref, id_ref, *refs):
    first_refs, refs = refs[:GROUP], refs[GROUP:]
    normed, label_ref, rank_ref, count_ref, over_ref, raw, arrived = refs
    rows, width = normed.shape
    segments = rows // LANES
    copies = []
    for s in range(segments):
        part = pl.ds(s * LANES, LANES)
        copies.append(pltpu.make_async_copy(emb_ref.at[part], raw.at[part], arrived.at[s]))
        copies[-1].start()

    me = lax.axis_index("blk")
    ids = id_ref[...]
    q = lax.rem(me, GROUP)
    offset = lax.rem(me - ids + 2 * blocks, blocks)
    turn = lax.bitwise_and(q - offset + SPAN, SPAN - 1)
    label = jnp.where(ids >= 0, lax.bitwise_xor(turn, q), SPAN)
    member = [jnp.where(label == m, 1.0, 0.0) for m in range(SPAN)]
    stacked = jnp.concatenate(member, axis=0).astype(jnp.bfloat16)
    before = lax.broadcasted_iota(jnp.int32, (LANES, LANES), 0) < lax.broadcasted_iota(
        jnp.int32, (LANES, LANES), 1
    )
    before = jnp.where(before, 1.0, 0.0).astype(jnp.bfloat16)
    ones = jnp.ones((LANES, LANES), jnp.bfloat16)
    size = SPAN * segments
    r = lax.broadcasted_iota(jnp.int32, (size, size), 0)
    c = lax.broadcasted_iota(jnp.int32, (size, size), 1)
    earlier = (lax.div(r, segments) == lax.div(c, segments)) & (c < r)
    earlier = jnp.where(earlier, 1.0, 0.0).astype(jnp.bfloat16)
    r = lax.broadcasted_iota(jnp.int32, (SPAN, size), 0)
    c = lax.broadcasted_iota(jnp.int32, (SPAN, size), 1)
    same = jnp.where(r == lax.div(c, segments), 1.0, 0.0).astype(jnp.bfloat16)
    within = dot(stacked, before)
    start = dot(dot(earlier, stacked).astype(jnp.bfloat16), ones)
    count = dot(dot(same, stacked).astype(jnp.bfloat16), ones).astype(jnp.int32)
    place = (within + start).astype(jnp.int32)
    rank = jnp.zeros_like(ids)
    for m in range(SPAN):
        rank = jnp.where(label == m, place[m * segments : (m + 1) * segments], rank)
    label_ref[...] = label
    rank_ref[...] = rank
    count_ref[...] = count
    over_ref[...] = jnp.max(jnp.where(count > ROOM, 1.0, 0.0), axis=0, keepdims=True)

    for s in range(segments):
        part = pl.ds(s * LANES, LANES)
        copies[s].wait()
        x = raw[part]
        scale = lax.rsqrt(jnp.sum(x * x, axis=1, keepdims=True) + 1e-06)
        normed[part] = (x * scale).astype(jnp.bfloat16)

    pick_rows(FIRST, label, rank, count, normed[...], first_refs)


def pack_first(embeddings, ids, blocks):
    rows, width = embeddings.shape
    segments = rows // LANES
    vmem = pl.BlockSpec(memory_space=pltpu.VMEM)
    shapes = [jax.ShapeDtypeStruct((ROOM, width), jnp.bfloat16)] * GROUP
    shapes += [jax.ShapeDtypeStruct((rows, width), jnp.bfloat16)]
    shapes += [jax.ShapeDtypeStruct((segments, LANES), jnp.int32)] * 2
    shapes += [jax.ShapeDtypeStruct((SPAN, LANES), jnp.int32)]
    shapes += [jax.ShapeDtypeStruct((1, LANES), jnp.float32)]
    return pl.pallas_call(
        functools.partial(pack_first_kernel, blocks),
        out_shape=shapes,
        in_specs=[pl.BlockSpec(memory_space=pl.ANY), vmem],
        out_specs=[vmem] * len(shapes),
        scratch_shapes=[
            pltpu.VMEM((rows, width), jnp.float32),
            pltpu.SemaphoreType.DMA((segments,)),
        ],
        compiler_params=pltpu.CompilerParams(vmem_limit_bytes=PACK_VMEM),
        cost_estimate=pl.CostEstimate(
            flops=2 * GROUP * ROOM * rows * width, bytes_accessed=rows * width * 4, transcendentals=rows
        ),
        name="pack_first",
    )(embeddings, ids)


def pack_second_kernel(normed, label_ref, rank_ref, count_ref, *out_refs):
    label, rank, count = label_ref[...], rank_ref[...], count_ref[...]
    pick_rows(SECOND, label, rank, count, normed[...], out_refs)


def pack_second(normed, label, rank, count):
    rows, width = normed.shape
    vmem = pl.BlockSpec(memory_space=pltpu.VMEM)
    return pl.pallas_call(
        pack_second_kernel,
        out_shape=[jax.ShapeDtypeStruct((ROOM, width), jnp.bfloat16)] * GROUP,
        in_specs=[vmem] * 4,
        out_specs=[vmem] * GROUP,
        compiler_params=pltpu.CompilerParams(vmem_limit_bytes=PACK_VMEM),
        cost_estimate=pl.CostEstimate(
            flops=2 * GROUP * ROOM * rows * width, bytes_accessed=rows * width * 4, transcendentals=0
        ),
        name="pack_second",
    )(normed, label, rank, count)


def penalty(rows):
    return jnp.where(rows[:, :LANES].astype(jnp.float32)[:, :1] > 1.5, -4.0, 0.0)


def best_within(rows):
    scores = dot_rows(rows, rows) + penalty(rows)
    i = lax.broadcasted_iota(jnp.int32, scores.shape, 0)
    j = lax.broadcasted_iota(jnp.int32, scores.shape, 1)
    return jnp.max(jnp.where(i == j, -1.0, scores), axis=0, keepdims=True)


def best_across(rows, columns):
    return jnp.max(dot_rows(rows, columns) + penalty(rows), axis=0, keepdims=True)


def stacked(refs):
    return jnp.concatenate([ref[...] for ref in refs], axis=0)


def join(old, new, before):
    rows = stacked(new)
    best = best_within(rows)
    if not old:
        return [best]
    others = stacked(old)
    best_old = jnp.maximum(before, best_across(rows, others))
    return [best_old, jnp.maximum(best, best_across(others, rows))]


def score_step_kernel(olds, news, *refs):
    old, new, refs = refs[:olds], refs[olds : olds + news], refs[olds + news :]
    before_ref, best_ref, over_ref = refs
    before = before_ref[...]
    best_ref[...] = jnp.concatenate(join(old, new, before), axis=1)
    over_ref[...] = before[:, :LANES]


def score_step(old, new, before):
    room, width = new[0].shape
    vmem = pl.BlockSpec(memory_space=pltpu.VMEM)
    count = len(old) + len(new)
    args = (*old, *new, before)
    return pl.pallas_call(
        functools.partial(score_step_kernel, len(old), len(new)),
        out_shape=[
            jax.ShapeDtypeStruct((1, count * room), jnp.float32),
            jax.ShapeDtypeStruct((1, LANES), jnp.float32),
        ],
        in_specs=[vmem] * len(args),
        out_specs=[vmem] * 2,
        compiler_params=pltpu.CompilerParams(vmem_limit_bytes=SCORE_VMEM),
        cost_estimate=pl.CostEstimate(
            flops=4 * len(new) * room * count * room * width, bytes_accessed=count * room * width * 2, transcendentals=0
        ),
        name=f"score_{count}",
    )(*args)


def score_last_kernel(blocks, order, olds, *refs):
    old, new, refs = refs[:olds], refs[olds:SPAN], refs[SPAN:]
    before_ref, over_ref, other_ref, best_ref = refs
    room = new[0].shape[0]
    me = lax.axis_index("blk")
    flag = jnp.maximum(over_ref[...], other_ref[...])
    padded = best_ref.shape[2]
    best_ref[...] = jnp.concatenate([flag[None]] * (padded // LANES), axis=2) + jnp.zeros_like(best_ref)
    bests = []
    for best in join(old, new, before_ref[...]):
        bests += [best[:, i : i + room] for i in range(0, best.shape[1], room)]
    for m, best in zip(order, bests):
        best_ref[partner(me, m, blocks, True), :, :room] = jnp.maximum(best, -1.0)


def score_last(order, old, new, before, over, other, blocks):
    room, width = new[0].shape
    padded = (pl.cdiv(room, LANES) if room % LANES else room // LANES + 1) * LANES
    vmem = pl.BlockSpec(memory_space=pltpu.VMEM)
    return pl.pallas_call(
        functools.partial(score_last_kernel, blocks, order, len(old)),
        out_shape=jax.ShapeDtypeStruct((blocks, 1, padded), jnp.float32),
        in_specs=[vmem] * (SPAN + 3),
        out_specs=vmem,
        compiler_params=pltpu.CompilerParams(vmem_limit_bytes=SCORE_VMEM),
        name="score_last",
    )(*old, *new, before, over, other)


def unpack_kernel(blocks, best_ref, label_ref, rank_ref, out_ref, over_ref):
    label, rank = label_ref[...], rank_ref[...]
    padded = best_ref.shape[2]
    me = lax.axis_index("blk")
    inner = lax.bitwise_and(rank, LANES - 1)
    result = jnp.full(label.shape, -1.0, jnp.float32)
    for m in range(SPAN):
        best = best_ref[partner(me, m, blocks, False)]
        for start in range(0, padded, LANES):
            table = jnp.broadcast_to(best[:, start : start + LANES], label.shape)
            value = jnp.take_along_axis(table, inner, axis=1)
            here = (label == m) & (rank >= start) & (rank < start + LANES)
            result = jnp.where(here, value, result)
    out_ref[...] = result
    flags = jnp.max(best_ref[:, :, padded - LANES :], axis=0)
    lane = lax.broadcasted_iota(jnp.int32, flags.shape, 1)
    over_ref[0, 0] = jnp.max(jnp.where(lane == LANES - 1, flags, 0.0))


def unpack(best, label, rank):
    vmem = pl.BlockSpec(memory_space=pltpu.VMEM)
    return pl.pallas_call(
        functools.partial(unpack_kernel, best.shape[0]),
        out_shape=[
            jax.ShapeDtypeStruct(label.shape, jnp.float32),
            jax.ShapeDtypeStruct((1, 1), jnp.float32),
        ],
        in_specs=[vmem] * 3,
        out_specs=[vmem, pl.BlockSpec(memory_space=pltpu.SMEM)],
        compiler_params=pltpu.CompilerParams(vmem_limit_bytes=4 * 1024 * 1024),
        name="unpack",
    )(best, label, rank)


def local(embeddings, cluster_id):
    blocks = lax.axis_size("blk")
    ids = cluster_id.reshape(-1, LANES)
    *first, normed, label, rank, count, over = pack_first(embeddings, ids, blocks)
    rows = {m: send(packed, m) for m, packed in zip(FIRST, first)}
    second = pack_second(normed, label, rank, count)
    rows |= {m: send(packed, m) for m, packed in zip(SECOND, second)}
    done, best = (), over
    for step in STEPS[:-1]:
        best, passed = score_step([rows[m] for m in done], [rows[m] for m in step], best)
        if not done:
            over = passed
        done += step
    other = over
    for distance in range(1, lax.axis_size("parts")):
        other = jnp.maximum(other, shifted(over, "parts", distance))
    order = done + STEPS[-1]
    old, new = [rows[m] for m in done], [rows[m] for m in STEPS[-1]]
    best = score_last(order, old, new, best, over, other, blocks)
    returned = lax.all_to_all(best, "blk", 0, 0, tiled=True)
    packed, flag = unpack(returned, label, rank)
    return lax.cond(
        flag[0, 0] > 0, lambda: by_ring(embeddings, cluster_id), lambda: packed.reshape(-1)
    )


def solution(mesh):
    in_specs = (P(("parts", "blk"), None), P(("parts", "blk")))
    out_specs = P(("parts", "blk"))
    return jax.shard_map(local, mesh=mesh, in_specs=in_specs, out_specs=out_specs, check_vma=False)
```

```python
import functools

import jax
import jax.numpy as jnp
from jax import lax
from jax.experimental import pallas as pl
from jax.experimental.pallas import tpu as pltpu
from jax.sharding import PartitionSpec as P

SPAN = 8
HOME = 4
GROUP = 4
ROOM = 176
LANES = 128
EMPTY = 2.0
PACK_VMEM = 24 * 1024 * 1024
SCORE_VMEM = 20 * 1024 * 1024


def shifted(block, axis, distance):
    if distance == 0:
        return block
    size = lax.axis_size(axis)
    route = [(i, (i + distance) % size) for i in range(size)]
    return lax.ppermute(block, axis, route)


def block_max(left, left_id, right, right_id, same_block):
    scores = lax.dot_general(
        left, right, (((1,), (1,)), ((), ())), preferred_element_type=jnp.float32
    )
    match = (left_id[:, None] == right_id[None, :]) & (left_id[:, None] >= 0)
    if same_block:
        count = left.shape[0]
        match = match & (jnp.arange(count)[:, None] != jnp.arange(count)[None, :])
    masked = jnp.where(match, scores, jnp.float32(-1.0))
    return (jnp.max(masked, axis=1), jnp.max(masked, axis=0))


def by_ring(embeddings, cluster_id):
    scale = lax.rsqrt(jnp.sum(embeddings * embeddings, axis=1, keepdims=True) + 1e-06)
    normed = (embeddings * scale).astype(jnp.bfloat16)
    best, unused_cols = block_max(normed, cluster_id, normed, cluster_id, True)
    visitor = (normed, cluster_id)
    for offset in range(1, SPAN):
        visitor = (shifted(visitor[0], "blk", 1), shifted(visitor[1], "blk", 1))
        row_best, col_best = block_max(normed, cluster_id, visitor[0], visitor[1], False)
        returned = shifted(col_best, "blk", -offset)
        best = jnp.maximum(best, jnp.maximum(row_best, returned))
    return best


OWN = GROUP
FIRST = (6, 0, 7, 2)
SECOND = (5, 1, 3, OWN)
STEPS = ((OWN, 6, 0), (7, 5), (2,), (1, 3))


def target(block, m, blocks):
    q = block % GROUP
    r = q ^ (m % GROUP)
    step = 0 if m >= GROUP else GROUP if r <= q else -GROUP
    return (block - q + r + step) % blocks


def partner(me, m, blocks, sender):
    q = lax.rem(me, GROUP)
    r = lax.bitwise_xor(q, m % GROUP)
    if m >= GROUP:
        return me - q + r
    back = (q <= r) if sender else (r > q)
    step = jnp.where(back, blocks - GROUP, GROUP)
    return lax.rem(me - q + r + step, blocks)


def send(rows, m):
    if m == OWN:
        return rows
    blocks = lax.axis_size("blk")
    return lax.ppermute(rows, "blk", [(i, target(i, m, blocks)) for i in range(blocks)])


def dot(a, b):
    return jnp.dot(a, b, preferred_element_type=jnp.float32)


def dot_rows(a, b):
    return lax.dot_general(a, b, (((1,), (1,)), ((), ())), preferred_element_type=jnp.float32)


def pick_rows(messages, label, rank, count, normed, out_refs):
    segments = label.shape[0]
    slot = lax.broadcasted_iota(jnp.int32, (ROOM, LANES), 0)
    lane = lax.broadcasted_iota(jnp.int32, (ROOM, LANES), 1)
    pick = []
    for m in messages:
        key = jnp.where(label == m, rank, -1)
        here = [jnp.where(slot == key[s : s + 1], 1.0, 0.0) for s in range(segments)]
        pick.append(jnp.concatenate([h.astype(jnp.bfloat16) for h in here], axis=1))
    picked = dot(jnp.concatenate(pick, axis=0), normed)
    for i, (m, out_ref) in enumerate(zip(messages, out_refs)):
        rows = picked[i * ROOM : (i + 1) * ROOM]
        empty = (slot >= count[m : m + 1]) & (lane == 0)
        first = jnp.where(empty, EMPTY, rows[:, :LANES])
        out_ref[:, :LANES] = first.astype(jnp.bfloat16)
        out_ref[:, LANES:] = rows[:, LANES:].astype(jnp.bfloat16)


def pack_first_kernel(blocks, emb_ref, id_ref, *refs):
    first_refs, refs = refs[:GROUP], refs[GROUP:]
    normed, label_ref, rank_ref, count_ref, over_ref, raw, arrived = refs
    rows, width = normed.shape
    segments = rows // LANES
    copies = []
    for s in range(segments):
        part = pl.ds(s * LANES, LANES)
        copies.append(pltpu.make_async_copy(emb_ref.at[part], raw.at[part], arrived.at[s]))
        copies[-1].start()

    me = lax.axis_index("blk")
    ids = id_ref[...]
    q = lax.rem(me, GROUP)
    offset = lax.rem(me - ids + 2 * blocks, blocks)
    turn = lax.bitwise_and(q - offset + SPAN, SPAN - 1)
    label = jnp.where(ids >= 0, lax.bitwise_xor(turn, q), SPAN)
    member = [jnp.where(label == m, 1.0, 0.0) for m in range(SPAN)]
    stacked = jnp.concatenate(member, axis=0).astype(jnp.bfloat16)
    before = lax.broadcasted_iota(jnp.int32, (LANES, LANES), 0) < lax.broadcasted_iota(
        jnp.int32, (LANES, LANES), 1
    )
    before = jnp.where(before, 1.0, 0.0).astype(jnp.bfloat16)
    ones = jnp.ones((LANES, LANES), jnp.bfloat16)
    size = SPAN * segments
    r = lax.broadcasted_iota(jnp.int32, (size, size), 0)
    c = lax.broadcasted_iota(jnp.int32, (size, size), 1)
    earlier = (lax.div(r, segments) == lax.div(c, segments)) & (c < r)
    earlier = jnp.where(earlier, 1.0, 0.0).astype(jnp.bfloat16)
    r = lax.broadcasted_iota(jnp.int32, (SPAN, size), 0)
    c = lax.broadcasted_iota(jnp.int32, (SPAN, size), 1)
    same = jnp.where(r == lax.div(c, segments), 1.0, 0.0).astype(jnp.bfloat16)
    within = dot(stacked, before)
    start = dot(dot(earlier, stacked).astype(jnp.bfloat16), ones)
    count = dot(dot(same, stacked).astype(jnp.bfloat16), ones).astype(jnp.int32)
    place = (within + start).astype(jnp.int32)
    rank = jnp.zeros_like(ids)
    for m in range(SPAN):
        rank = jnp.where(label == m, place[m * segments : (m + 1) * segments], rank)
    label_ref[...] = label
    rank_ref[...] = rank
    count_ref[...] = count
    over_ref[...] = jnp.max(jnp.where(count > ROOM, 1.0, 0.0), axis=0, keepdims=True)

    for s in range(segments):
        part = pl.ds(s * LANES, LANES)
        copies[s].wait()
        x = raw[part]
        scale = lax.rsqrt(jnp.sum(x * x, axis=1, keepdims=True) + 1e-06)
        normed[part] = (x * scale).astype(jnp.bfloat16)

    pick_rows(FIRST, label, rank, count, normed[...], first_refs)


def pack_first(embeddings, ids, blocks):
    rows, width = embeddings.shape
    segments = rows // LANES
    vmem = pl.BlockSpec(memory_space=pltpu.VMEM)
    shapes = [jax.ShapeDtypeStruct((ROOM, width), jnp.bfloat16)] * GROUP
    shapes += [jax.ShapeDtypeStruct((rows, width), jnp.bfloat16)]
    shapes += [jax.ShapeDtypeStruct((segments, LANES), jnp.int32)] * 2
    shapes += [jax.ShapeDtypeStruct((SPAN, LANES), jnp.int32)]
    shapes += [jax.ShapeDtypeStruct((1, LANES), jnp.float32)]
    return pl.pallas_call(
        functools.partial(pack_first_kernel, blocks),
        out_shape=shapes,
        in_specs=[pl.BlockSpec(memory_space=pl.ANY), vmem],
        out_specs=[vmem] * len(shapes),
        scratch_shapes=[
            pltpu.VMEM((rows, width), jnp.float32),
            pltpu.SemaphoreType.DMA((segments,)),
        ],
        compiler_params=pltpu.CompilerParams(vmem_limit_bytes=PACK_VMEM),
        cost_estimate=pl.CostEstimate(
            flops=2 * GROUP * ROOM * rows * width, bytes_accessed=rows * width * 4, transcendentals=rows
        ),
        name="pack_first",
    )(embeddings, ids)


def pack_second_kernel(normed, label_ref, rank_ref, count_ref, *out_refs):
    label, rank, count = label_ref[...], rank_ref[...], count_ref[...]
    pick_rows(SECOND, label, rank, count, normed[...], out_refs)


def pack_second(normed, label, rank, count):
    rows, width = normed.shape
    vmem = pl.BlockSpec(memory_space=pltpu.VMEM)
    return pl.pallas_call(
        pack_second_kernel,
        out_shape=[jax.ShapeDtypeStruct((ROOM, width), jnp.bfloat16)] * GROUP,
        in_specs=[vmem] * 4,
        out_specs=[vmem] * GROUP,
        compiler_params=pltpu.CompilerParams(vmem_limit_bytes=PACK_VMEM),
        cost_estimate=pl.CostEstimate(
            flops=2 * GROUP * ROOM * rows * width, bytes_accessed=rows * width * 4, transcendentals=0
        ),
        name="pack_second",
    )(normed, label, rank, count)


def penalty(rows):
    return jnp.where(rows[:, :LANES].astype(jnp.float32)[:, :1] > 1.5, -4.0, 0.0)


def best_within(rows):
    scores = dot_rows(rows, rows) + penalty(rows)
    i = lax.broadcasted_iota(jnp.int32, scores.shape, 0)
    j = lax.broadcasted_iota(jnp.int32, scores.shape, 1)
    return jnp.max(jnp.where(i == j, -1.0, scores), axis=0, keepdims=True)


def best_across(rows, columns):
    return jnp.max(dot_rows(rows, columns) + penalty(rows), axis=0, keepdims=True)


def stacked(refs):
    return jnp.concatenate([ref[...] for ref in refs], axis=0)


def join(old, new, before):
    rows = stacked(new)
    best = best_within(rows)
    if not old:
        return [best]
    others = stacked(old)
    best_old = jnp.maximum(before, best_across(rows, others))
    return [best_old, jnp.maximum(best, best_across(others, rows))]


def score_step_kernel(olds, news, *refs):
    old, new, refs = refs[:olds], refs[olds : olds + news], refs[olds + news :]
    before_ref, best_ref, over_ref = refs
    before = before_ref[...]
    best_ref[...] = jnp.concatenate(join(old, new, before), axis=1)
    over_ref[...] = before[:, :LANES]


def score_step(old, new, before):
    room, width = new[0].shape
    vmem = pl.BlockSpec(memory_space=pltpu.VMEM)
    count = len(old) + len(new)
    args = (*old, *new, before)
    return pl.pallas_call(
        functools.partial(score_step_kernel, len(old), len(new)),
        out_shape=[
            jax.ShapeDtypeStruct((1, count * room), jnp.float32),
            jax.ShapeDtypeStruct((1, LANES), jnp.float32),
        ],
        in_specs=[vmem] * len(args),
        out_specs=[vmem] * 2,
        compiler_params=pltpu.CompilerParams(vmem_limit_bytes=SCORE_VMEM),
        cost_estimate=pl.CostEstimate(
            flops=4 * len(new) * room * count * room * width, bytes_accessed=count * room * width * 2, transcendentals=0
        ),
        name=f"score_{count}",
    )(*args)


def score_last_kernel(blocks, order, olds, *refs):
    old, new, refs = refs[:olds], refs[olds:SPAN], refs[SPAN:]
    before_ref, over_ref, other_ref, best_ref = refs
    room = new[0].shape[0]
    me = lax.axis_index("blk")
    flag = jnp.maximum(over_ref[...], other_ref[...])
    padded = best_ref.shape[2]
    best_ref[...] = jnp.concatenate([flag[None]] * (padded // LANES), axis=2) + jnp.zeros_like(best_ref)
    bests = []
    for best in join(old, new, before_ref[...]):
        bests += [best[:, i : i + room] for i in range(0, best.shape[1], room)]
    for m, best in zip(order, bests):
        best_ref[partner(me, m, blocks, True), :, :room] = jnp.maximum(best, -1.0)


def score_last(order, old, new, before, over, other, blocks):
    room, width = new[0].shape
    padded = (pl.cdiv(room, LANES) if room % LANES else room // LANES + 1) * LANES
    vmem = pl.BlockSpec(memory_space=pltpu.VMEM)
    return pl.pallas_call(
        functools.partial(score_last_kernel, blocks, order, len(old)),
        out_shape=jax.ShapeDtypeStruct((blocks, 1, padded), jnp.float32),
        in_specs=[vmem] * (SPAN + 3),
        out_specs=vmem,
        compiler_params=pltpu.CompilerParams(vmem_limit_bytes=SCORE_VMEM),
        name="score_last",
    )(*old, *new, before, over, other)


def unpack_kernel(blocks, best_ref, label_ref, rank_ref, out_ref, over_ref):
    label, rank = label_ref[...], rank_ref[...]
    padded = best_ref.shape[2]
    me = lax.axis_index("blk")
    inner = lax.bitwise_and(rank, LANES - 1)
    result = jnp.full(label.shape, -1.0, jnp.float32)
    for m in range(SPAN):
        best = best_ref[partner(me, m, blocks, False)]
        for start in range(0, padded, LANES):
            table = jnp.broadcast_to(best[:, start : start + LANES], label.shape)
            value = jnp.take_along_axis(table, inner, axis=1)
            here = (label == m) & (rank >= start) & (rank < start + LANES)
            result = jnp.where(here, value, result)
    out_ref[...] = result
    flags = jnp.max(best_ref[:, :, padded - LANES :], axis=0)
    lane = lax.broadcasted_iota(jnp.int32, flags.shape, 1)
    over_ref[0, 0] = jnp.max(jnp.where(lane == LANES - 1, flags, 0.0))


def unpack(best, label, rank):
    vmem = pl.BlockSpec(memory_space=pltpu.VMEM)
    return pl.pallas_call(
        functools.partial(unpack_kernel, best.shape[0]),
        out_shape=[
            jax.ShapeDtypeStruct(label.shape, jnp.float32),
            jax.ShapeDtypeStruct((1, 1), jnp.float32),
        ],
        in_specs=[vmem] * 3,
        out_specs=[vmem, pl.BlockSpec(memory_space=pltpu.SMEM)],
        compiler_params=pltpu.CompilerParams(vmem_limit_bytes=4 * 1024 * 1024),
        name="unpack",
    )(best, label, rank)


def local(embeddings, cluster_id):
    blocks = lax.axis_size("blk")
    ids = cluster_id.reshape(-1, LANES)
    *first, normed, label, rank, count, over = pack_first(embeddings, ids, blocks)
    rows = {m: send(packed, m) for m, packed in zip(FIRST, first)}
    second = pack_second(normed, label, rank, count)
    rows |= {m: send(packed, m) for m, packed in zip(SECOND, second)}
    done, best = (), over
    for step in STEPS[:-1]:
        best, passed = score_step([rows[m] for m in done], [rows[m] for m in step], best)
        if not done:
            over = passed
        done += step
    other = over
    for distance in range(1, lax.axis_size("parts")):
        other = jnp.maximum(other, shifted(over, "parts", distance))
    order = done + STEPS[-1]
    old, new = [rows[m] for m in done], [rows[m] for m in STEPS[-1]]
    best = score_last(order, old, new, best, over, other, blocks)
    returned = lax.all_to_all(best, "blk", 0, 0, tiled=True)
    packed, flag = unpack(returned, label, rank)
    return lax.cond(
        flag[0, 0] > 0, lambda: by_ring(embeddings, cluster_id), lambda: packed.reshape(-1)
    )


def solution(mesh):
    in_specs = (P(("parts", "blk"), None), P(("parts", "blk")))
    out_specs = P(("parts", "blk"))
    return jax.shard_map(local, mesh=mesh, in_specs=in_specs, out_specs=out_specs, check_vma=False)
```

```python
import functools

import jax
import jax.numpy as jnp
from jax import lax
from jax.experimental import pallas as pl
from jax.experimental.pallas import tpu as pltpu
from jax.sharding import PartitionSpec as P

SPAN = 8
HOME = 4
GROUP = 4
ROOMS = (160, 256)
LANES = 128
EMPTY = 2.0
PACK_VMEM = 24 * 1024 * 1024
SCORE_VMEM = 20 * 1024 * 1024


def shifted(block, axis, distance):
    if distance == 0:
        return block
    size = lax.axis_size(axis)
    route = [(i, (i + distance) % size) for i in range(size)]
    return lax.ppermute(block, axis, route)


def block_max(left, left_id, right, right_id, same_block):
    scores = lax.dot_general(
        left, right, (((1,), (1,)), ((), ())), preferred_element_type=jnp.float32
    )
    match = (left_id[:, None] == right_id[None, :]) & (left_id[:, None] >= 0)
    if same_block:
        count = left.shape[0]
        match = match & (jnp.arange(count)[:, None] != jnp.arange(count)[None, :])
    masked = jnp.where(match, scores, jnp.float32(-1.0))
    return (jnp.max(masked, axis=1), jnp.max(masked, axis=0))


def by_ring(embeddings, cluster_id):
    scale = lax.rsqrt(jnp.sum(embeddings * embeddings, axis=1, keepdims=True) + 1e-06)
    normed = (embeddings * scale).astype(jnp.bfloat16)
    best, unused_cols = block_max(normed, cluster_id, normed, cluster_id, True)
    visitor = (normed, cluster_id)
    for offset in range(1, SPAN):
        visitor = (shifted(visitor[0], "blk", 1), shifted(visitor[1], "blk", 1))
        row_best, col_best = block_max(normed, cluster_id, visitor[0], visitor[1], False)
        returned = shifted(col_best, "blk", -offset)
        best = jnp.maximum(best, jnp.maximum(row_best, returned))
    return best


OWN = GROUP
PACKED = ((6, 0), (7, 2), (5, 1, 3, OWN))
STEPS = ((OWN, 6, 0), (7, 5), (2,), (1, 3))


def target(block, m, blocks):
    q = block % GROUP
    r = q ^ (m % GROUP)
    step = 0 if m >= GROUP else GROUP if r <= q else -GROUP
    return (block - q + r + step) % blocks


def partner(me, m, blocks, sender):
    q = lax.rem(me, GROUP)
    r = lax.bitwise_xor(q, m % GROUP)
    if m >= GROUP:
        return me - q + r
    back = (q <= r) if sender else (r > q)
    step = jnp.where(back, blocks - GROUP, GROUP)
    return lax.rem(me - q + r + step, blocks)


def send(rows, m):
    if m == OWN:
        return rows
    blocks = lax.axis_size("blk")
    return lax.ppermute(rows, "blk", [(i, target(i, m, blocks)) for i in range(blocks)])


def dot(a, b):
    return jnp.dot(a, b, preferred_element_type=jnp.float32)


def dot_rows(a, b):
    return lax.dot_general(a, b, (((1,), (1,)), ((), ())), preferred_element_type=jnp.float32)


def pick_rows(messages, label, rank, count, normed, out_refs):
    segments, room = label.shape[0], out_refs[0].shape[0]
    slot = lax.broadcasted_iota(jnp.int32, (room, LANES), 0)
    lane = lax.broadcasted_iota(jnp.int32, (room, LANES), 1)
    pick = []
    for m in messages:
        key = jnp.where(label == m, rank, -1)
        here = [jnp.where(slot == key[s : s + 1], 1.0, 0.0) for s in range(segments)]
        pick.append(jnp.concatenate([h.astype(jnp.bfloat16) for h in here], axis=1))
    picked = dot(jnp.concatenate(pick, axis=0), normed)
    for i, (m, out_ref) in enumerate(zip(messages, out_refs)):
        rows = picked[i * room : (i + 1) * room]
        empty = (slot >= count[m : m + 1]) & (lane == 0)
        first = jnp.where(empty, EMPTY, rows[:, :LANES])
        out_ref[:, :LANES] = first.astype(jnp.bfloat16)
        out_ref[:, LANES:] = rows[:, LANES:].astype(jnp.bfloat16)


def pack_first_kernel(blocks, emb_ref, id_ref, *refs):
    first_refs, refs = refs[: len(PACKED[0])], refs[len(PACKED[0]) :]
    normed, label_ref, rank_ref, count_ref, over_ref, raw, arrived = refs
    rows, width = normed.shape
    segments = rows // LANES
    copies = []
    for s in range(segments):
        part = pl.ds(s * LANES, LANES)
        copies.append(pltpu.make_async_copy(emb_ref.at[part], raw.at[part], arrived.at[s]))
        copies[-1].start()

    me = lax.axis_index("blk")
    ids = id_ref[...]
    q = lax.rem(me, GROUP)
    offset = lax.rem(me - ids + 2 * blocks, blocks)
    turn = lax.bitwise_and(q - offset + SPAN, SPAN - 1)
    label = jnp.where(ids >= 0, lax.bitwise_xor(turn, q), SPAN)
    member = [jnp.where(label == m, 1.0, 0.0) for m in range(SPAN)]
    stacked = jnp.concatenate(member, axis=0).astype(jnp.bfloat16)
    before = lax.broadcasted_iota(jnp.int32, (LANES, LANES), 0) < lax.broadcasted_iota(
        jnp.int32, (LANES, LANES), 1
    )
    before = jnp.where(before, 1.0, 0.0).astype(jnp.bfloat16)
    ones = jnp.ones((LANES, LANES), jnp.bfloat16)
    size = SPAN * segments
    r = lax.broadcasted_iota(jnp.int32, (size, size), 0)
    c = lax.broadcasted_iota(jnp.int32, (size, size), 1)
    earlier = (lax.div(r, segments) == lax.div(c, segments)) & (c < r)
    earlier = jnp.where(earlier, 1.0, 0.0).astype(jnp.bfloat16)
    r = lax.broadcasted_iota(jnp.int32, (SPAN, size), 0)
    c = lax.broadcasted_iota(jnp.int32, (SPAN, size), 1)
    same = jnp.where(r == lax.div(c, segments), 1.0, 0.0).astype(jnp.bfloat16)
    within = dot(stacked, before)
    start = dot(dot(earlier, stacked).astype(jnp.bfloat16), ones)
    count = dot(dot(same, stacked).astype(jnp.bfloat16), ones).astype(jnp.int32)
    place = (within + start).astype(jnp.int32)
    rank = jnp.zeros_like(ids)
    for m in range(SPAN):
        rank = jnp.where(label == m, place[m * segments : (m + 1) * segments], rank)
    label_ref[...] = label
    rank_ref[...] = rank
    count_ref[...] = count
    over_ref[...] = jnp.max(jnp.where(count > first_refs[0].shape[0], 1, 0), axis=0, keepdims=True)

    for s in range(segments):
        part = pl.ds(s * LANES, LANES)
        copies[s].wait()
        x = raw[part]
        scale = lax.rsqrt(jnp.sum(x * x, axis=1, keepdims=True) + 1e-06)
        normed[part] = (x * scale).astype(jnp.bfloat16)

    pick_rows(PACKED[0], label, rank, count, normed[...], first_refs)


def pack_first(embeddings, ids, blocks, room):
    rows, width = embeddings.shape
    segments = rows // LANES
    vmem = pl.BlockSpec(memory_space=pltpu.VMEM)
    shapes = [jax.ShapeDtypeStruct((room, width), jnp.bfloat16)] * len(PACKED[0])
    shapes += [jax.ShapeDtypeStruct((rows, width), jnp.bfloat16)]
    shapes += [jax.ShapeDtypeStruct((segments, LANES), jnp.int32)] * 2
    shapes += [jax.ShapeDtypeStruct((SPAN, LANES), jnp.int32)]
    shapes += [jax.ShapeDtypeStruct((1, LANES), jnp.int32)]
    return pl.pallas_call(
        functools.partial(pack_first_kernel, blocks),
        out_shape=shapes,
        in_specs=[pl.BlockSpec(memory_space=pl.ANY), vmem],
        out_specs=[vmem] * len(shapes),
        scratch_shapes=[
            pltpu.VMEM((rows, width), jnp.float32),
            pltpu.SemaphoreType.DMA((segments,)),
        ],
        compiler_params=pltpu.CompilerParams(vmem_limit_bytes=PACK_VMEM),
        cost_estimate=pl.CostEstimate(
            flops=2 * GROUP * room * rows * width, bytes_accessed=rows * width * 4, transcendentals=rows
        ),
        name="pack_first",
    )(embeddings, ids)


def pack_more_kernel(messages, normed, label_ref, rank_ref, count_ref, *out_refs):
    label, rank, count = label_ref[...], rank_ref[...], count_ref[...]
    pick_rows(messages, label, rank, count, normed[...], out_refs)


def pack_more(messages, room, normed, label, rank, count):
    rows, width = normed.shape
    vmem = pl.BlockSpec(memory_space=pltpu.VMEM)
    return pl.pallas_call(
        functools.partial(pack_more_kernel, messages),
        out_shape=[jax.ShapeDtypeStruct((room, width), jnp.bfloat16)] * len(messages),
        in_specs=[vmem] * 4,
        out_specs=[vmem] * len(messages),
        compiler_params=pltpu.CompilerParams(vmem_limit_bytes=PACK_VMEM),
        cost_estimate=pl.CostEstimate(
            flops=2 * len(messages) * room * rows * width, bytes_accessed=rows * width * 4, transcendentals=0
        ),
        name=f"pack_{len(messages)}",
    )(normed, label, rank, count)


def same_place(count):
    i = lax.broadcasted_iota(jnp.int32, (count, count), 0)
    j = lax.broadcasted_iota(jnp.int32, (count, count), 1)
    return i == j


def stacked(refs):
    return jnp.concatenate([ref[...] for ref in refs], axis=0)


def join(old, new, before):
    count, width = new.shape
    diagonal = same_place(count)
    unused = jnp.where(new[:, :LANES].astype(jnp.float32)[:, :1] > 1.5, -4.0, 0.0)
    scores = jnp.where(diagonal, -1.0, dot_rows(new, new) + unused)
    best = jnp.max(scores, axis=0, keepdims=True)
    if old is None:
        return None, best
    i = lax.broadcasted_iota(jnp.int32, (16, width), 0)
    j = lax.broadcasted_iota(jnp.int32, (16, width), 1)
    first = jnp.where((i == 0) & (j == 0), 1.0, 0.0).astype(jnp.bfloat16)
    scores = dot_rows(jnp.concatenate([new, first], axis=0), old)
    markers, scores = scores[count : count + 1], scores[:count]
    best_old = jnp.maximum(before, jnp.max(scores + unused, axis=0, keepdims=True))
    best_new = jnp.max(scores + jnp.where(markers > 1.5, -4.0, 0.0), axis=1, keepdims=True)
    best_new = jnp.max(jnp.where(diagonal, best_new, -4.0), axis=0, keepdims=True)
    return best_old, jnp.maximum(best, best_new)


def score_first_kernel(*refs):
    new, (over_ref, best_ref, rows_ref, passed_ref) = refs[:-4], refs[-4:]
    rows_ref[...] = stacked(new)
    best_ref[...] = join(None, rows_ref[...], None)[1]
    passed_ref[...] = over_ref[...]


def score_step_kernel(old_ref, *refs):
    new, (before_ref, best_ref, rows_ref) = refs[:-3], refs[-3:]
    olds = old_ref.shape[0]
    rows_ref[:olds] = old_ref[...]
    rows_ref[olds:] = stacked(new)
    best_old, best_new = join(old_ref[...], rows_ref[olds:], before_ref[...])
    best_ref[...] = jnp.concatenate([best_old, best_new], axis=1)


def score_step(old, new, before):
    room, width = new[0].shape
    vmem = pl.BlockSpec(memory_space=pltpu.VMEM)
    rows = len(new) * room + (0 if old is None else old.shape[0])
    args = (*new, before) if old is None else (old, *new, before)
    shapes = [jax.ShapeDtypeStruct((1, rows), jnp.float32), jax.ShapeDtypeStruct((rows, width), jnp.bfloat16)]
    if old is None:
        shapes += [jax.ShapeDtypeStruct(before.shape, before.dtype)]
    return pl.pallas_call(
        score_first_kernel if old is None else score_step_kernel,
        out_shape=shapes,
        in_specs=[vmem] * len(args),
        out_specs=[vmem] * len(shapes),
        compiler_params=pltpu.CompilerParams(vmem_limit_bytes=SCORE_VMEM),
        cost_estimate=pl.CostEstimate(
            flops=4 * len(new) * room * rows * width, bytes_accessed=rows * width * 2, transcendentals=0
        ),
        name=f"score_{rows // room}",
    )(*args)


def score_last_kernel(blocks, room, old_ref, *refs):
    new, (before_ref, over_ref, other_ref, best_ref) = refs[:-4], refs[-4:]
    me = lax.axis_index("blk")
    flag = jnp.maximum(over_ref[...], other_ref[...]).astype(jnp.float32)
    padded = best_ref.shape[2]
    best_ref[...] = jnp.concatenate([flag[None]] * (padded // LANES), axis=2) + jnp.zeros_like(best_ref)
    bests = []
    for best in join(old_ref[...], stacked(new), before_ref[...]):
        bests += [best[:, i : i + room] for i in range(0, best.shape[1], room)]
    for m, best in zip(sum(STEPS, ()), bests):
        best_ref[partner(me, m, blocks, True), :, :room] = jnp.maximum(best, -1.0)


def score_last(old, new, before, over, other, blocks):
    room, width = new[0].shape
    padded = (pl.cdiv(room, LANES) if room % LANES else room // LANES + 1) * LANES
    vmem = pl.BlockSpec(memory_space=pltpu.VMEM)
    return pl.pallas_call(
        functools.partial(score_last_kernel, blocks, room),
        out_shape=jax.ShapeDtypeStruct((blocks, 1, padded), jnp.float32),
        in_specs=[vmem] * (len(new) + 4),
        out_specs=vmem,
        compiler_params=pltpu.CompilerParams(vmem_limit_bytes=SCORE_VMEM),
        name="score_last",
    )(old, *new, before, over, other)


def unpack_kernel(blocks, best_ref, label_ref, rank_ref, out_ref, over_ref):
    label, rank = label_ref[...], rank_ref[...]
    padded = best_ref.shape[2]
    me = lax.axis_index("blk")
    inner = lax.bitwise_and(rank, LANES - 1)
    result = jnp.full(label.shape, -1.0, jnp.float32)
    for m in range(SPAN):
        best = best_ref[partner(me, m, blocks, False)]
        for start in range(0, padded, LANES):
            table = jnp.broadcast_to(best[:, start : start + LANES], label.shape)
            value = jnp.take_along_axis(table, inner, axis=1)
            here = (label == m) & (rank >= start) & (rank < start + LANES)
            result = jnp.where(here, value, result)
    out_ref[...] = result
    flags = jnp.max(best_ref[:, :, padded - LANES :], axis=0)
    lane = lax.broadcasted_iota(jnp.int32, flags.shape, 1)
    over_ref[0, 0] = jnp.max(jnp.where(lane == LANES - 1, flags, 0.0)).astype(jnp.int32)


def unpack(best, label, rank):
    vmem = pl.BlockSpec(memory_space=pltpu.VMEM)
    return pl.pallas_call(
        functools.partial(unpack_kernel, best.shape[0]),
        out_shape=[
            jax.ShapeDtypeStruct(label.shape, jnp.float32),
            jax.ShapeDtypeStruct((1, 1), jnp.int32),
        ],
        in_specs=[vmem] * 3,
        out_specs=[vmem, pl.BlockSpec(memory_space=pltpu.SMEM)],
        compiler_params=pltpu.CompilerParams(vmem_limit_bytes=4 * 1024 * 1024),
        name="unpack",
    )(best, label, rank)


def by_home(embeddings, cluster_id, rooms):
    blocks = lax.axis_size("blk")
    room = rooms[0]
    ids = cluster_id.reshape(-1, LANES)
    *packed, normed, label, rank, count, over = pack_first(embeddings, ids, blocks, room)
    rows = {m: send(p, m) for m, p in zip(PACKED[0], packed)}
    for messages in PACKED[1:]:
        packed = pack_more(messages, room, normed, label, rank, count)
        rows |= {m: send(p, m) for m, p in zip(messages, packed)}
    best, old, over = score_step(None, [rows[m] for m in STEPS[0]], over)
    other = over
    for distance in range(1, lax.axis_size("parts")):
        other = jnp.maximum(other, shifted(over, "parts", distance))
    for step in STEPS[1:-1]:
        best, old = score_step(old, [rows[m] for m in step], best)
    best = score_last(old, [rows[m] for m in STEPS[-1]], best, over, other, blocks)
    returned = lax.all_to_all(best, "blk", 0, 0, tiled=True)
    result, flag = unpack(returned, label, rank)

    def again():
        if len(rooms) == 1:
            return by_ring(embeddings, cluster_id)
        return by_home(embeddings, cluster_id, rooms[1:])

    return lax.switch(flag[0, 0], [lambda: result.reshape(-1), again])


def local(embeddings, cluster_id):
    return by_home(embeddings, cluster_id, ROOMS)


def solution(mesh):
    in_specs = (P(("parts", "blk"), None), P(("parts", "blk")))
    out_specs = P(("parts", "blk"))
    return jax.shard_map(local, mesh=mesh, in_specs=in_specs, out_specs=out_specs, check_vma=False)
```

```python
import functools

import jax
import jax.numpy as jnp
from jax import lax
from jax.experimental import pallas as pl
from jax.experimental.pallas import tpu as pltpu
from jax.sharding import PartitionSpec as P

SPAN = 8
HOME = 4
GROUP = 4
ROOMS = (160, 256)
LANES = 128
EMPTY = 2.0
PACK_VMEM = 24 * 1024 * 1024
SCORE_VMEM = 20 * 1024 * 1024


def shifted(block, axis, distance):
    if distance == 0:
        return block
    size = lax.axis_size(axis)
    route = [(i, (i + distance) % size) for i in range(size)]
    return lax.ppermute(block, axis, route)


def block_max(left, left_id, right, right_id, same_block):
    scores = lax.dot_general(
        left, right, (((1,), (1,)), ((), ())), preferred_element_type=jnp.float32
    )
    match = (left_id[:, None] == right_id[None, :]) & (left_id[:, None] >= 0)
    if same_block:
        count = left.shape[0]
        match = match & (jnp.arange(count)[:, None] != jnp.arange(count)[None, :])
    masked = jnp.where(match, scores, jnp.float32(-1.0))
    return (jnp.max(masked, axis=1), jnp.max(masked, axis=0))


def by_ring(embeddings, cluster_id):
    scale = lax.rsqrt(jnp.sum(embeddings * embeddings, axis=1, keepdims=True) + 1e-06)
    normed = (embeddings * scale).astype(jnp.bfloat16)
    best, unused_cols = block_max(normed, cluster_id, normed, cluster_id, True)
    visitor = (normed, cluster_id)
    for offset in range(1, SPAN):
        visitor = (shifted(visitor[0], "blk", 1), shifted(visitor[1], "blk", 1))
        row_best, col_best = block_max(normed, cluster_id, visitor[0], visitor[1], False)
        returned = shifted(col_best, "blk", -offset)
        best = jnp.maximum(best, jnp.maximum(row_best, returned))
    return best


OWN = GROUP
PACKED = ((6, 0), (7, 2), (5, 1, 3, OWN))
STEPS = ((OWN, 6, 0), (7, 5), (2,), (1, 3))


def target(block, m, blocks):
    q = block % GROUP
    r = q ^ (m % GROUP)
    step = 0 if m >= GROUP else GROUP if r <= q else -GROUP
    return (block - q + r + step) % blocks


def send(rows, m, back=False):
    if m == OWN:
        return rows
    blocks = lax.axis_size("blk")
    route = [(i, target(i, m, blocks)) for i in range(blocks)]
    return lax.ppermute(rows, "blk", [(j, i) for i, j in route] if back else route)


def dot(a, b):
    return jnp.dot(a, b, preferred_element_type=jnp.float32)


def dot_rows(a, b):
    return lax.dot_general(a, b, (((1,), (1,)), ((), ())), preferred_element_type=jnp.float32)


def pick_rows(messages, label, rank, count, normed, out_refs):
    segments, room = label.shape[0], out_refs[0].shape[0]
    slot = lax.broadcasted_iota(jnp.int32, (room, LANES), 0)
    lane = lax.broadcasted_iota(jnp.int32, (room, LANES), 1)
    pick = []
    for m in messages:
        key = jnp.where(label == m, rank, -1)
        here = [jnp.where(slot == key[s : s + 1], 1.0, 0.0) for s in range(segments)]
        pick.append(jnp.concatenate([h.astype(jnp.bfloat16) for h in here], axis=1))
    picked = dot(jnp.concatenate(pick, axis=0), normed)
    for i, (m, out_ref) in enumerate(zip(messages, out_refs)):
        rows = picked[i * room : (i + 1) * room]
        empty = (slot >= count[m : m + 1]) & (lane == 0)
        first = jnp.where(empty, EMPTY, rows[:, :LANES])
        out_ref[:, :LANES] = first.astype(jnp.bfloat16)
        out_ref[:, LANES:] = rows[:, LANES:].astype(jnp.bfloat16)


def pack_first_kernel(blocks, emb_ref, id_ref, *refs):
    first_refs, refs = refs[: len(PACKED[0])], refs[len(PACKED[0]) :]
    normed, label_ref, rank_ref, count_ref, over_ref, raw, arrived = refs
    rows, width = normed.shape
    segments = rows // LANES
    copies = []
    for s in range(segments):
        part = pl.ds(s * LANES, LANES)
        copies.append(pltpu.make_async_copy(emb_ref.at[part], raw.at[part], arrived.at[s]))
        copies[-1].start()

    me = lax.axis_index("blk")
    ids = id_ref[...]
    q = lax.rem(me, GROUP)
    offset = lax.rem(me - ids + 2 * blocks, blocks)
    turn = lax.bitwise_and(q - offset + SPAN, SPAN - 1)
    label = jnp.where(ids >= 0, lax.bitwise_xor(turn, q), SPAN)
    member = [jnp.where(label == m, 1.0, 0.0) for m in range(SPAN)]
    stacked = jnp.concatenate(member, axis=0).astype(jnp.bfloat16)
    before = lax.broadcasted_iota(jnp.int32, (LANES, LANES), 0) < lax.broadcasted_iota(
        jnp.int32, (LANES, LANES), 1
    )
    before = jnp.where(before, 1.0, 0.0).astype(jnp.bfloat16)
    ones = jnp.ones((LANES, LANES), jnp.bfloat16)
    size = SPAN * segments
    r = lax.broadcasted_iota(jnp.int32, (size, size), 0)
    c = lax.broadcasted_iota(jnp.int32, (size, size), 1)
    earlier = (lax.div(r, segments) == lax.div(c, segments)) & (c < r)
    earlier = jnp.where(earlier, 1.0, 0.0).astype(jnp.bfloat16)
    r = lax.broadcasted_iota(jnp.int32, (SPAN, size), 0)
    c = lax.broadcasted_iota(jnp.int32, (SPAN, size), 1)
    same = jnp.where(r == lax.div(c, segments), 1.0, 0.0).astype(jnp.bfloat16)
    within = dot(stacked, before)
    start = dot(dot(earlier, stacked).astype(jnp.bfloat16), ones)
    count = dot(dot(same, stacked).astype(jnp.bfloat16), ones).astype(jnp.int32)
    place = (within + start).astype(jnp.int32)
    rank = jnp.zeros_like(ids)
    for m in range(SPAN):
        rank = jnp.where(label == m, place[m * segments : (m + 1) * segments], rank)
    label_ref[...] = label
    rank_ref[...] = rank
    count_ref[...] = count
    over_ref[...] = jnp.max(jnp.where(count > first_refs[0].shape[0], 1, 0), axis=0, keepdims=True)

    for s in range(segments):
        part = pl.ds(s * LANES, LANES)
        copies[s].wait()
        x = raw[part]
        scale = lax.rsqrt(jnp.sum(x * x, axis=1, keepdims=True) + 1e-06)
        normed[part] = (x * scale).astype(jnp.bfloat16)

    pick_rows(PACKED[0], label, rank, count, normed[...], first_refs)


def pack_first(embeddings, ids, blocks, room):
    rows, width = embeddings.shape
    segments = rows // LANES
    vmem = pl.BlockSpec(memory_space=pltpu.VMEM)
    shapes = [jax.ShapeDtypeStruct((room, width), jnp.bfloat16)] * len(PACKED[0])
    shapes += [jax.ShapeDtypeStruct((rows, width), jnp.bfloat16)]
    shapes += [jax.ShapeDtypeStruct((segments, LANES), jnp.int32)] * 2
    shapes += [jax.ShapeDtypeStruct((SPAN, LANES), jnp.int32)]
    shapes += [jax.ShapeDtypeStruct((1, LANES), jnp.int32)]
    return pl.pallas_call(
        functools.partial(pack_first_kernel, blocks),
        out_shape=shapes,
        in_specs=[pl.BlockSpec(memory_space=pl.ANY), vmem],
        out_specs=[vmem] * len(shapes),
        scratch_shapes=[
            pltpu.VMEM((rows, width), jnp.float32),
            pltpu.SemaphoreType.DMA((segments,)),
        ],
        compiler_params=pltpu.CompilerParams(vmem_limit_bytes=PACK_VMEM),
        cost_estimate=pl.CostEstimate(
            flops=2 * GROUP * room * rows * width, bytes_accessed=rows * width * 4, transcendentals=rows
        ),
        name="pack_first",
    )(embeddings, ids)


def pack_more_kernel(messages, normed, label_ref, rank_ref, count_ref, *out_refs):
    label, rank, count = label_ref[...], rank_ref[...], count_ref[...]
    pick_rows(messages, label, rank, count, normed[...], out_refs)


def pack_more(messages, room, normed, label, rank, count):
    rows, width = normed.shape
    vmem = pl.BlockSpec(memory_space=pltpu.VMEM)
    return pl.pallas_call(
        functools.partial(pack_more_kernel, messages),
        out_shape=[jax.ShapeDtypeStruct((room, width), jnp.bfloat16)] * len(messages),
        in_specs=[vmem] * 4,
        out_specs=[vmem] * len(messages),
        compiler_params=pltpu.CompilerParams(vmem_limit_bytes=PACK_VMEM),
        cost_estimate=pl.CostEstimate(
            flops=2 * len(messages) * room * rows * width, bytes_accessed=rows * width * 4, transcendentals=0
        ),
        name=f"pack_{len(messages)}",
    )(normed, label, rank, count)


def same_place(count):
    i = lax.broadcasted_iota(jnp.int32, (count, count), 0)
    j = lax.broadcasted_iota(jnp.int32, (count, count), 1)
    return i == j


def stacked(refs):
    return jnp.concatenate([ref[...] for ref in refs], axis=0)


def join(old, new, before):
    count, width = new.shape
    diagonal = same_place(count)
    unused = jnp.where(new[:, :LANES].astype(jnp.float32)[:, :1] > 1.5, -4.0, 0.0)
    scores = jnp.where(diagonal, -1.0, dot_rows(new, new) + unused)
    best = jnp.max(scores, axis=0, keepdims=True)
    if old is None:
        return None, best
    i = lax.broadcasted_iota(jnp.int32, (16, width), 0)
    j = lax.broadcasted_iota(jnp.int32, (16, width), 1)
    first = jnp.where((i == 0) & (j == 0), 1.0, 0.0).astype(jnp.bfloat16)
    scores = dot_rows(jnp.concatenate([new, first], axis=0), old)
    markers, scores = scores[count : count + 1], scores[:count]
    best_old = jnp.maximum(before, jnp.max(scores + unused, axis=0, keepdims=True))
    best_new = jnp.max(scores + jnp.where(markers > 1.5, -4.0, 0.0), axis=1, keepdims=True)
    best_new = jnp.max(jnp.where(diagonal, best_new, -4.0), axis=0, keepdims=True)
    return best_old, jnp.maximum(best, best_new)


def score_first_kernel(*refs):
    new, (over_ref, best_ref, rows_ref, flags_ref) = refs[:-4], refs[-4:]
    rows_ref[...] = stacked(new)
    best_ref[...] = join(None, rows_ref[...], None)[1]
    flags_ref[...] = jnp.broadcast_to(over_ref[...][None], flags_ref.shape)


def score_step_kernel(old_ref, *refs):
    new, (before_ref, best_ref, rows_ref) = refs[:-3], refs[-3:]
    olds = old_ref.shape[0]
    rows_ref[:olds] = old_ref[...]
    rows_ref[olds:] = stacked(new)
    best_old, best_new = join(old_ref[...], rows_ref[olds:], before_ref[...])
    best_ref[...] = jnp.concatenate([best_old, best_new], axis=1)


def score_first(new, over, devices):
    room, width = new[0].shape
    rows = len(new) * room
    vmem = pl.BlockSpec(memory_space=pltpu.VMEM)
    return pl.pallas_call(
        score_first_kernel,
        out_shape=[
            jax.ShapeDtypeStruct((1, rows), jnp.float32),
            jax.ShapeDtypeStruct((rows, width), jnp.bfloat16),
            jax.ShapeDtypeStruct((devices,) + over.shape, over.dtype),
        ],
        in_specs=[vmem] * (len(new) + 1),
        out_specs=[vmem] * 3,
        compiler_params=pltpu.CompilerParams(vmem_limit_bytes=SCORE_VMEM),
        cost_estimate=pl.CostEstimate(
            flops=2 * rows * rows * width, bytes_accessed=rows * width * 2, transcendentals=0
        ),
        name="score_first",
    )(*new, over)


def score_step(old, new, before):
    room, width = new[0].shape
    vmem = pl.BlockSpec(memory_space=pltpu.VMEM)
    rows = len(new) * room + old.shape[0]
    return pl.pallas_call(
        score_step_kernel,
        out_shape=[
            jax.ShapeDtypeStruct((1, rows), jnp.float32),
            jax.ShapeDtypeStruct((rows, width), jnp.bfloat16),
        ],
        in_specs=[vmem] * (len(new) + 2),
        out_specs=[vmem] * 2,
        compiler_params=pltpu.CompilerParams(vmem_limit_bytes=SCORE_VMEM),
        cost_estimate=pl.CostEstimate(
            flops=4 * len(new) * room * rows * width, bytes_accessed=rows * width * 2, transcendentals=0
        ),
        name=f"score_{rows // room}",
    )(old, *new, before)


def score_last_kernel(room, old_ref, *refs):
    new, (before_ref, flags_ref) = refs[: -SPAN - 3], refs[-SPAN - 3 : -SPAN - 1]
    best_refs, any_ref = refs[-SPAN - 1 : -1], refs[-1]
    bests = []
    for best in join(old_ref[...], stacked(new), before_ref[...]):
        bests += [best[:, i : i + room] for i in range(0, best.shape[1], room)]
    for m, best in zip(sum(STEPS, ()), bests):
        best_refs[m][:, :room] = jnp.maximum(best, -1.0)
    any_ref[0, 0] = jnp.max(jnp.max(flags_ref[...], axis=0))


def score_last(old, new, before, flags):
    room, width = new[0].shape
    padded = pl.cdiv(room, LANES) * LANES
    vmem = pl.BlockSpec(memory_space=pltpu.VMEM)
    *best, flag = pl.pallas_call(
        functools.partial(score_last_kernel, room),
        out_shape=[jax.ShapeDtypeStruct((1, padded), jnp.float32)] * SPAN + [jax.ShapeDtypeStruct((1, 1), jnp.int32)],
        in_specs=[vmem] * (len(new) + 3),
        out_specs=[vmem] * SPAN + [pl.BlockSpec(memory_space=pltpu.SMEM)],
        compiler_params=pltpu.CompilerParams(vmem_limit_bytes=SCORE_VMEM),
        name="score_last",
    )(old, *new, before, flags)
    return best, flag


def unpack_kernel(*refs):
    best_refs, (label_ref, rank_ref, other_ref, flag_ref, out_ref) = refs[:SPAN], refs[SPAN:]
    label, rank = label_ref[...], rank_ref[...]
    inner = lax.bitwise_and(rank, LANES - 1)
    result = jnp.full(label.shape, -1.0, jnp.float32)
    for m, best_ref in enumerate(best_refs):
        best = best_ref[...]
        for start in range(0, best.shape[1], LANES):
            table = jnp.broadcast_to(best[:, start : start + LANES], label.shape)
            value = jnp.take_along_axis(table, inner, axis=1)
            here = (label == m) & (rank >= start) & (rank < start + LANES)
            result = jnp.where(here, value, result)
    out_ref[...] = jnp.where(flag_ref[0, 0] > 0, other_ref[...], result)


def unpack(best, label, rank, other, flag):
    vmem = pl.BlockSpec(memory_space=pltpu.VMEM)
    return pl.pallas_call(
        unpack_kernel,
        out_shape=jax.ShapeDtypeStruct(label.shape, jnp.float32),
        in_specs=[vmem] * (SPAN + 3) + [pl.BlockSpec(memory_space=pltpu.SMEM)],
        out_specs=vmem,
        compiler_params=pltpu.CompilerParams(vmem_limit_bytes=1024 * 1024),
        name="unpack",
    )(*best, label, rank, other, flag)


def by_home(embeddings, cluster_id, rooms):
    blocks = lax.axis_size("blk")
    room = rooms[0]
    ids = cluster_id.reshape(-1, LANES)
    *packed, normed, label, rank, count, over = pack_first(embeddings, ids, blocks, room)
    rows = {m: send(p, m) for m, p in zip(PACKED[0], packed)}
    for messages in PACKED[1:]:
        packed = pack_more(messages, room, normed, label, rank, count)
        rows |= {m: send(p, m) for m, p in zip(messages, packed)}
    devices = lax.axis_size("parts") * blocks
    best, old, flags = score_first([rows[m] for m in STEPS[0]], over, devices)
    flags = lax.all_to_all(flags, ("parts", "blk"), 0, 0, tiled=True)
    for step in STEPS[1:-1]:
        best, old = score_step(old, [rows[m] for m in step], best)
    best, flag = score_last(old, [rows[m] for m in STEPS[-1]], best, flags)
    returned = [send(b, m, back=True) for m, b in enumerate(best)]

    def again():
        if len(rooms) == 1:
            return by_ring(embeddings, cluster_id).reshape(ids.shape)
        return by_home(embeddings, cluster_id, rooms[1:])

    other = lax.switch(flag[0, 0], [lambda: jnp.zeros(ids.shape, jnp.float32), again])
    return unpack(returned, label, rank, other, flag)


def local(embeddings, cluster_id):
    return by_home(embeddings, cluster_id, ROOMS).reshape(-1)


def solution(mesh):
    in_specs = (P(("parts", "blk"), None), P(("parts", "blk")))
    out_specs = P(("parts", "blk"))
    return jax.shard_map(local, mesh=mesh, in_specs=in_specs, out_specs=out_specs, check_vma=False)
```

```python
import functools

import jax
import jax.numpy as jnp
from jax import lax
from jax.experimental import pallas as pl
from jax.experimental.pallas import tpu as pltpu
from jax.sharding import PartitionSpec as P

SPAN = 8
HOME = 4
GROUP = 4
ROOMS = (160, 256)
LANES = 128
EMPTY = 2.0
PACK_VMEM = 24 * 1024 * 1024
SCORE_VMEM = 20 * 1024 * 1024


def shifted(block, axis, distance):
    if distance == 0:
        return block
    size = lax.axis_size(axis)
    route = [(i, (i + distance) % size) for i in range(size)]
    return lax.ppermute(block, axis, route)


def block_max(left, left_id, right, right_id, same_block):
    scores = lax.dot_general(
        left, right, (((1,), (1,)), ((), ())), preferred_element_type=jnp.float32
    )
    match = (left_id[:, None] == right_id[None, :]) & (left_id[:, None] >= 0)
    if same_block:
        count = left.shape[0]
        match = match & (jnp.arange(count)[:, None] != jnp.arange(count)[None, :])
    masked = jnp.where(match, scores, jnp.float32(-1.0))
    return (jnp.max(masked, axis=1), jnp.max(masked, axis=0))


def by_ring(embeddings, cluster_id):
    scale = lax.rsqrt(jnp.sum(embeddings * embeddings, axis=1, keepdims=True) + 1e-06)
    normed = (embeddings * scale).astype(jnp.bfloat16)
    best, unused_cols = block_max(normed, cluster_id, normed, cluster_id, True)
    visitor = (normed, cluster_id)
    for offset in range(1, SPAN):
        visitor = (shifted(visitor[0], "blk", 1), shifted(visitor[1], "blk", 1))
        row_best, col_best = block_max(normed, cluster_id, visitor[0], visitor[1], False)
        returned = shifted(col_best, "blk", -offset)
        best = jnp.maximum(best, jnp.maximum(row_best, returned))
    return best


OWN = GROUP
PACKED = ((6, 0), (7, 2), (5, 1, 3, OWN))
STEPS = ((OWN, 6, 0), (7, 2, 5), (1, 3))


def target(block, m, blocks):
    q = block % GROUP
    r = q ^ (m % GROUP)
    step = 0 if m >= GROUP else GROUP if r <= q else -GROUP
    return (block - q + r + step) % blocks


def partner(me, m, blocks, sender):
    q = lax.rem(me, GROUP)
    r = lax.bitwise_xor(q, m % GROUP)
    if m >= GROUP:
        return me - q + r
    back = (q <= r) if sender else (r > q)
    step = jnp.where(back, blocks - GROUP, GROUP)
    return lax.rem(me - q + r + step, blocks)


def send(rows, m):
    if m == OWN:
        return rows
    blocks = lax.axis_size("blk")
    return lax.ppermute(rows, "blk", [(i, target(i, m, blocks)) for i in range(blocks)])


def dot(a, b):
    return jnp.dot(a, b, preferred_element_type=jnp.float32)


def dot_rows(a, b):
    return lax.dot_general(a, b, (((1,), (1,)), ((), ())), preferred_element_type=jnp.float32)


def pick_rows(messages, label, rank, count, normed, out_refs):
    segments, room = label.shape[0], out_refs[0].shape[0]
    slot = lax.broadcasted_iota(jnp.int32, (room, LANES), 0)
    lane = lax.broadcasted_iota(jnp.int32, (room, LANES), 1)
    pick = []
    for m in messages:
        key = jnp.where(label == m, rank, -1)
        here = [jnp.where(slot == key[s : s + 1], 1.0, 0.0) for s in range(segments)]
        pick.append(jnp.concatenate([h.astype(jnp.bfloat16) for h in here], axis=1))
    picked = dot(jnp.concatenate(pick, axis=0), normed)
    for i, (m, out_ref) in enumerate(zip(messages, out_refs)):
        rows = picked[i * room : (i + 1) * room]
        empty = (slot >= count[m : m + 1]) & (lane == 0)
        first = jnp.where(empty, EMPTY, rows[:, :LANES])
        out_ref[:, :LANES] = first.astype(jnp.bfloat16)
        out_ref[:, LANES:] = rows[:, LANES:].astype(jnp.bfloat16)


def pack_first_kernel(blocks, emb_ref, id_ref, *refs):
    first_refs, refs = refs[: len(PACKED[0])], refs[len(PACKED[0]) :]
    normed, label_ref, rank_ref, count_ref, over_ref, raw, arrived = refs
    rows, width = normed.shape
    segments = rows // LANES
    copies = []
    for s in range(segments):
        part = pl.ds(s * LANES, LANES)
        copies.append(pltpu.make_async_copy(emb_ref.at[part], raw.at[part], arrived.at[s]))
        copies[-1].start()

    me = lax.axis_index("blk")
    ids = id_ref[...]
    q = lax.rem(me, GROUP)
    offset = lax.rem(me - ids + 2 * blocks, blocks)
    turn = lax.bitwise_and(q - offset + SPAN, SPAN - 1)
    label = jnp.where(ids >= 0, lax.bitwise_xor(turn, q), SPAN)
    member = [jnp.where(label == m, 1.0, 0.0) for m in range(SPAN)]
    stacked = jnp.concatenate(member, axis=0).astype(jnp.bfloat16)
    before = lax.broadcasted_iota(jnp.int32, (LANES, LANES), 0) < lax.broadcasted_iota(
        jnp.int32, (LANES, LANES), 1
    )
    before = jnp.where(before, 1.0, 0.0).astype(jnp.bfloat16)
    ones = jnp.ones((LANES, LANES), jnp.bfloat16)
    size = SPAN * segments
    r = lax.broadcasted_iota(jnp.int32, (size, size), 0)
    c = lax.broadcasted_iota(jnp.int32, (size, size), 1)
    earlier = (lax.div(r, segments) == lax.div(c, segments)) & (c < r)
    earlier = jnp.where(earlier, 1.0, 0.0).astype(jnp.bfloat16)
    r = lax.broadcasted_iota(jnp.int32, (SPAN, size), 0)
    c = lax.broadcasted_iota(jnp.int32, (SPAN, size), 1)
    same = jnp.where(r == lax.div(c, segments), 1.0, 0.0).astype(jnp.bfloat16)
    within = dot(stacked, before)
    start = dot(dot(earlier, stacked).astype(jnp.bfloat16), ones)
    count = dot(dot(same, stacked).astype(jnp.bfloat16), ones).astype(jnp.int32)
    place = (within + start).astype(jnp.int32)
    rank = jnp.zeros_like(ids)
    for m in range(SPAN):
        rank = jnp.where(label == m, place[m * segments : (m + 1) * segments], rank)
    label_ref[...] = label
    rank_ref[...] = rank
    count_ref[...] = count
    over_ref[...] = jnp.max(jnp.where(count > first_refs[0].shape[0], 1, 0), axis=0, keepdims=True)

    for s in range(segments):
        part = pl.ds(s * LANES, LANES)
        copies[s].wait()
        x = raw[part]
        scale = lax.rsqrt(jnp.sum(x * x, axis=1, keepdims=True) + 1e-06)
        normed[part] = (x * scale).astype(jnp.bfloat16)

    pick_rows(PACKED[0], label, rank, count, normed[...], first_refs)


def pack_first(embeddings, ids, blocks, room):
    rows, width = embeddings.shape
    segments = rows // LANES
    vmem = pl.BlockSpec(memory_space=pltpu.VMEM)
    shapes = [jax.ShapeDtypeStruct((room, width), jnp.bfloat16)] * len(PACKED[0])
    shapes += [jax.ShapeDtypeStruct((rows, width), jnp.bfloat16)]
    shapes += [jax.ShapeDtypeStruct((segments, LANES), jnp.int32)] * 2
    shapes += [jax.ShapeDtypeStruct((SPAN, LANES), jnp.int32)]
    shapes += [jax.ShapeDtypeStruct((1, LANES), jnp.int32)]
    return pl.pallas_call(
        functools.partial(pack_first_kernel, blocks),
        out_shape=shapes,
        in_specs=[pl.BlockSpec(memory_space=pl.ANY), vmem],
        out_specs=[vmem] * len(shapes),
        scratch_shapes=[
            pltpu.VMEM((rows, width), jnp.float32),
            pltpu.SemaphoreType.DMA((segments,)),
        ],
        compiler_params=pltpu.CompilerParams(vmem_limit_bytes=PACK_VMEM),
        cost_estimate=pl.CostEstimate(
            flops=2 * GROUP * room * rows * width, bytes_accessed=rows * width * 4, transcendentals=rows
        ),
        name="pack_first",
    )(embeddings, ids)


def pack_more_kernel(messages, normed, label_ref, rank_ref, count_ref, *out_refs):
    label, rank, count = label_ref[...], rank_ref[...], count_ref[...]
    pick_rows(messages, label, rank, count, normed[...], out_refs)


def pack_more(messages, room, normed, label, rank, count):
    rows, width = normed.shape
    vmem = pl.BlockSpec(memory_space=pltpu.VMEM)
    return pl.pallas_call(
        functools.partial(pack_more_kernel, messages),
        out_shape=[jax.ShapeDtypeStruct((room, width), jnp.bfloat16)] * len(messages),
        in_specs=[vmem] * 4,
        out_specs=[vmem] * len(messages),
        compiler_params=pltpu.CompilerParams(vmem_limit_bytes=PACK_VMEM),
        cost_estimate=pl.CostEstimate(
            flops=2 * len(messages) * room * rows * width, bytes_accessed=rows * width * 4, transcendentals=0
        ),
        name=f"pack_{len(messages)}",
    )(normed, label, rank, count)


def same_place(count):
    i = lax.broadcasted_iota(jnp.int32, (count, count), 0)
    j = lax.broadcasted_iota(jnp.int32, (count, count), 1)
    return i == j


def stacked(refs):
    return jnp.concatenate([ref[...] for ref in refs], axis=0)


def join(old, new, before):
    count, width = new.shape
    diagonal = same_place(count)
    unused = jnp.where(new[:, :LANES].astype(jnp.float32)[:, :1] > 1.5, -4.0, 0.0)
    scores = jnp.where(diagonal, -1.0, dot_rows(new, new) + unused)
    best = jnp.max(scores, axis=0, keepdims=True)
    if old is None:
        return None, best
    i = lax.broadcasted_iota(jnp.int32, (16, width), 0)
    j = lax.broadcasted_iota(jnp.int32, (16, width), 1)
    first = jnp.where((i == 0) & (j == 0), 1.0, 0.0).astype(jnp.bfloat16)
    scores = dot_rows(jnp.concatenate([new, first], axis=0), old)
    markers, scores = scores[count : count + 1], scores[:count]
    best_old = jnp.maximum(before, jnp.max(scores + unused, axis=0, keepdims=True))
    best_new = jnp.max(scores + jnp.where(markers > 1.5, -4.0, 0.0), axis=1, keepdims=True)
    best_new = jnp.max(jnp.where(diagonal, best_new, -4.0), axis=0, keepdims=True)
    return best_old, jnp.maximum(best, best_new)


def score_first_kernel(*refs):
    new, (over_ref, best_ref, rows_ref, passed_ref) = refs[:-4], refs[-4:]
    rows_ref[...] = stacked(new)
    best_ref[...] = join(None, rows_ref[...], None)[1]
    passed_ref[...] = over_ref[...]


def score_step_kernel(old_ref, *refs):
    new, (before_ref, best_ref, rows_ref) = refs[:-3], refs[-3:]
    olds = old_ref.shape[0]
    rows_ref[:olds] = old_ref[...]
    rows_ref[olds:] = stacked(new)
    best_old, best_new = join(old_ref[...], rows_ref[olds:], before_ref[...])
    best_ref[...] = jnp.concatenate([best_old, best_new], axis=1)


def score_step(old, new, before):
    room, width = new[0].shape
    vmem = pl.BlockSpec(memory_space=pltpu.VMEM)
    rows = len(new) * room + (0 if old is None else old.shape[0])
    args = (*new, before) if old is None else (old, *new, before)
    shapes = [jax.ShapeDtypeStruct((1, rows), jnp.float32), jax.ShapeDtypeStruct((rows, width), jnp.bfloat16)]
    if old is None:
        shapes += [jax.ShapeDtypeStruct(before.shape, before.dtype)]
    return pl.pallas_call(
        score_first_kernel if old is None else score_step_kernel,
        out_shape=shapes,
        in_specs=[vmem] * len(args),
        out_specs=[vmem] * len(shapes),
        compiler_params=pltpu.CompilerParams(vmem_limit_bytes=SCORE_VMEM),
        cost_estimate=pl.CostEstimate(
            flops=4 * len(new) * room * rows * width, bytes_accessed=rows * width * 2, transcendentals=0
        ),
        name=f"score_{rows // room}",
    )(*args)


def score_last_kernel(blocks, room, old_ref, *refs):
    new, (before_ref, over_ref, other_ref, best_ref) = refs[:-4], refs[-4:]
    me = lax.axis_index("blk")
    flag = jnp.maximum(over_ref[...], other_ref[...]).astype(jnp.float32)
    padded = best_ref.shape[2]
    best_ref[...] = jnp.concatenate([flag[None]] * (padded // LANES), axis=2) + jnp.zeros_like(best_ref)
    bests = []
    for best in join(old_ref[...], stacked(new), before_ref[...]):
        bests += [best[:, i : i + room] for i in range(0, best.shape[1], room)]
    for m, best in zip(sum(STEPS, ()), bests):
        best_ref[partner(me, m, blocks, True), :, :room] = jnp.maximum(best, -1.0)


def score_last(old, new, before, over, other, blocks):
    room, width = new[0].shape
    padded = (pl.cdiv(room, LANES) if room % LANES else room // LANES + 1) * LANES
    vmem = pl.BlockSpec(memory_space=pltpu.VMEM)
    return pl.pallas_call(
        functools.partial(score_last_kernel, blocks, room),
        out_shape=jax.ShapeDtypeStruct((blocks, 1, padded), jnp.float32),
        in_specs=[vmem] * (len(new) + 4),
        out_specs=vmem,
        compiler_params=pltpu.CompilerParams(vmem_limit_bytes=SCORE_VMEM),
        name="score_last",
    )(old, *new, before, over, other)


def unpack_kernel(blocks, best_ref, label_ref, rank_ref, out_ref, over_ref):
    label, rank = label_ref[...], rank_ref[...]
    padded = best_ref.shape[2]
    me = lax.axis_index("blk")
    inner = lax.bitwise_and(rank, LANES - 1)
    result = jnp.full(label.shape, -1.0, jnp.float32)
    for m in range(SPAN):
        best = best_ref[partner(me, m, blocks, False)]
        for start in range(0, padded, LANES):
            table = jnp.broadcast_to(best[:, start : start + LANES], label.shape)
            value = jnp.take_along_axis(table, inner, axis=1)
            here = (label == m) & (rank >= start) & (rank < start + LANES)
            result = jnp.where(here, value, result)
    out_ref[...] = result
    flags = jnp.max(best_ref[:, :, padded - LANES :], axis=0)
    over_ref[...] = jnp.roll(flags, 1, axis=1).astype(jnp.int32)


def unpack(best, label, rank):
    vmem = pl.BlockSpec(memory_space=pltpu.VMEM)
    return pl.pallas_call(
        functools.partial(unpack_kernel, best.shape[0]),
        out_shape=[
            jax.ShapeDtypeStruct(label.shape, jnp.float32),
            jax.ShapeDtypeStruct((1, LANES), jnp.int32),
        ],
        in_specs=[vmem] * 3,
        out_specs=[vmem] * 2,
        compiler_params=pltpu.CompilerParams(vmem_limit_bytes=4 * 1024 * 1024),
        name="unpack",
    )(best, label, rank)


def by_home(embeddings, cluster_id, rooms):
    blocks = lax.axis_size("blk")
    room = rooms[0]
    ids = cluster_id.reshape(-1, LANES)
    *packed, normed, label, rank, count, over = pack_first(embeddings, ids, blocks, room)
    rows = {m: send(p, m) for m, p in zip(PACKED[0], packed)}
    for messages in PACKED[1:]:
        packed = pack_more(messages, room, normed, label, rank, count)
        rows |= {m: send(p, m) for m, p in zip(messages, packed)}
    best, old, over = score_step(None, [rows[m] for m in STEPS[0]], over)
    other = over
    for distance in range(1, lax.axis_size("parts")):
        other = jnp.maximum(other, shifted(over, "parts", distance))
    for step in STEPS[1:-1]:
        best, old = score_step(old, [rows[m] for m in step], best)
    best = score_last(old, [rows[m] for m in STEPS[-1]], best, over, other, blocks)
    returned = lax.all_to_all(best, "blk", 0, 0, tiled=True)
    result, flag = unpack(returned, label, rank)

    def again():
        if len(rooms) == 1:
            return by_ring(embeddings, cluster_id)
        return by_home(embeddings, cluster_id, rooms[1:])

    return lax.switch(flag[0, 0], [lambda: result.reshape(-1), again])


def local(embeddings, cluster_id):
    return by_home(embeddings, cluster_id, ROOMS)


def solution(mesh):
    in_specs = (P(("parts", "blk"), None), P(("parts", "blk")))
    out_specs = P(("parts", "blk"))
    return jax.shard_map(local, mesh=mesh, in_specs=in_specs, out_specs=out_specs, check_vma=False)
```

```python
import functools

import jax
import jax.numpy as jnp
from jax import lax
from jax.experimental import pallas as pl
from jax.experimental.pallas import tpu as pltpu
from jax.sharding import PartitionSpec as P

SPAN = 8
HOME = 4
GROUP = 4
ROOMS = (160, 256)
LANES = 128
EMPTY = 2.0
PACK_VMEM = 24 * 1024 * 1024
SCORE_VMEM = 20 * 1024 * 1024


def shifted(block, axis, distance):
    if distance == 0:
        return block
    size = lax.axis_size(axis)
    route = [(i, (i + distance) % size) for i in range(size)]
    return lax.ppermute(block, axis, route)


def block_max(left, left_id, right, right_id, same_block):
    scores = lax.dot_general(
        left, right, (((1,), (1,)), ((), ())), preferred_element_type=jnp.float32
    )
    match = (left_id[:, None] == right_id[None, :]) & (left_id[:, None] >= 0)
    if same_block:
        count = left.shape[0]
        match = match & (jnp.arange(count)[:, None] != jnp.arange(count)[None, :])
    masked = jnp.where(match, scores, jnp.float32(-1.0))
    return (jnp.max(masked, axis=1), jnp.max(masked, axis=0))


def by_ring(embeddings, cluster_id):
    scale = lax.rsqrt(jnp.sum(embeddings * embeddings, axis=1, keepdims=True) + 1e-06)
    normed = (embeddings * scale).astype(jnp.bfloat16)
    best, unused_cols = block_max(normed, cluster_id, normed, cluster_id, True)
    visitor = (normed, cluster_id)
    for offset in range(1, SPAN):
        visitor = (shifted(visitor[0], "blk", 1), shifted(visitor[1], "blk", 1))
        row_best, col_best = block_max(normed, cluster_id, visitor[0], visitor[1], False)
        returned = shifted(col_best, "blk", -offset)
        best = jnp.maximum(best, jnp.maximum(row_best, returned))
    return best


OWN = GROUP
PACKED = ((6, 0), (7, 2), (5, 1, 3, OWN))
STEPS = ((OWN, 6, 0), (7, 2, 5), (1, 3))


def target(block, m, blocks):
    q = block % GROUP
    r = q ^ (m % GROUP)
    step = 0 if m >= GROUP else GROUP if r <= q else -GROUP
    return (block - q + r + step) % blocks


def partner(me, m, blocks, sender):
    q = lax.rem(me, GROUP)
    r = lax.bitwise_xor(q, m % GROUP)
    if m >= GROUP:
        return me - q + r
    back = (q <= r) if sender else (r > q)
    step = jnp.where(back, blocks - GROUP, GROUP)
    return lax.rem(me - q + r + step, blocks)


def send(rows, m):
    if m == OWN:
        return rows
    blocks = lax.axis_size("blk")
    return lax.ppermute(rows, "blk", [(i, target(i, m, blocks)) for i in range(blocks)])


def dot(a, b):
    return jnp.dot(a, b, preferred_element_type=jnp.float32)


def dot_rows(a, b):
    return lax.dot_general(a, b, (((1,), (1,)), ((), ())), preferred_element_type=jnp.float32)


def pick_rows(messages, label, rank, count, normed, out_refs):
    segments, room = label.shape[0], out_refs[0].shape[0]
    slot = lax.broadcasted_iota(jnp.int32, (room, LANES), 0)
    lane = lax.broadcasted_iota(jnp.int32, (room, LANES), 1)
    pick = []
    for m in messages:
        key = jnp.where(label == m, rank, -1)
        here = [jnp.where(slot == key[s : s + 1], 1.0, 0.0) for s in range(segments)]
        pick.append(jnp.concatenate([h.astype(jnp.bfloat16) for h in here], axis=1))
    picked = dot(jnp.concatenate(pick, axis=0), normed)
    for i, (m, out_ref) in enumerate(zip(messages, out_refs)):
        rows = picked[i * room : (i + 1) * room]
        empty = (slot >= count[m : m + 1]) & (lane == 0)
        first = jnp.where(empty, EMPTY, rows[:, :LANES])
        out_ref[:, :LANES] = first.astype(jnp.bfloat16)
        out_ref[:, LANES:] = rows[:, LANES:].astype(jnp.bfloat16)


def pack_first_kernel(blocks, emb_ref, id_ref, *refs):
    first_refs, refs = refs[: len(PACKED[0])], refs[len(PACKED[0]) :]
    normed, label_ref, rank_ref, count_ref, over_ref, raw, arrived = refs
    rows, width = normed.shape
    segments = rows // LANES
    copies = []
    for s in range(segments):
        part = pl.ds(s * LANES, LANES)
        copies.append(pltpu.make_async_copy(emb_ref.at[part], raw.at[part], arrived.at[s]))
        copies[-1].start()

    me = lax.axis_index("blk")
    ids = id_ref[...]
    q = lax.rem(me, GROUP)
    offset = lax.rem(me - ids + 2 * blocks, blocks)
    turn = lax.bitwise_and(q - offset + SPAN, SPAN - 1)
    label = jnp.where(ids >= 0, lax.bitwise_xor(turn, q), SPAN)
    member = [jnp.where(label == m, 1.0, 0.0) for m in range(SPAN)]
    stacked = jnp.concatenate(member, axis=0).astype(jnp.bfloat16)
    before = lax.broadcasted_iota(jnp.int32, (LANES, LANES), 0) < lax.broadcasted_iota(
        jnp.int32, (LANES, LANES), 1
    )
    before = jnp.where(before, 1.0, 0.0).astype(jnp.bfloat16)
    ones = jnp.ones((LANES, LANES), jnp.bfloat16)
    size = SPAN * segments
    r = lax.broadcasted_iota(jnp.int32, (size, size), 0)
    c = lax.broadcasted_iota(jnp.int32, (size, size), 1)
    earlier = (lax.div(r, segments) == lax.div(c, segments)) & (c < r)
    earlier = jnp.where(earlier, 1.0, 0.0).astype(jnp.bfloat16)
    r = lax.broadcasted_iota(jnp.int32, (SPAN, size), 0)
    c = lax.broadcasted_iota(jnp.int32, (SPAN, size), 1)
    same = jnp.where(r == lax.div(c, segments), 1.0, 0.0).astype(jnp.bfloat16)
    within = dot(stacked, before)
    start = dot(dot(earlier, stacked).astype(jnp.bfloat16), ones)
    count = dot(dot(same, stacked).astype(jnp.bfloat16), ones).astype(jnp.int32)
    place = (within + start).astype(jnp.int32)
    rank = jnp.zeros_like(ids)
    for m in range(SPAN):
        rank = jnp.where(label == m, place[m * segments : (m + 1) * segments], rank)
    label_ref[...] = label
    rank_ref[...] = rank
    count_ref[...] = count
    over_ref[...] = jnp.max(jnp.where(count > first_refs[0].shape[0], 1, 0), axis=0, keepdims=True)

    for s in range(segments):
        part = pl.ds(s * LANES, LANES)
        copies[s].wait()
        x = raw[part]
        scale = lax.rsqrt(jnp.sum(x * x, axis=1, keepdims=True) + 1e-06)
        normed[part] = (x * scale).astype(jnp.bfloat16)

    pick_rows(PACKED[0], label, rank, count, normed[...], first_refs)


def pack_first(embeddings, ids, blocks, room):
    rows, width = embeddings.shape
    segments = rows // LANES
    vmem = pl.BlockSpec(memory_space=pltpu.VMEM)
    shapes = [jax.ShapeDtypeStruct((room, width), jnp.bfloat16)] * len(PACKED[0])
    shapes += [jax.ShapeDtypeStruct((rows, width), jnp.bfloat16)]
    shapes += [jax.ShapeDtypeStruct((segments, LANES), jnp.int32)] * 2
    shapes += [jax.ShapeDtypeStruct((SPAN, LANES), jnp.int32)]
    shapes += [jax.ShapeDtypeStruct((1, LANES), jnp.int32)]
    return pl.pallas_call(
        functools.partial(pack_first_kernel, blocks),
        out_shape=shapes,
        in_specs=[pl.BlockSpec(memory_space=pl.ANY), vmem],
        out_specs=[vmem] * len(shapes),
        scratch_shapes=[
            pltpu.VMEM((rows, width), jnp.float32),
            pltpu.SemaphoreType.DMA((segments,)),
        ],
        compiler_params=pltpu.CompilerParams(vmem_limit_bytes=PACK_VMEM),
        cost_estimate=pl.CostEstimate(
            flops=2 * GROUP * room * rows * width, bytes_accessed=rows * width * 4, transcendentals=rows
        ),
        name="pack_first",
    )(embeddings, ids)


def pack_more_kernel(messages, normed, label_ref, rank_ref, count_ref, *out_refs):
    label, rank, count = label_ref[...], rank_ref[...], count_ref[...]
    pick_rows(messages, label, rank, count, normed[...], out_refs)


def pack_more(messages, room, normed, label, rank, count):
    rows, width = normed.shape
    vmem = pl.BlockSpec(memory_space=pltpu.VMEM)
    return pl.pallas_call(
        functools.partial(pack_more_kernel, messages),
        out_shape=[jax.ShapeDtypeStruct((room, width), jnp.bfloat16)] * len(messages),
        in_specs=[vmem] * 4,
        out_specs=[vmem] * len(messages),
        compiler_params=pltpu.CompilerParams(vmem_limit_bytes=PACK_VMEM),
        cost_estimate=pl.CostEstimate(
            flops=2 * len(messages) * room * rows * width, bytes_accessed=rows * width * 4, transcendentals=0
        ),
        name=f"pack_{len(messages)}",
    )(normed, label, rank, count)


def same_place(count):
    i = lax.broadcasted_iota(jnp.int32, (count, count), 0)
    j = lax.broadcasted_iota(jnp.int32, (count, count), 1)
    return i == j


def stacked(refs):
    return jnp.concatenate([ref[...] for ref in refs], axis=0)


def join(old, new, before):
    count, width = new.shape
    diagonal = same_place(count)
    unused = jnp.where(new[:, :LANES].astype(jnp.float32)[:, :1] > 1.5, -4.0, 0.0)
    scores = jnp.where(diagonal, -1.0, dot_rows(new, new) + unused)
    best = jnp.max(scores, axis=0, keepdims=True)
    if old is None:
        return None, best
    i = lax.broadcasted_iota(jnp.int32, (16, width), 0)
    j = lax.broadcasted_iota(jnp.int32, (16, width), 1)
    first = jnp.where((i == 0) & (j == 0), 1.0, 0.0).astype(jnp.bfloat16)
    scores = dot_rows(jnp.concatenate([new, first], axis=0), old)
    markers, scores = scores[count : count + 1], scores[:count]
    best_old = jnp.maximum(before, jnp.max(scores + unused, axis=0, keepdims=True))
    best_new = jnp.max(scores + jnp.where(markers > 1.5, -4.0, 0.0), axis=1, keepdims=True)
    best_new = jnp.max(jnp.where(diagonal, best_new, -4.0), axis=0, keepdims=True)
    return best_old, jnp.maximum(best, best_new)


def score_first_kernel(*refs):
    new, (over_ref, best_ref, rows_ref, passed_ref) = refs[:-4], refs[-4:]
    rows_ref[...] = stacked(new)
    best_ref[...] = join(None, rows_ref[...], None)[1]
    passed_ref[...] = over_ref[...]


def score_step_kernel(old_ref, *refs):
    new, (before_ref, best_ref, rows_ref) = refs[:-3], refs[-3:]
    olds = old_ref.shape[0]
    rows_ref[:olds] = old_ref[...]
    rows_ref[olds:] = stacked(new)
    best_old, best_new = join(old_ref[...], rows_ref[olds:], before_ref[...])
    best_ref[...] = jnp.concatenate([best_old, best_new], axis=1)


def score_step(old, new, before):
    room, width = new[0].shape
    vmem = pl.BlockSpec(memory_space=pltpu.VMEM)
    rows = len(new) * room + (0 if old is None else old.shape[0])
    args = (*new, before) if old is None else (old, *new, before)
    shapes = [jax.ShapeDtypeStruct((1, rows), jnp.float32), jax.ShapeDtypeStruct((rows, width), jnp.bfloat16)]
    if old is None:
        shapes += [jax.ShapeDtypeStruct(before.shape, before.dtype)]
    return pl.pallas_call(
        score_first_kernel if old is None else score_step_kernel,
        out_shape=shapes,
        in_specs=[vmem] * len(args),
        out_specs=[vmem] * len(shapes),
        compiler_params=pltpu.CompilerParams(vmem_limit_bytes=SCORE_VMEM),
        cost_estimate=pl.CostEstimate(
            flops=4 * len(new) * room * rows * width, bytes_accessed=rows * width * 2, transcendentals=0
        ),
        name=f"score_{rows // room}",
    )(*args)


def score_last_kernel(blocks, room, old_ref, *refs):
    new, (before_ref, over_ref, other_ref, best_ref) = refs[:-4], refs[-4:]
    me = lax.axis_index("blk")
    flag = jnp.maximum(over_ref[...], other_ref[...]).astype(jnp.float32)
    padded = best_ref.shape[2]
    best_ref[...] = jnp.concatenate([flag[None]] * (padded // LANES), axis=2) + jnp.zeros_like(best_ref)
    bests = []
    for best in join(old_ref[...], stacked(new), before_ref[...]):
        bests += [best[:, i : i + room] for i in range(0, best.shape[1], room)]
    for m, best in zip(sum(STEPS, ()), bests):
        best_ref[blocks - 1 - partner(me, m, blocks, True), :, :room] = jnp.maximum(best, -1.0)


def score_last(old, new, before, over, other, blocks):
    room, width = new[0].shape
    padded = (pl.cdiv(room, LANES) if room % LANES else room // LANES + 1) * LANES
    vmem = pl.BlockSpec(memory_space=pltpu.VMEM)
    return pl.pallas_call(
        functools.partial(score_last_kernel, blocks, room),
        out_shape=jax.ShapeDtypeStruct((blocks, 1, padded), jnp.float32),
        in_specs=[vmem] * (len(new) + 4),
        out_specs=vmem,
        compiler_params=pltpu.CompilerParams(vmem_limit_bytes=SCORE_VMEM),
        name="score_last",
    )(old, *new, before, over, other)


def unpack_kernel(blocks, best_ref, label_ref, rank_ref, out_ref, over_ref):
    label, rank = label_ref[...], rank_ref[...]
    padded = best_ref.shape[2]
    me = lax.axis_index("blk")
    inner = lax.bitwise_and(rank, LANES - 1)
    result = jnp.full(label.shape, -1.0, jnp.float32)
    for m in range(SPAN):
        best = best_ref[blocks - 1 - partner(me, m, blocks, False)]
        for start in range(0, padded, LANES):
            table = jnp.broadcast_to(best[:, start : start + LANES], label.shape)
            value = jnp.take_along_axis(table, inner, axis=1)
            here = (label == m) & (rank >= start) & (rank < start + LANES)
            result = jnp.where(here, value, result)
    out_ref[...] = result
    flags = jnp.max(best_ref[:, :, padded - LANES :], axis=0)
    over_ref[...] = jnp.roll(flags, 1, axis=1).astype(jnp.int32)


def unpack(best, label, rank):
    vmem = pl.BlockSpec(memory_space=pltpu.VMEM)
    return pl.pallas_call(
        functools.partial(unpack_kernel, best.shape[0]),
        out_shape=[
            jax.ShapeDtypeStruct(label.shape, jnp.float32),
            jax.ShapeDtypeStruct((1, LANES), jnp.int32),
        ],
        in_specs=[vmem] * 3,
        out_specs=[vmem] * 2,
        compiler_params=pltpu.CompilerParams(vmem_limit_bytes=4 * 1024 * 1024),
        name="unpack",
    )(best, label, rank)


def by_home(embeddings, cluster_id, rooms):
    blocks = lax.axis_size("blk")
    room = rooms[0]
    ids = cluster_id.reshape(-1, LANES)
    *packed, normed, label, rank, count, over = pack_first(embeddings, ids, blocks, room)
    rows = {m: send(p, m) for m, p in zip(PACKED[0], packed)}
    for messages in PACKED[1:]:
        packed = pack_more(messages, room, normed, label, rank, count)
        rows |= {m: send(p, m) for m, p in zip(messages, packed)}
    best, old, over = score_step(None, [rows[m] for m in STEPS[0]], over)
    other = over
    for distance in range(1, lax.axis_size("parts")):
        other = jnp.maximum(other, shifted(over, "parts", distance))
    for step in STEPS[1:-1]:
        best, old = score_step(old, [rows[m] for m in step], best)
    best = score_last(old, [rows[m] for m in STEPS[-1]], best, over, other, blocks)
    backward = [list(reversed(range(blocks)))]
    returned = lax.all_to_all(best, "blk", 0, 0, axis_index_groups=backward, tiled=True)
    result, flag = unpack(returned, label, rank)

    def again():
        if len(rooms) == 1:
            return by_ring(embeddings, cluster_id)
        return by_home(embeddings, cluster_id, rooms[1:])

    return lax.switch(flag[0, 0], [lambda: result.reshape(-1), again])


def local(embeddings, cluster_id):
    return by_home(embeddings, cluster_id, ROOMS)


def solution(mesh):
    in_specs = (P(("parts", "blk"), None), P(("parts", "blk")))
    out_specs = P(("parts", "blk"))
    return jax.shard_map(local, mesh=mesh, in_specs=in_specs, out_specs=out_specs, check_vma=False)
```

```python
import functools

import jax
import jax.numpy as jnp
from jax import lax
from jax.experimental import pallas as pl
from jax.experimental.pallas import tpu as pltpu
from jax.sharding import PartitionSpec as P

SPAN = 8
HOME = 4
GROUP = 4
ROOMS = (160, 256)
LANES = 128
EMPTY = 2.0
PACK_VMEM = 24 * 1024 * 1024
SCORE_VMEM = 20 * 1024 * 1024


def shifted(block, axis, distance):
    if distance == 0:
        return block
    size = lax.axis_size(axis)
    route = [(i, (i + distance) % size) for i in range(size)]
    return lax.ppermute(block, axis, route)


def block_max(left, left_id, right, right_id, same_block):
    scores = lax.dot_general(
        left, right, (((1,), (1,)), ((), ())), preferred_element_type=jnp.float32
    )
    match = (left_id[:, None] == right_id[None, :]) & (left_id[:, None] >= 0)
    if same_block:
        count = left.shape[0]
        match = match & (jnp.arange(count)[:, None] != jnp.arange(count)[None, :])
    masked = jnp.where(match, scores, jnp.float32(-1.0))
    return (jnp.max(masked, axis=1), jnp.max(masked, axis=0))


def by_ring(embeddings, cluster_id):
    scale = lax.rsqrt(jnp.sum(embeddings * embeddings, axis=1, keepdims=True) + 1e-06)
    normed = (embeddings * scale).astype(jnp.bfloat16)
    best, unused_cols = block_max(normed, cluster_id, normed, cluster_id, True)
    visitor = (normed, cluster_id)
    for offset in range(1, SPAN):
        visitor = (shifted(visitor[0], "blk", 1), shifted(visitor[1], "blk", 1))
        row_best, col_best = block_max(normed, cluster_id, visitor[0], visitor[1], False)
        returned = shifted(col_best, "blk", -offset)
        best = jnp.maximum(best, jnp.maximum(row_best, returned))
    return best


OWN = GROUP
PACKED = ((6, 0), (7, 2, OWN), (1, 3, 5))
STEPS = ((OWN, 6, 0), (7, 2), (1, 3, 5))


def target(block, m, blocks):
    q = block % GROUP
    r = q ^ (m % GROUP)
    step = 0 if m >= GROUP else GROUP if r <= q else -GROUP
    return (block - q + r + step) % blocks


def partner(me, m, blocks, sender):
    q = lax.rem(me, GROUP)
    r = lax.bitwise_xor(q, m % GROUP)
    if m >= GROUP:
        return me - q + r
    back = (q <= r) if sender else (r > q)
    step = jnp.where(back, blocks - GROUP, GROUP)
    return lax.rem(me - q + r + step, blocks)


def send(rows, m):
    if m == OWN:
        return rows
    blocks = lax.axis_size("blk")
    return lax.ppermute(rows, "blk", [(i, target(i, m, blocks)) for i in range(blocks)])


def dot(a, b):
    return jnp.dot(a, b, preferred_element_type=jnp.float32)


def dot_rows(a, b):
    return lax.dot_general(a, b, (((1,), (1,)), ((), ())), preferred_element_type=jnp.float32)


def pick_rows(messages, label, rank, count, normed, out_refs):
    segments, room = label.shape[0], out_refs[0].shape[0]
    slot = lax.broadcasted_iota(jnp.int32, (room, LANES), 0)
    lane = lax.broadcasted_iota(jnp.int32, (room, LANES), 1)
    pick = []
    for m in messages:
        key = jnp.where(label == m, rank, -1)
        here = [jnp.where(slot == key[s : s + 1], 1.0, 0.0) for s in range(segments)]
        pick.append(jnp.concatenate([h.astype(jnp.bfloat16) for h in here], axis=1))
    picked = dot(jnp.concatenate(pick, axis=0), normed)
    for i, (m, out_ref) in enumerate(zip(messages, out_refs)):
        rows = picked[i * room : (i + 1) * room]
        empty = (slot >= count[m : m + 1]) & (lane == 0)
        first = jnp.where(empty, EMPTY, rows[:, :LANES])
        out_ref[:, :LANES] = first.astype(jnp.bfloat16)
        out_ref[:, LANES:] = rows[:, LANES:].astype(jnp.bfloat16)


def pack_first_kernel(blocks, emb_ref, id_ref, *refs):
    first_refs, refs = refs[: len(PACKED[0])], refs[len(PACKED[0]) :]
    normed, label_ref, rank_ref, count_ref, over_ref, raw, arrived = refs
    rows, width = normed.shape
    segments = rows // LANES
    copies = []
    for s in range(segments):
        part = pl.ds(s * LANES, LANES)
        copies.append(pltpu.make_async_copy(emb_ref.at[part], raw.at[part], arrived.at[s]))
        copies[-1].start()

    me = lax.axis_index("blk")
    ids = id_ref[...]
    q = lax.rem(me, GROUP)
    offset = lax.rem(me - ids + 2 * blocks, blocks)
    turn = lax.bitwise_and(q - offset + SPAN, SPAN - 1)
    label = jnp.where(ids >= 0, lax.bitwise_xor(turn, q), SPAN)
    member = [jnp.where(label == m, 1.0, 0.0) for m in range(SPAN)]
    stacked = jnp.concatenate(member, axis=0).astype(jnp.bfloat16)
    before = lax.broadcasted_iota(jnp.int32, (LANES, LANES), 0) < lax.broadcasted_iota(
        jnp.int32, (LANES, LANES), 1
    )
    before = jnp.where(before, 1.0, 0.0).astype(jnp.bfloat16)
    ones = jnp.ones((LANES, LANES), jnp.bfloat16)
    size = SPAN * segments
    r = lax.broadcasted_iota(jnp.int32, (size, size), 0)
    c = lax.broadcasted_iota(jnp.int32, (size, size), 1)
    earlier = (lax.div(r, segments) == lax.div(c, segments)) & (c < r)
    earlier = jnp.where(earlier, 1.0, 0.0).astype(jnp.bfloat16)
    r = lax.broadcasted_iota(jnp.int32, (SPAN, size), 0)
    c = lax.broadcasted_iota(jnp.int32, (SPAN, size), 1)
    same = jnp.where(r == lax.div(c, segments), 1.0, 0.0).astype(jnp.bfloat16)
    within = dot(stacked, before)
    start = dot(dot(earlier, stacked).astype(jnp.bfloat16), ones)
    count = dot(dot(same, stacked).astype(jnp.bfloat16), ones).astype(jnp.int32)
    place = (within + start).astype(jnp.int32)
    rank = jnp.zeros_like(ids)
    for m in range(SPAN):
        rank = jnp.where(label == m, place[m * segments : (m + 1) * segments], rank)
    label_ref[...] = label
    rank_ref[...] = rank
    count_ref[...] = count
    over_ref[...] = jnp.max(jnp.where(count > first_refs[0].shape[0], 1, 0), axis=0, keepdims=True)

    for s in range(segments):
        part = pl.ds(s * LANES, LANES)
        copies[s].wait()
        x = raw[part]
        scale = lax.rsqrt(jnp.sum(x * x, axis=1, keepdims=True) + 1e-06)
        normed[part] = (x * scale).astype(jnp.bfloat16)

    pick_rows(PACKED[0], label, rank, count, normed[...], first_refs)


def pack_first(embeddings, ids, blocks, room):
    rows, width = embeddings.shape
    segments = rows // LANES
    vmem = pl.BlockSpec(memory_space=pltpu.VMEM)
    shapes = [jax.ShapeDtypeStruct((room, width), jnp.bfloat16)] * len(PACKED[0])
    shapes += [jax.ShapeDtypeStruct((rows, width), jnp.bfloat16)]
    shapes += [jax.ShapeDtypeStruct((segments, LANES), jnp.int32)] * 2
    shapes += [jax.ShapeDtypeStruct((SPAN, LANES), jnp.int32)]
    shapes += [jax.ShapeDtypeStruct((1, LANES), jnp.int32)]
    return pl.pallas_call(
        functools.partial(pack_first_kernel, blocks),
        out_shape=shapes,
        in_specs=[pl.BlockSpec(memory_space=pl.ANY), vmem],
        out_specs=[vmem] * len(shapes),
        scratch_shapes=[
            pltpu.VMEM((rows, width), jnp.float32),
            pltpu.SemaphoreType.DMA((segments,)),
        ],
        compiler_params=pltpu.CompilerParams(vmem_limit_bytes=PACK_VMEM),
        cost_estimate=pl.CostEstimate(
            flops=2 * GROUP * room * rows * width, bytes_accessed=rows * width * 4, transcendentals=rows
        ),
        name="pack_first",
    )(embeddings, ids)


def pack_more_kernel(messages, normed, label_ref, rank_ref, count_ref, *out_refs):
    label, rank, count = label_ref[...], rank_ref[...], count_ref[...]
    pick_rows(messages, label, rank, count, normed[...], out_refs)


def pack_more(messages, room, normed, label, rank, count):
    rows, width = normed.shape
    vmem = pl.BlockSpec(memory_space=pltpu.VMEM)
    return pl.pallas_call(
        functools.partial(pack_more_kernel, messages),
        out_shape=[jax.ShapeDtypeStruct((room, width), jnp.bfloat16)] * len(messages),
        in_specs=[vmem] * 4,
        out_specs=[vmem] * len(messages),
        compiler_params=pltpu.CompilerParams(vmem_limit_bytes=PACK_VMEM),
        cost_estimate=pl.CostEstimate(
            flops=2 * len(messages) * room * rows * width, bytes_accessed=rows * width * 4, transcendentals=0
        ),
        name=f"pack_{len(messages)}",
    )(normed, label, rank, count)


def same_place(count):
    i = lax.broadcasted_iota(jnp.int32, (count, count), 0)
    j = lax.broadcasted_iota(jnp.int32, (count, count), 1)
    return i == j


def stacked(refs):
    return jnp.concatenate([ref[...] for ref in refs], axis=0)


def join(old, new, before):
    count, width = new.shape
    diagonal = same_place(count)
    unused = jnp.where(new[:, :LANES].astype(jnp.float32)[:, :1] > 1.5, -4.0, 0.0)
    scores = jnp.where(diagonal, -1.0, dot_rows(new, new) + unused)
    best = jnp.max(scores, axis=0, keepdims=True)
    if old is None:
        return None, best
    i = lax.broadcasted_iota(jnp.int32, (16, width), 0)
    j = lax.broadcasted_iota(jnp.int32, (16, width), 1)
    first = jnp.where((i == 0) & (j == 0), 1.0, 0.0).astype(jnp.bfloat16)
    scores = dot_rows(jnp.concatenate([new, first], axis=0), old)
    markers, scores = scores[count : count + 1], scores[:count]
    best_old = jnp.maximum(before, jnp.max(scores + unused, axis=0, keepdims=True))
    best_new = jnp.max(scores + jnp.where(markers > 1.5, -4.0, 0.0), axis=1, keepdims=True)
    best_new = jnp.max(jnp.where(diagonal, best_new, -4.0), axis=0, keepdims=True)
    return best_old, jnp.maximum(best, best_new)


def score_first_kernel(*refs):
    new, (over_ref, best_ref, rows_ref, passed_ref) = refs[:-4], refs[-4:]
    rows_ref[...] = stacked(new)
    best_ref[...] = join(None, rows_ref[...], None)[1]
    passed_ref[...] = over_ref[...]


def score_step_kernel(old_ref, *refs):
    new, (before_ref, best_ref, rows_ref) = refs[:-3], refs[-3:]
    olds = old_ref.shape[0]
    rows_ref[:olds] = old_ref[...]
    rows_ref[olds:] = stacked(new)
    best_old, best_new = join(old_ref[...], rows_ref[olds:], before_ref[...])
    best_ref[...] = jnp.concatenate([best_old, best_new], axis=1)


def score_step(old, new, before):
    room, width = new[0].shape
    vmem = pl.BlockSpec(memory_space=pltpu.VMEM)
    rows = len(new) * room + (0 if old is None else old.shape[0])
    args = (*new, before) if old is None else (old, *new, before)
    shapes = [jax.ShapeDtypeStruct((1, rows), jnp.float32), jax.ShapeDtypeStruct((rows, width), jnp.bfloat16)]
    if old is None:
        shapes += [jax.ShapeDtypeStruct(before.shape, before.dtype)]
    return pl.pallas_call(
        score_first_kernel if old is None else score_step_kernel,
        out_shape=shapes,
        in_specs=[vmem] * len(args),
        out_specs=[vmem] * len(shapes),
        compiler_params=pltpu.CompilerParams(vmem_limit_bytes=SCORE_VMEM),
        cost_estimate=pl.CostEstimate(
            flops=4 * len(new) * room * rows * width, bytes_accessed=rows * width * 2, transcendentals=0
        ),
        name=f"score_{rows // room}",
    )(*args)


def score_last_kernel(blocks, room, old_ref, *refs):
    new, (before_ref, over_ref, other_ref, best_ref) = refs[:-4], refs[-4:]
    me = lax.axis_index("blk")
    flag = jnp.maximum(over_ref[...], other_ref[...]).astype(jnp.float32)
    padded = best_ref.shape[2]
    best_ref[...] = jnp.concatenate([flag[None]] * (padded // LANES), axis=2) + jnp.zeros_like(best_ref)
    bests = []
    for best in join(old_ref[...], stacked(new), before_ref[...]):
        bests += [best[:, i : i + room] for i in range(0, best.shape[1], room)]
    for m, best in zip(sum(STEPS, ()), bests):
        best_ref[blocks - 1 - partner(me, m, blocks, True), :, :room] = jnp.maximum(best, -1.0)


def score_last(old, new, before, over, other, blocks):
    room, width = new[0].shape
    padded = (pl.cdiv(room, LANES) if room % LANES else room // LANES + 1) * LANES
    vmem = pl.BlockSpec(memory_space=pltpu.VMEM)
    return pl.pallas_call(
        functools.partial(score_last_kernel, blocks, room),
        out_shape=jax.ShapeDtypeStruct((blocks, 1, padded), jnp.float32),
        in_specs=[vmem] * (len(new) + 4),
        out_specs=vmem,
        compiler_params=pltpu.CompilerParams(vmem_limit_bytes=SCORE_VMEM),
        name="score_last",
    )(old, *new, before, over, other)


def unpack_kernel(blocks, best_ref, label_ref, rank_ref, out_ref, over_ref):
    label, rank = label_ref[...], rank_ref[...]
    padded = best_ref.shape[2]
    me = lax.axis_index("blk")
    inner = lax.bitwise_and(rank, LANES - 1)
    result = jnp.full(label.shape, -1.0, jnp.float32)
    for m in range(SPAN):
        best = best_ref[blocks - 1 - partner(me, m, blocks, False)]
        for start in range(0, padded, LANES):
            table = jnp.broadcast_to(best[:, start : start + LANES], label.shape)
            value = jnp.take_along_axis(table, inner, axis=1)
            here = (label == m) & (rank >= start) & (rank < start + LANES)
            result = jnp.where(here, value, result)
    out_ref[...] = result
    flags = jnp.max(best_ref[:, :, padded - LANES :], axis=0)
    over_ref[...] = jnp.roll(flags, 1, axis=1).astype(jnp.int32)


def unpack(best, label, rank):
    vmem = pl.BlockSpec(memory_space=pltpu.VMEM)
    return pl.pallas_call(
        functools.partial(unpack_kernel, best.shape[0]),
        out_shape=[
            jax.ShapeDtypeStruct(label.shape, jnp.float32),
            jax.ShapeDtypeStruct((1, LANES), jnp.int32),
        ],
        in_specs=[vmem] * 3,
        out_specs=[vmem] * 2,
        compiler_params=pltpu.CompilerParams(vmem_limit_bytes=4 * 1024 * 1024),
        name="unpack",
    )(best, label, rank)


def by_home(embeddings, cluster_id, rooms):
    blocks = lax.axis_size("blk")
    room = rooms[0]
    ids = cluster_id.reshape(-1, LANES)
    *packed, normed, label, rank, count, over = pack_first(embeddings, ids, blocks, room)
    rows = {m: send(p, m) for m, p in zip(PACKED[0], packed)}
    for messages in PACKED[1:]:
        packed = pack_more(messages, room, normed, label, rank, count)
        rows |= {m: send(p, m) for m, p in zip(messages, packed)}
    best, old, over = score_step(None, [rows[m] for m in STEPS[0]], over)
    other = over
    for distance in range(1, lax.axis_size("parts")):
        other = jnp.maximum(other, shifted(over, "parts", distance))
    for step in STEPS[1:-1]:
        best, old = score_step(old, [rows[m] for m in step], best)
    best = score_last(old, [rows[m] for m in STEPS[-1]], best, over, other, blocks)
    backward = [list(reversed(range(blocks)))]
    returned = lax.all_to_all(best, "blk", 0, 0, axis_index_groups=backward, tiled=True)
    result, flag = unpack(returned, label, rank)

    def again():
        if len(rooms) == 1:
            return by_ring(embeddings, cluster_id)
        return by_home(embeddings, cluster_id, rooms[1:])

    return lax.switch(flag[0, 0], [lambda: result.reshape(-1), again])


def local(embeddings, cluster_id):
    return by_home(embeddings, cluster_id, ROOMS)


def solution(mesh):
    in_specs = (P(("parts", "blk"), None), P(("parts", "blk")))
    out_specs = P(("parts", "blk"))
    return jax.shard_map(local, mesh=mesh, in_specs=in_specs, out_specs=out_specs, check_vma=False)
```

```python
import functools

import jax
import jax.numpy as jnp
from jax import lax
from jax.experimental import pallas as pl
from jax.experimental.pallas import tpu as pltpu
from jax.sharding import PartitionSpec as P

SPAN = 8
HOME = 4
GROUP = 4
ROOMS = (160, 256)
LANES = 128
EMPTY = 2.0
PACK_VMEM = 24 * 1024 * 1024
SCORE_VMEM = 20 * 1024 * 1024


def shifted(block, axis, distance):
    if distance == 0:
        return block
    size = lax.axis_size(axis)
    route = [(i, (i + distance) % size) for i in range(size)]
    return lax.ppermute(block, axis, route)


def block_max(left, left_id, right, right_id, same_block):
    scores = lax.dot_general(
        left, right, (((1,), (1,)), ((), ())), preferred_element_type=jnp.float32
    )
    match = (left_id[:, None] == right_id[None, :]) & (left_id[:, None] >= 0)
    if same_block:
        count = left.shape[0]
        match = match & (jnp.arange(count)[:, None] != jnp.arange(count)[None, :])
    masked = jnp.where(match, scores, jnp.float32(-1.0))
    return (jnp.max(masked, axis=1), jnp.max(masked, axis=0))


def by_ring(embeddings, cluster_id):
    scale = lax.rsqrt(jnp.sum(embeddings * embeddings, axis=1, keepdims=True) + 1e-06)
    normed = (embeddings * scale).astype(jnp.bfloat16)
    best, unused_cols = block_max(normed, cluster_id, normed, cluster_id, True)
    visitor = (normed, cluster_id)
    for offset in range(1, SPAN):
        visitor = (shifted(visitor[0], "blk", 1), shifted(visitor[1], "blk", 1))
        row_best, col_best = block_max(normed, cluster_id, visitor[0], visitor[1], False)
        returned = shifted(col_best, "blk", -offset)
        best = jnp.maximum(best, jnp.maximum(row_best, returned))
    return best


OWN = GROUP
PACKED = ((6, 0), (7, 2, OWN), (1, 3, 5))
STEPS = ((OWN, 6, 0), (7, 2, 5), (1, 3))


def target(block, m, blocks):
    q = block % GROUP
    r = q ^ (m % GROUP)
    step = 0 if m >= GROUP else GROUP if r <= q else -GROUP
    return (block - q + r + step) % blocks


def partner(me, m, blocks, sender):
    q = lax.rem(me, GROUP)
    r = lax.bitwise_xor(q, m % GROUP)
    if m >= GROUP:
        return me - q + r
    back = (q <= r) if sender else (r > q)
    step = jnp.where(back, blocks - GROUP, GROUP)
    return lax.rem(me - q + r + step, blocks)


def send(rows, m):
    if m == OWN:
        return rows
    blocks = lax.axis_size("blk")
    return lax.ppermute(rows, "blk", [(i, target(i, m, blocks)) for i in range(blocks)])


def dot(a, b):
    return jnp.dot(a, b, preferred_element_type=jnp.float32)


def dot_rows(a, b):
    return lax.dot_general(a, b, (((1,), (1,)), ((), ())), preferred_element_type=jnp.float32)


def selection(messages, label, rank, room):
    slot = lax.broadcasted_iota(jnp.int32, (room, LANES), 0)
    rows = []
    for m in messages:
        key = jnp.where(label == m, rank, -1)
        here = [jnp.where(slot == key[s : s + 1], 1.0, 0.0) for s in range(label.shape[0])]
        rows.append(jnp.concatenate([h.astype(jnp.bfloat16) for h in here], axis=1))
    return jnp.concatenate(rows, axis=0)


def pick_rows(messages, selected, count, normed, out_refs):
    room = out_refs[0].shape[0]
    slot = lax.broadcasted_iota(jnp.int32, (room, LANES), 0)
    lane = lax.broadcasted_iota(jnp.int32, (room, LANES), 1)
    picked = dot(selected, normed)
    for i, (m, out_ref) in enumerate(zip(messages, out_refs)):
        rows = picked[i * room : (i + 1) * room]
        empty = (slot >= count[m : m + 1]) & (lane == 0)
        first = jnp.where(empty, EMPTY, rows[:, :LANES])
        out_ref[:, :LANES] = first.astype(jnp.bfloat16)
        out_ref[:, LANES:] = rows[:, LANES:].astype(jnp.bfloat16)


def pack_first_kernel(blocks, emb_ref, id_ref, *refs):
    first_refs, refs = refs[: len(PACKED[0])], refs[len(PACKED[0]) :]
    normed, label_ref, rank_ref, count_ref, over_ref, raw, selected_ref, arrived = refs
    rows, width = normed.shape
    segments = rows // LANES
    copies = []
    for s in range(segments):
        part = pl.ds(s * LANES, LANES)
        copies.append(pltpu.make_async_copy(emb_ref.at[part], raw.at[part], arrived.at[s]))
        copies[-1].start()

    me = lax.axis_index("blk")
    ids = id_ref[...]
    q = lax.rem(me, GROUP)
    offset = lax.rem(me - ids + 2 * blocks, blocks)
    turn = lax.bitwise_and(q - offset + SPAN, SPAN - 1)
    label = jnp.where(ids >= 0, lax.bitwise_xor(turn, q), SPAN)
    member = [jnp.where(label == m, 1.0, 0.0) for m in range(SPAN)]
    stacked = jnp.concatenate(member, axis=0).astype(jnp.bfloat16)
    before = lax.broadcasted_iota(jnp.int32, (LANES, LANES), 0) < lax.broadcasted_iota(
        jnp.int32, (LANES, LANES), 1
    )
    before = jnp.where(before, 1.0, 0.0).astype(jnp.bfloat16)
    ones = jnp.ones((LANES, LANES), jnp.bfloat16)
    size = SPAN * segments
    r = lax.broadcasted_iota(jnp.int32, (size, size), 0)
    c = lax.broadcasted_iota(jnp.int32, (size, size), 1)
    earlier = (lax.div(r, segments) == lax.div(c, segments)) & (c < r)
    earlier = jnp.where(earlier, 1.0, 0.0).astype(jnp.bfloat16)
    r = lax.broadcasted_iota(jnp.int32, (SPAN, size), 0)
    c = lax.broadcasted_iota(jnp.int32, (SPAN, size), 1)
    same = jnp.where(r == lax.div(c, segments), 1.0, 0.0).astype(jnp.bfloat16)
    within = dot(stacked, before)
    start = dot(dot(earlier, stacked).astype(jnp.bfloat16), ones)
    count = dot(dot(same, stacked).astype(jnp.bfloat16), ones).astype(jnp.int32)
    place = (within + start).astype(jnp.int32)
    rank = jnp.zeros_like(ids)
    for m in range(SPAN):
        rank = jnp.where(label == m, place[m * segments : (m + 1) * segments], rank)
    label_ref[...] = label
    rank_ref[...] = rank
    count_ref[...] = count
    over_ref[...] = jnp.max(jnp.where(count > first_refs[0].shape[0], 1, 0), axis=0, keepdims=True)

    selected_ref[...] = selection(PACKED[0], label, rank, first_refs[0].shape[0])
    for s in range(segments):
        part = pl.ds(s * LANES, LANES)
        copies[s].wait()
        x = raw[part]
        scale = lax.rsqrt(jnp.sum(x * x, axis=1, keepdims=True) + 1e-06)
        normed[part] = (x * scale).astype(jnp.bfloat16)

    pick_rows(PACKED[0], selected_ref[...], count, normed[...], first_refs)


def pack_first(embeddings, ids, blocks, room):
    rows, width = embeddings.shape
    segments = rows // LANES
    vmem = pl.BlockSpec(memory_space=pltpu.VMEM)
    shapes = [jax.ShapeDtypeStruct((room, width), jnp.bfloat16)] * len(PACKED[0])
    shapes += [jax.ShapeDtypeStruct((rows, width), jnp.bfloat16)]
    shapes += [jax.ShapeDtypeStruct((segments, LANES), jnp.int32)] * 2
    shapes += [jax.ShapeDtypeStruct((SPAN, LANES), jnp.int32)]
    shapes += [jax.ShapeDtypeStruct((1, LANES), jnp.int32)]
    return pl.pallas_call(
        functools.partial(pack_first_kernel, blocks),
        out_shape=shapes,
        in_specs=[pl.BlockSpec(memory_space=pl.ANY), vmem],
        out_specs=[vmem] * len(shapes),
        scratch_shapes=[
            pltpu.VMEM((rows, width), jnp.float32),
            pltpu.VMEM((len(PACKED[0]) * room, rows), jnp.bfloat16),
            pltpu.SemaphoreType.DMA((segments,)),
        ],
        compiler_params=pltpu.CompilerParams(vmem_limit_bytes=PACK_VMEM),
        cost_estimate=pl.CostEstimate(
            flops=2 * GROUP * room * rows * width, bytes_accessed=rows * width * 4, transcendentals=rows
        ),
        name="pack_first",
    )(embeddings, ids)


def pack_more_kernel(messages, normed, label_ref, rank_ref, count_ref, *out_refs):
    label, rank, count = label_ref[...], rank_ref[...], count_ref[...]
    selected = selection(messages, label, rank, out_refs[0].shape[0])
    pick_rows(messages, selected, count, normed[...], out_refs)


def pack_more(messages, room, normed, label, rank, count):
    rows, width = normed.shape
    vmem = pl.BlockSpec(memory_space=pltpu.VMEM)
    return pl.pallas_call(
        functools.partial(pack_more_kernel, messages),
        out_shape=[jax.ShapeDtypeStruct((room, width), jnp.bfloat16)] * len(messages),
        in_specs=[vmem] * 4,
        out_specs=[vmem] * len(messages),
        compiler_params=pltpu.CompilerParams(vmem_limit_bytes=PACK_VMEM),
        cost_estimate=pl.CostEstimate(
            flops=2 * len(messages) * room * rows * width, bytes_accessed=rows * width * 4, transcendentals=0
        ),
        name=f"pack_{len(messages)}",
    )(normed, label, rank, count)


def same_place(count):
    i = lax.broadcasted_iota(jnp.int32, (count, count), 0)
    j = lax.broadcasted_iota(jnp.int32, (count, count), 1)
    return i == j


def stacked(refs):
    return jnp.concatenate([ref[...] for ref in refs], axis=0)


def join(old, new, before):
    count, width = new.shape
    diagonal = same_place(count)
    unused = jnp.where(new[:, :LANES].astype(jnp.float32)[:, :1] > 1.5, -4.0, 0.0)
    scores = jnp.where(diagonal, -1.0, dot_rows(new, new) + unused)
    best = jnp.max(scores, axis=0, keepdims=True)
    if old is None:
        return None, best
    i = lax.broadcasted_iota(jnp.int32, (16, width), 0)
    j = lax.broadcasted_iota(jnp.int32, (16, width), 1)
    first = jnp.where((i == 0) & (j == 0), 1.0, 0.0).astype(jnp.bfloat16)
    scores = dot_rows(jnp.concatenate([new, first], axis=0), old)
    markers, scores = scores[count : count + 1], scores[:count]
    best_old = jnp.maximum(before, jnp.max(scores + unused, axis=0, keepdims=True))
    best_new = jnp.max(scores + jnp.where(markers > 1.5, -4.0, 0.0), axis=1, keepdims=True)
    best_new = jnp.max(jnp.where(diagonal, best_new, -4.0), axis=0, keepdims=True)
    return best_old, jnp.maximum(best, best_new)


def score_first_kernel(*refs):
    new, (over_ref, best_ref, rows_ref, passed_ref) = refs[:-4], refs[-4:]
    rows_ref[...] = stacked(new)
    best_ref[...] = join(None, rows_ref[...], None)[1]
    passed_ref[...] = over_ref[...]


def score_step_kernel(old_ref, *refs):
    new, (before_ref, best_ref, rows_ref) = refs[:-3], refs[-3:]
    olds = old_ref.shape[0]
    rows_ref[:olds] = old_ref[...]
    rows_ref[olds:] = stacked(new)
    best_old, best_new = join(old_ref[...], rows_ref[olds:], before_ref[...])
    best_ref[...] = jnp.concatenate([best_old, best_new], axis=1)


def score_step(old, new, before):
    room, width = new[0].shape
    vmem = pl.BlockSpec(memory_space=pltpu.VMEM)
    rows = len(new) * room + (0 if old is None else old.shape[0])
    args = (*new, before) if old is None else (old, *new, before)
    shapes = [jax.ShapeDtypeStruct((1, rows), jnp.float32), jax.ShapeDtypeStruct((rows, width), jnp.bfloat16)]
    if old is None:
        shapes += [jax.ShapeDtypeStruct(before.shape, before.dtype)]
    return pl.pallas_call(
        score_first_kernel if old is None else score_step_kernel,
        out_shape=shapes,
        in_specs=[vmem] * len(args),
        out_specs=[vmem] * len(shapes),
        compiler_params=pltpu.CompilerParams(vmem_limit_bytes=SCORE_VMEM),
        cost_estimate=pl.CostEstimate(
            flops=4 * len(new) * room * rows * width, bytes_accessed=rows * width * 2, transcendentals=0
        ),
        name=f"score_{rows // room}",
    )(*args)


def score_last_kernel(blocks, room, old_ref, *refs):
    new, (before_ref, over_ref, other_ref, best_ref) = refs[:-4], refs[-4:]
    me = lax.axis_index("blk")
    flag = jnp.maximum(over_ref[...], other_ref[...]).astype(jnp.float32)
    padded = best_ref.shape[2]
    best_ref[...] = jnp.concatenate([flag[None]] * (padded // LANES), axis=2) + jnp.zeros_like(best_ref)
    bests = []
    for best in join(old_ref[...], stacked(new), before_ref[...]):
        bests += [best[:, i : i + room] for i in range(0, best.shape[1], room)]
    for m, best in zip(sum(STEPS, ()), bests):
        best_ref[blocks - 1 - partner(me, m, blocks, True), :, :room] = jnp.maximum(best, -1.0)


def score_last(old, new, before, over, other, blocks):
    room, width = new[0].shape
    padded = (pl.cdiv(room, LANES) if room % LANES else room // LANES + 1) * LANES
    vmem = pl.BlockSpec(memory_space=pltpu.VMEM)
    return pl.pallas_call(
        functools.partial(score_last_kernel, blocks, room),
        out_shape=jax.ShapeDtypeStruct((blocks, 1, padded), jnp.float32),
        in_specs=[vmem] * (len(new) + 4),
        out_specs=vmem,
        compiler_params=pltpu.CompilerParams(vmem_limit_bytes=SCORE_VMEM),
        name="score_last",
    )(old, *new, before, over, other)


def unpack_kernel(blocks, best_ref, label_ref, rank_ref, out_ref, over_ref):
    label, rank = label_ref[...], rank_ref[...]
    padded = best_ref.shape[2]
    me = lax.axis_index("blk")
    inner = lax.bitwise_and(rank, LANES - 1)
    result = jnp.full(label.shape, -1.0, jnp.float32)
    for m in range(SPAN):
        best = best_ref[blocks - 1 - partner(me, m, blocks, False)]
        for start in range(0, padded, LANES):
            table = jnp.broadcast_to(best[:, start : start + LANES], label.shape)
            value = jnp.take_along_axis(table, inner, axis=1)
            here = (label == m) & (rank >= start) & (rank < start + LANES)
            result = jnp.where(here, value, result)
    out_ref[...] = result
    flags = jnp.max(best_ref[:, :, padded - LANES :], axis=0)
    over_ref[...] = jnp.roll(flags, 1, axis=1).astype(jnp.int32)


def unpack(best, label, rank):
    vmem = pl.BlockSpec(memory_space=pltpu.VMEM)
    return pl.pallas_call(
        functools.partial(unpack_kernel, best.shape[0]),
        out_shape=[
            jax.ShapeDtypeStruct(label.shape, jnp.float32),
            jax.ShapeDtypeStruct((1, LANES), jnp.int32),
        ],
        in_specs=[vmem] * 3,
        out_specs=[vmem] * 2,
        compiler_params=pltpu.CompilerParams(vmem_limit_bytes=4 * 1024 * 1024),
        name="unpack",
    )(best, label, rank)


def by_home(embeddings, cluster_id, rooms):
    blocks = lax.axis_size("blk")
    room = rooms[0]
    ids = cluster_id.reshape(-1, LANES)
    *packed, normed, label, rank, count, over = pack_first(embeddings, ids, blocks, room)
    rows = {m: send(p, m) for m, p in zip(PACKED[0], packed)}
    for messages in PACKED[1:]:
        packed = pack_more(messages, room, normed, label, rank, count)
        rows |= {m: send(p, m) for m, p in zip(messages, packed)}
    best, old, over = score_step(None, [rows[m] for m in STEPS[0]], over)
    other = over
    for distance in range(1, lax.axis_size("parts")):
        other = jnp.maximum(other, shifted(over, "parts", distance))
    for step in STEPS[1:-1]:
        best, old = score_step(old, [rows[m] for m in step], best)
    best = score_last(old, [rows[m] for m in STEPS[-1]], best, over, other, blocks)
    backward = [list(reversed(range(blocks)))]
    returned = lax.all_to_all(best, "blk", 0, 0, axis_index_groups=backward, tiled=True)
    result, flag = unpack(returned, label, rank)

    def again():
        if len(rooms) == 1:
            return by_ring(embeddings, cluster_id)
        return by_home(embeddings, cluster_id, rooms[1:])

    return lax.switch(flag[0, 0], [lambda: result.reshape(-1), again])


def local(embeddings, cluster_id):
    return by_home(embeddings, cluster_id, ROOMS)


def solution(mesh):
    in_specs = (P(("parts", "blk"), None), P(("parts", "blk")))
    out_specs = P(("parts", "blk"))
    return jax.shard_map(local, mesh=mesh, in_specs=in_specs, out_specs=out_specs, check_vma=False)
```

```python
import functools

import jax
import jax.numpy as jnp
from jax import lax
from jax.experimental import pallas as pl
from jax.experimental.pallas import tpu as pltpu
from jax.sharding import PartitionSpec as P

SPAN = 8
HOME = 4
GROUP = 4
ROOMS = (160, 256)
LANES = 128
EMPTY = 2.0
PACK_VMEM = 24 * 1024 * 1024
SCORE_VMEM = 20 * 1024 * 1024


def shifted(block, axis, distance):
    if distance == 0:
        return block
    size = lax.axis_size(axis)
    route = [(i, (i + distance) % size) for i in range(size)]
    return lax.ppermute(block, axis, route)


def block_max(left, left_id, right, right_id, same_block):
    scores = lax.dot_general(
        left, right, (((1,), (1,)), ((), ())), preferred_element_type=jnp.float32
    )
    match = (left_id[:, None] == right_id[None, :]) & (left_id[:, None] >= 0)
    if same_block:
        count = left.shape[0]
        match = match & (jnp.arange(count)[:, None] != jnp.arange(count)[None, :])
    masked = jnp.where(match, scores, jnp.float32(-1.0))
    return (jnp.max(masked, axis=1), jnp.max(masked, axis=0))


def by_ring(embeddings, cluster_id):
    scale = lax.rsqrt(jnp.sum(embeddings * embeddings, axis=1, keepdims=True) + 1e-06)
    normed = (embeddings * scale).astype(jnp.bfloat16)
    best, unused_cols = block_max(normed, cluster_id, normed, cluster_id, True)
    visitor = (normed, cluster_id)
    for offset in range(1, SPAN):
        visitor = (shifted(visitor[0], "blk", 1), shifted(visitor[1], "blk", 1))
        row_best, col_best = block_max(normed, cluster_id, visitor[0], visitor[1], False)
        returned = shifted(col_best, "blk", -offset)
        best = jnp.maximum(best, jnp.maximum(row_best, returned))
    return best


OWN = GROUP
PACKED = ((6, 0), (7, 2, 5, OWN), (1, 3))
STEPS = ((OWN, 6, 0), (7, 2, 5), (1, 3))


def target(block, m, blocks):
    q = block % GROUP
    r = q ^ (m % GROUP)
    step = 0 if m >= GROUP else GROUP if r <= q else -GROUP
    return (block - q + r + step) % blocks


def partner(me, m, blocks, sender):
    q = lax.rem(me, GROUP)
    r = lax.bitwise_xor(q, m % GROUP)
    if m >= GROUP:
        return me - q + r
    back = (q <= r) if sender else (r > q)
    step = jnp.where(back, blocks - GROUP, GROUP)
    return lax.rem(me - q + r + step, blocks)


def send(rows, m):
    if m == OWN:
        return rows
    blocks = lax.axis_size("blk")
    return lax.ppermute(rows, "blk", [(i, target(i, m, blocks)) for i in range(blocks)])


def dot(a, b):
    return jnp.dot(a, b, preferred_element_type=jnp.float32)


def dot_rows(a, b):
    return lax.dot_general(a, b, (((1,), (1,)), ((), ())), preferred_element_type=jnp.float32)


def selection(messages, label, rank, room):
    slot = lax.broadcasted_iota(jnp.int32, (room, LANES), 0)
    rows = []
    for m in messages:
        key = jnp.where(label == m, rank, -1)
        here = [jnp.where(slot == key[s : s + 1], 1.0, 0.0) for s in range(label.shape[0])]
        rows.append(jnp.concatenate([h.astype(jnp.bfloat16) for h in here], axis=1))
    return jnp.concatenate(rows, axis=0)


def put_rows(messages, picked, count, out_refs):
    room = out_refs[0].shape[0]
    slot = lax.broadcasted_iota(jnp.int32, (room, LANES), 0)
    lane = lax.broadcasted_iota(jnp.int32, (room, LANES), 1)
    for i, (m, out_ref) in enumerate(zip(messages, out_refs)):
        rows = picked[i * room : (i + 1) * room]
        empty = (slot >= count[m : m + 1]) & (lane == 0)
        first = jnp.where(empty, EMPTY, rows[:, :LANES])
        out_ref[:, :LANES] = first.astype(jnp.bfloat16)
        out_ref[:, LANES:] = rows[:, LANES:].astype(jnp.bfloat16)


def pack_first_kernel(blocks, emb_ref, id_ref, *refs):
    first_refs, refs = refs[: len(PACKED[0])], refs[len(PACKED[0]) :]
    normed, label_ref, rank_ref, count_ref, over_ref, raw, selected_ref, picked_ref, arrived = refs
    rows, width = normed.shape
    segments = rows // LANES
    copies = []
    for s in range(segments):
        part = pl.ds(s * LANES, LANES)
        copies.append(pltpu.make_async_copy(emb_ref.at[part], raw.at[part], arrived.at[s]))
        copies[-1].start()

    me = lax.axis_index("blk")
    ids = id_ref[...]
    q = lax.rem(me, GROUP)
    offset = lax.rem(me - ids + 2 * blocks, blocks)
    turn = lax.bitwise_and(q - offset + SPAN, SPAN - 1)
    label = jnp.where(ids >= 0, lax.bitwise_xor(turn, q), SPAN)
    member = [jnp.where(label == m, 1.0, 0.0) for m in range(SPAN)]
    stacked = jnp.concatenate(member, axis=0).astype(jnp.bfloat16)
    before = lax.broadcasted_iota(jnp.int32, (LANES, LANES), 0) < lax.broadcasted_iota(
        jnp.int32, (LANES, LANES), 1
    )
    before = jnp.where(before, 1.0, 0.0).astype(jnp.bfloat16)
    ones = jnp.ones((LANES, LANES), jnp.bfloat16)
    size = SPAN * segments
    r = lax.broadcasted_iota(jnp.int32, (size, size), 0)
    c = lax.broadcasted_iota(jnp.int32, (size, size), 1)
    earlier = (lax.div(r, segments) == lax.div(c, segments)) & (c < r)
    earlier = jnp.where(earlier, 1.0, 0.0).astype(jnp.bfloat16)
    r = lax.broadcasted_iota(jnp.int32, (SPAN, size), 0)
    c = lax.broadcasted_iota(jnp.int32, (SPAN, size), 1)
    same = jnp.where(r == lax.div(c, segments), 1.0, 0.0).astype(jnp.bfloat16)
    within = dot(stacked, before)
    start = dot(dot(earlier, stacked).astype(jnp.bfloat16), ones)
    count = dot(dot(same, stacked).astype(jnp.bfloat16), ones).astype(jnp.int32)
    place = (within + start).astype(jnp.int32)
    rank = jnp.zeros_like(ids)
    for m in range(SPAN):
        rank = jnp.where(label == m, place[m * segments : (m + 1) * segments], rank)
    label_ref[...] = label
    rank_ref[...] = rank
    count_ref[...] = count
    over_ref[...] = jnp.max(jnp.where(count > first_refs[0].shape[0], 1, 0), axis=0, keepdims=True)

    selected_ref[...] = selection(PACKED[0], label, rank, first_refs[0].shape[0])
    for s in range(segments):
        part = pl.ds(s * LANES, LANES)
        copies[s].wait()
        x = raw[part]
        scale = lax.rsqrt(jnp.sum(x * x, axis=1, keepdims=True) + 1e-06)
        normed[part] = (x * scale).astype(jnp.bfloat16)
        if s % 2:
            pair = pl.ds((s - 1) * LANES, 2 * LANES)
            product = dot(selected_ref[:, pair], normed[pair])
            picked_ref[...] = product if s == 1 else picked_ref[...] + product

    put_rows(PACKED[0], picked_ref[...], count, first_refs)


def pack_first(embeddings, ids, blocks, room):
    rows, width = embeddings.shape
    segments = rows // LANES
    vmem = pl.BlockSpec(memory_space=pltpu.VMEM)
    shapes = [jax.ShapeDtypeStruct((room, width), jnp.bfloat16)] * len(PACKED[0])
    shapes += [jax.ShapeDtypeStruct((rows, width), jnp.bfloat16)]
    shapes += [jax.ShapeDtypeStruct((segments, LANES), jnp.int32)] * 2
    shapes += [jax.ShapeDtypeStruct((SPAN, LANES), jnp.int32)]
    shapes += [jax.ShapeDtypeStruct((1, LANES), jnp.int32)]
    return pl.pallas_call(
        functools.partial(pack_first_kernel, blocks),
        out_shape=shapes,
        in_specs=[pl.BlockSpec(memory_space=pl.ANY), vmem],
        out_specs=[vmem] * len(shapes),
        scratch_shapes=[
            pltpu.VMEM((rows, width), jnp.float32),
            pltpu.VMEM((len(PACKED[0]) * room, rows), jnp.bfloat16),
            pltpu.VMEM((len(PACKED[0]) * room, width), jnp.float32),
            pltpu.SemaphoreType.DMA((segments,)),
        ],
        compiler_params=pltpu.CompilerParams(vmem_limit_bytes=PACK_VMEM),
        cost_estimate=pl.CostEstimate(
            flops=2 * GROUP * room * rows * width, bytes_accessed=rows * width * 4, transcendentals=rows
        ),
        name="pack_first",
    )(embeddings, ids)


def pack_more_kernel(messages, normed, label_ref, rank_ref, count_ref, *out_refs):
    label, rank, count = label_ref[...], rank_ref[...], count_ref[...]
    selected = selection(messages, label, rank, out_refs[0].shape[0])
    put_rows(messages, dot(selected, normed[...]), count, out_refs)


def pack_more(messages, room, normed, label, rank, count):
    rows, width = normed.shape
    vmem = pl.BlockSpec(memory_space=pltpu.VMEM)
    return pl.pallas_call(
        functools.partial(pack_more_kernel, messages),
        out_shape=[jax.ShapeDtypeStruct((room, width), jnp.bfloat16)] * len(messages),
        in_specs=[vmem] * 4,
        out_specs=[vmem] * len(messages),
        compiler_params=pltpu.CompilerParams(vmem_limit_bytes=PACK_VMEM),
        cost_estimate=pl.CostEstimate(
            flops=2 * len(messages) * room * rows * width, bytes_accessed=rows * width * 4, transcendentals=0
        ),
        name=f"pack_{len(messages)}",
    )(normed, label, rank, count)


def same_place(count):
    i = lax.broadcasted_iota(jnp.int32, (count, count), 0)
    j = lax.broadcasted_iota(jnp.int32, (count, count), 1)
    return i == j


def stacked(refs):
    return jnp.concatenate([ref[...] for ref in refs], axis=0)


def join(old, new, before):
    count, width = new.shape
    diagonal = same_place(count)
    unused = jnp.where(new[:, :LANES].astype(jnp.float32)[:, :1] > 1.5, -4.0, 0.0)
    scores = jnp.where(diagonal, -1.0, dot_rows(new, new) + unused)
    best = jnp.max(scores, axis=0, keepdims=True)
    if old is None:
        return None, best
    i = lax.broadcasted_iota(jnp.int32, (16, width), 0)
    j = lax.broadcasted_iota(jnp.int32, (16, width), 1)
    first = jnp.where((i == 0) & (j == 0), 1.0, 0.0).astype(jnp.bfloat16)
    scores = dot_rows(jnp.concatenate([new, first], axis=0), old)
    markers, scores = scores[count : count + 1], scores[:count]
    best_old = jnp.maximum(before, jnp.max(scores + unused, axis=0, keepdims=True))
    best_new = jnp.max(scores + jnp.where(markers > 1.5, -4.0, 0.0), axis=1, keepdims=True)
    best_new = jnp.max(jnp.where(diagonal, best_new, -4.0), axis=0, keepdims=True)
    return best_old, jnp.maximum(best, best_new)


def score_first_kernel(*refs):
    new, (over_ref, best_ref, rows_ref, passed_ref) = refs[:-4], refs[-4:]
    rows_ref[...] = stacked(new)
    best_ref[...] = join(None, rows_ref[...], None)[1]
    passed_ref[...] = over_ref[...]


def score_step_kernel(old_ref, *refs):
    new, (before_ref, best_ref, rows_ref) = refs[:-3], refs[-3:]
    olds = old_ref.shape[0]
    rows_ref[:olds] = old_ref[...]
    rows_ref[olds:] = stacked(new)
    best_old, best_new = join(old_ref[...], rows_ref[olds:], before_ref[...])
    best_ref[...] = jnp.concatenate([best_old, best_new], axis=1)


def score_step(old, new, before):
    room, width = new[0].shape
    vmem = pl.BlockSpec(memory_space=pltpu.VMEM)
    rows = len(new) * room + (0 if old is None else old.shape[0])
    args = (*new, before) if old is None else (old, *new, before)
    shapes = [jax.ShapeDtypeStruct((1, rows), jnp.float32), jax.ShapeDtypeStruct((rows, width), jnp.bfloat16)]
    if old is None:
        shapes += [jax.ShapeDtypeStruct(before.shape, before.dtype)]
    return pl.pallas_call(
        score_first_kernel if old is None else score_step_kernel,
        out_shape=shapes,
        in_specs=[vmem] * len(args),
        out_specs=[vmem] * len(shapes),
        compiler_params=pltpu.CompilerParams(vmem_limit_bytes=SCORE_VMEM),
        cost_estimate=pl.CostEstimate(
            flops=4 * len(new) * room * rows * width, bytes_accessed=rows * width * 2, transcendentals=0
        ),
        name=f"score_{rows // room}",
    )(*args)


def score_last_kernel(blocks, room, old_ref, *refs):
    new, (before_ref, over_ref, other_ref, best_ref) = refs[:-4], refs[-4:]
    me = lax.axis_index("blk")
    flag = jnp.maximum(over_ref[...], other_ref[...]).astype(jnp.float32)
    padded = best_ref.shape[2]
    best_ref[...] = jnp.concatenate([flag[None]] * (padded // LANES), axis=2) + jnp.zeros_like(best_ref)
    bests = []
    for best in join(old_ref[...], stacked(new), before_ref[...]):
        bests += [best[:, i : i + room] for i in range(0, best.shape[1], room)]
    for m, best in zip(sum(STEPS, ()), bests):
        best_ref[blocks - 1 - partner(me, m, blocks, True), :, :room] = jnp.maximum(best, -1.0)


def score_last(old, new, before, over, other, blocks):
    room, width = new[0].shape
    padded = (pl.cdiv(room, LANES) if room % LANES else room // LANES + 1) * LANES
    vmem = pl.BlockSpec(memory_space=pltpu.VMEM)
    return pl.pallas_call(
        functools.partial(score_last_kernel, blocks, room),
        out_shape=jax.ShapeDtypeStruct((blocks, 1, padded), jnp.float32),
        in_specs=[vmem] * (len(new) + 4),
        out_specs=vmem,
        compiler_params=pltpu.CompilerParams(vmem_limit_bytes=SCORE_VMEM),
        name="score_last",
    )(old, *new, before, over, other)


def unpack_kernel(blocks, best_ref, label_ref, rank_ref, out_ref, over_ref):
    label, rank = label_ref[...], rank_ref[...]
    padded = best_ref.shape[2]
    me = lax.axis_index("blk")
    inner = lax.bitwise_and(rank, LANES - 1)
    result = jnp.full(label.shape, -1.0, jnp.float32)
    for m in range(SPAN):
        best = best_ref[blocks - 1 - partner(me, m, blocks, False)]
        for start in range(0, padded, LANES):
            table = jnp.broadcast_to(best[:, start : start + LANES], label.shape)
            value = jnp.take_along_axis(table, inner, axis=1)
            here = (label == m) & (rank >= start) & (rank < start + LANES)
            result = jnp.where(here, value, result)
    out_ref[...] = result
    flags = jnp.max(best_ref[:, :, padded - LANES :], axis=0)
    over_ref[...] = jnp.roll(flags, 1, axis=1).astype(jnp.int32)


def unpack(best, label, rank):
    vmem = pl.BlockSpec(memory_space=pltpu.VMEM)
    return pl.pallas_call(
        functools.partial(unpack_kernel, best.shape[0]),
        out_shape=[
            jax.ShapeDtypeStruct(label.shape, jnp.float32),
            jax.ShapeDtypeStruct((1, LANES), jnp.int32),
        ],
        in_specs=[vmem] * 3,
        out_specs=[vmem] * 2,
        compiler_params=pltpu.CompilerParams(vmem_limit_bytes=4 * 1024 * 1024),
        name="unpack",
    )(best, label, rank)


def by_home(embeddings, cluster_id, rooms):
    blocks = lax.axis_size("blk")
    room = rooms[0]
    ids = cluster_id.reshape(-1, LANES)
    *packed, normed, label, rank, count, over = pack_first(embeddings, ids, blocks, room)
    rows = {m: send(p, m) for m, p in zip(PACKED[0], packed)}
    for messages in PACKED[1:]:
        packed = pack_more(messages, room, normed, label, rank, count)
        rows |= {m: send(p, m) for m, p in zip(messages, packed)}
    best, old, over = score_step(None, [rows[m] for m in STEPS[0]], over)
    other = over
    for distance in range(1, lax.axis_size("parts")):
        other = jnp.maximum(other, shifted(over, "parts", distance))
    for step in STEPS[1:-1]:
        best, old = score_step(old, [rows[m] for m in step], best)
    best = score_last(old, [rows[m] for m in STEPS[-1]], best, over, other, blocks)
    backward = [list(reversed(range(blocks)))]
    returned = lax.all_to_all(best, "blk", 0, 0, axis_index_groups=backward, tiled=True)
    result, flag = unpack(returned, label, rank)

    def again():
        if len(rooms) == 1:
            return by_ring(embeddings, cluster_id)
        return by_home(embeddings, cluster_id, rooms[1:])

    return lax.switch(flag[0, 0], [lambda: result.reshape(-1), again])


def local(embeddings, cluster_id):
    return by_home(embeddings, cluster_id, ROOMS)


def solution(mesh):
    in_specs = (P(("parts", "blk"), None), P(("parts", "blk")))
    out_specs = P(("parts", "blk"))
    return jax.shard_map(local, mesh=mesh, in_specs=in_specs, out_specs=out_specs, check_vma=False)
```

```python
import functools

import jax
import jax.numpy as jnp
from jax import lax
from jax.experimental import pallas as pl
from jax.experimental.pallas import tpu as pltpu
from jax.sharding import PartitionSpec as P

SPAN = 8
HOME = 4
GROUP = 4
ROOMS = (160, 256)
LANES = 128
EMPTY = 2.0
PACK_VMEM = 24 * 1024 * 1024
SCORE_VMEM = 20 * 1024 * 1024


def shifted(block, axis, distance):
    if distance == 0:
        return block
    size = lax.axis_size(axis)
    route = [(i, (i + distance) % size) for i in range(size)]
    return lax.ppermute(block, axis, route)


def block_max(left, left_id, right, right_id, same_block):
    scores = lax.dot_general(
        left, right, (((1,), (1,)), ((), ())), preferred_element_type=jnp.float32
    )
    match = (left_id[:, None] == right_id[None, :]) & (left_id[:, None] >= 0)
    if same_block:
        count = left.shape[0]
        match = match & (jnp.arange(count)[:, None] != jnp.arange(count)[None, :])
    masked = jnp.where(match, scores, jnp.float32(-1.0))
    return (jnp.max(masked, axis=1), jnp.max(masked, axis=0))


def by_ring(embeddings, cluster_id):
    scale = lax.rsqrt(jnp.sum(embeddings * embeddings, axis=1, keepdims=True) + 1e-06)
    normed = (embeddings * scale).astype(jnp.bfloat16)
    best, unused_cols = block_max(normed, cluster_id, normed, cluster_id, True)
    visitor = (normed, cluster_id)
    for offset in range(1, SPAN):
        visitor = (shifted(visitor[0], "blk", 1), shifted(visitor[1], "blk", 1))
        row_best, col_best = block_max(normed, cluster_id, visitor[0], visitor[1], False)
        returned = shifted(col_best, "blk", -offset)
        best = jnp.maximum(best, jnp.maximum(row_best, returned))
    return best


OWN = GROUP
PACKED = ((6, 0), (7, 2, 5, OWN), (1, 3))
STEPS = ((OWN, 6, 0), (7, 2, 5), (1, 3))


def target(block, m, blocks):
    q = block % GROUP
    r = q ^ (m % GROUP)
    step = 0 if m >= GROUP else GROUP if r <= q else -GROUP
    return (block - q + r + step) % blocks


def partner(me, m, blocks, sender):
    q = lax.rem(me, GROUP)
    r = lax.bitwise_xor(q, m % GROUP)
    if m >= GROUP:
        return me - q + r
    back = (q <= r) if sender else (r > q)
    step = jnp.where(back, blocks - GROUP, GROUP)
    return lax.rem(me - q + r + step, blocks)


def send(rows, m):
    if m == OWN:
        return rows
    blocks = lax.axis_size("blk")
    return lax.ppermute(rows, "blk", [(i, target(i, m, blocks)) for i in range(blocks)])


def dot(a, b):
    return jnp.dot(a, b, preferred_element_type=jnp.float32)


def dot_rows(a, b):
    return lax.dot_general(a, b, (((1,), (1,)), ((), ())), preferred_element_type=jnp.float32)


def selection(messages, label, rank, room):
    slot = lax.broadcasted_iota(jnp.int32, (room, LANES), 0)
    rows = []
    for m in messages:
        key = jnp.where(label == m, rank, -1)
        here = [jnp.where(slot == key[s : s + 1], 1.0, 0.0) for s in range(label.shape[0])]
        rows.append(jnp.concatenate([h.astype(jnp.bfloat16) for h in here], axis=1))
    return jnp.concatenate(rows, axis=0)


def pick_rows(messages, selected, count, normed, out_refs):
    room = out_refs[0].shape[0]
    slot = lax.broadcasted_iota(jnp.int32, (room, LANES), 0)
    lane = lax.broadcasted_iota(jnp.int32, (room, LANES), 1)
    picked = dot(selected, normed)
    for i, (m, out_ref) in enumerate(zip(messages, out_refs)):
        rows = picked[i * room : (i + 1) * room]
        empty = (slot >= count[m : m + 1]) & (lane == 0)
        first = jnp.where(empty, EMPTY, rows[:, :LANES])
        out_ref[:, :LANES] = first.astype(jnp.bfloat16)
        out_ref[:, LANES:] = rows[:, LANES:].astype(jnp.bfloat16)


def pack_first_kernel(blocks, emb_ref, id_ref, *refs):
    first_refs, refs = refs[: len(PACKED[0])], refs[len(PACKED[0]) :]
    normed, label_ref, rank_ref, count_ref, over_ref, raw, selected_ref, arrived = refs
    rows, width = normed.shape
    segments = rows // LANES
    copies = []
    for s in range(segments):
        part = pl.ds(s * LANES, LANES)
        copies.append(pltpu.make_async_copy(emb_ref.at[part], raw.at[part], arrived.at[s]))
        copies[-1].start()

    me = lax.axis_index("blk")
    ids = id_ref[...]
    q = lax.rem(me, GROUP)
    offset = lax.rem(me - ids + 2 * blocks, blocks)
    turn = lax.bitwise_and(q - offset + SPAN, SPAN - 1)
    label = jnp.where(ids >= 0, lax.bitwise_xor(turn, q), SPAN)
    member = [jnp.where(label == m, 1.0, 0.0) for m in range(SPAN)]
    stacked = jnp.concatenate(member, axis=0).astype(jnp.bfloat16)
    before = lax.broadcasted_iota(jnp.int32, (LANES, LANES), 0) < lax.broadcasted_iota(
        jnp.int32, (LANES, LANES), 1
    )
    before = jnp.where(before, 1.0, 0.0).astype(jnp.bfloat16)
    ones = jnp.ones((LANES, LANES), jnp.bfloat16)
    size = SPAN * segments
    r = lax.broadcasted_iota(jnp.int32, (size, size), 0)
    c = lax.broadcasted_iota(jnp.int32, (size, size), 1)
    earlier = (lax.div(r, segments) == lax.div(c, segments)) & (c < r)
    earlier = jnp.where(earlier, 1.0, 0.0).astype(jnp.bfloat16)
    r = lax.broadcasted_iota(jnp.int32, (SPAN, size), 0)
    c = lax.broadcasted_iota(jnp.int32, (SPAN, size), 1)
    same = jnp.where(r == lax.div(c, segments), 1.0, 0.0).astype(jnp.bfloat16)
    within = dot(stacked, before)
    start = dot(dot(earlier, stacked).astype(jnp.bfloat16), ones)
    count = dot(dot(same, stacked).astype(jnp.bfloat16), ones).astype(jnp.int32)
    place = (within + start).astype(jnp.int32)
    rank = jnp.zeros_like(ids)
    for m in range(SPAN):
        rank = jnp.where(label == m, place[m * segments : (m + 1) * segments], rank)
    label_ref[...] = label
    rank_ref[...] = rank
    count_ref[...] = count
    over_ref[...] = jnp.max(jnp.where(count > first_refs[0].shape[0], 1, 0), axis=0, keepdims=True)

    selected_ref[...] = selection(PACKED[0], label, rank, first_refs[0].shape[0])
    for s in range(segments):
        part = pl.ds(s * LANES, LANES)
        copies[s].wait()
        x = raw[part]
        scale = lax.rsqrt(jnp.sum(x * x, axis=1, keepdims=True) + 1e-06)
        normed[part] = (x * scale).astype(jnp.bfloat16)

    pick_rows(PACKED[0], selected_ref[...], count, normed[...], first_refs)


def pack_first(embeddings, ids, blocks, room):
    rows, width = embeddings.shape
    segments = rows // LANES
    vmem = pl.BlockSpec(memory_space=pltpu.VMEM)
    shapes = [jax.ShapeDtypeStruct((room, width), jnp.bfloat16)] * len(PACKED[0])
    shapes += [jax.ShapeDtypeStruct((rows, width), jnp.bfloat16)]
    shapes += [jax.ShapeDtypeStruct((segments, LANES), jnp.int32)] * 2
    shapes += [jax.ShapeDtypeStruct((SPAN, LANES), jnp.int32)]
    shapes += [jax.ShapeDtypeStruct((1, LANES), jnp.int32)]
    return pl.pallas_call(
        functools.partial(pack_first_kernel, blocks),
        out_shape=shapes,
        in_specs=[pl.BlockSpec(memory_space=pl.ANY), vmem],
        out_specs=[vmem] * len(shapes),
        scratch_shapes=[
            pltpu.VMEM((rows, width), jnp.float32),
            pltpu.VMEM((len(PACKED[0]) * room, rows), jnp.bfloat16),
            pltpu.SemaphoreType.DMA((segments,)),
        ],
        compiler_params=pltpu.CompilerParams(vmem_limit_bytes=PACK_VMEM),
        cost_estimate=pl.CostEstimate(
            flops=2 * GROUP * room * rows * width, bytes_accessed=rows * width * 4, transcendentals=rows
        ),
        name="pack_first",
    )(embeddings, ids)


def pack_more_kernel(messages, normed, label_ref, rank_ref, count_ref, *out_refs):
    label, rank, count = label_ref[...], rank_ref[...], count_ref[...]
    selected = selection(messages, label, rank, out_refs[0].shape[0])
    pick_rows(messages, selected, count, normed[...], out_refs)


def pack_more(messages, room, normed, label, rank, count):
    rows, width = normed.shape
    vmem = pl.BlockSpec(memory_space=pltpu.VMEM)
    return pl.pallas_call(
        functools.partial(pack_more_kernel, messages),
        out_shape=[jax.ShapeDtypeStruct((room, width), jnp.bfloat16)] * len(messages),
        in_specs=[vmem] * 4,
        out_specs=[vmem] * len(messages),
        compiler_params=pltpu.CompilerParams(vmem_limit_bytes=PACK_VMEM),
        cost_estimate=pl.CostEstimate(
            flops=2 * len(messages) * room * rows * width, bytes_accessed=rows * width * 4, transcendentals=0
        ),
        name=f"pack_{len(messages)}",
    )(normed, label, rank, count)


def same_place(count):
    i = lax.broadcasted_iota(jnp.int32, (count, count), 0)
    j = lax.broadcasted_iota(jnp.int32, (count, count), 1)
    return i == j


def stacked(refs):
    return jnp.concatenate([ref[...] for ref in refs], axis=0)


def join(old, new, before):
    count, width = new.shape
    diagonal = same_place(count)
    unused = jnp.where(new[:, :LANES].astype(jnp.float32)[:, :1] > 1.5, -4.0, 0.0)
    scores = jnp.where(diagonal, -1.0, dot_rows(new, new) + unused)
    best = jnp.max(scores, axis=0, keepdims=True)
    if old is None:
        return None, best
    i = lax.broadcasted_iota(jnp.int32, (16, width), 0)
    j = lax.broadcasted_iota(jnp.int32, (16, width), 1)
    first = jnp.where((i == 0) & (j == 0), 1.0, 0.0).astype(jnp.bfloat16)
    scores = dot_rows(jnp.concatenate([new, first], axis=0), old)
    markers, scores = scores[count : count + 1], scores[:count]
    best_old = jnp.maximum(before, jnp.max(scores + unused, axis=0, keepdims=True))
    best_new = jnp.max(scores + jnp.where(markers > 1.5, -4.0, 0.0), axis=1, keepdims=True)
    best_new = jnp.max(jnp.where(diagonal, best_new, -4.0), axis=0, keepdims=True)
    return best_old, jnp.maximum(best, best_new)


def score_first_kernel(*refs):
    new, (over_ref, best_ref, rows_ref, passed_ref) = refs[:-4], refs[-4:]
    rows_ref[...] = stacked(new)
    best_ref[...] = join(None, rows_ref[...], None)[1]
    passed_ref[...] = over_ref[...]


def score_step_kernel(old_ref, *refs):
    new, (before_ref, best_ref, rows_ref) = refs[:-3], refs[-3:]
    olds = old_ref.shape[0]
    rows_ref[:olds] = old_ref[...]
    rows_ref[olds:] = stacked(new)
    best_old, best_new = join(old_ref[...], rows_ref[olds:], before_ref[...])
    best_ref[...] = jnp.concatenate([best_old, best_new], axis=1)


def score_step(old, new, before):
    room, width = new[0].shape
    vmem = pl.BlockSpec(memory_space=pltpu.VMEM)
    rows = len(new) * room + (0 if old is None else old.shape[0])
    args = (*new, before) if old is None else (old, *new, before)
    shapes = [jax.ShapeDtypeStruct((1, rows), jnp.float32), jax.ShapeDtypeStruct((rows, width), jnp.bfloat16)]
    if old is None:
        shapes += [jax.ShapeDtypeStruct(before.shape, before.dtype)]
    return pl.pallas_call(
        score_first_kernel if old is None else score_step_kernel,
        out_shape=shapes,
        in_specs=[vmem] * len(args),
        out_specs=[vmem] * len(shapes),
        compiler_params=pltpu.CompilerParams(vmem_limit_bytes=SCORE_VMEM),
        cost_estimate=pl.CostEstimate(
            flops=4 * len(new) * room * rows * width, bytes_accessed=rows * width * 2, transcendentals=0
        ),
        name=f"score_{rows // room}",
    )(*args)


def score_last_kernel(blocks, room, old_ref, *refs):
    new, (before_ref, over_ref, other_ref, best_ref) = refs[:-4], refs[-4:]
    me = lax.axis_index("blk")
    flag = jnp.maximum(over_ref[...], other_ref[...]).astype(jnp.float32)
    padded = best_ref.shape[2]
    best_ref[...] = jnp.concatenate([flag[None]] * (padded // LANES), axis=2) + jnp.zeros_like(best_ref)
    bests = []
    for best in join(old_ref[...], stacked(new), before_ref[...]):
        bests += [best[:, i : i + room] for i in range(0, best.shape[1], room)]
    for m, best in zip(sum(STEPS, ()), bests):
        best_ref[blocks - 1 - partner(me, m, blocks, True), :, :room] = jnp.maximum(best, -1.0)


def score_last(old, new, before, over, other, blocks):
    room, width = new[0].shape
    padded = (pl.cdiv(room, LANES) if room % LANES else room // LANES + 1) * LANES
    vmem = pl.BlockSpec(memory_space=pltpu.VMEM)
    return pl.pallas_call(
        functools.partial(score_last_kernel, blocks, room),
        out_shape=jax.ShapeDtypeStruct((blocks, 1, padded), jnp.float32),
        in_specs=[vmem] * (len(new) + 4),
        out_specs=vmem,
        compiler_params=pltpu.CompilerParams(vmem_limit_bytes=SCORE_VMEM),
        name="score_last",
    )(old, *new, before, over, other)


def unpack_kernel(blocks, best_ref, label_ref, rank_ref, out_ref, over_ref):
    label, rank = label_ref[...], rank_ref[...]
    padded = best_ref.shape[2]
    me = lax.axis_index("blk")
    inner = lax.bitwise_and(rank, LANES - 1)
    result = jnp.full(label.shape, -1.0, jnp.float32)
    for m in range(SPAN):
        best = best_ref[blocks - 1 - partner(me, m, blocks, False)]
        for start in range(0, padded, LANES):
            table = jnp.broadcast_to(best[:, start : start + LANES], label.shape)
            value = jnp.take_along_axis(table, inner, axis=1)
            here = (label == m) & (rank >= start) & (rank < start + LANES)
            result = jnp.where(here, value, result)
    out_ref[...] = result
    flags = jnp.max(best_ref[:, :, padded - LANES :], axis=0)
    over_ref[...] = jnp.roll(flags, 1, axis=1).astype(jnp.int32)


def unpack(best, label, rank):
    vmem = pl.BlockSpec(memory_space=pltpu.VMEM)
    return pl.pallas_call(
        functools.partial(unpack_kernel, best.shape[0]),
        out_shape=[
            jax.ShapeDtypeStruct(label.shape, jnp.float32),
            jax.ShapeDtypeStruct((1, LANES), jnp.int32),
        ],
        in_specs=[vmem] * 3,
        out_specs=[vmem] * 2,
        compiler_params=pltpu.CompilerParams(vmem_limit_bytes=4 * 1024 * 1024),
        name="unpack",
    )(best, label, rank)


def by_home(embeddings, cluster_id, rooms):
    blocks = lax.axis_size("blk")
    room = rooms[0]
    ids = cluster_id.reshape(-1, LANES)
    *packed, normed, label, rank, count, over = pack_first(embeddings, ids, blocks, room)
    rows = {m: send(p, m) for m, p in zip(PACKED[0], packed)}
    for messages in PACKED[1:]:
        packed = pack_more(messages, room, normed, label, rank, count)
        rows |= {m: send(p, m) for m, p in zip(messages, packed)}
    best, old, over = score_step(None, [rows[m] for m in STEPS[0]], over)
    other = over
    for distance in range(1, lax.axis_size("parts")):
        other = jnp.maximum(other, shifted(over, "parts", distance))
    for step in STEPS[1:-1]:
        best, old = score_step(old, [rows[m] for m in step], best)
    best = score_last(old, [rows[m] for m in STEPS[-1]], best, over, other, blocks)
    backward = [list(reversed(range(blocks)))]
    returned = lax.all_to_all(best, "blk", 0, 0, axis_index_groups=backward, tiled=True)
    result, flag = unpack(returned, label, rank)

    def again():
        if len(rooms) == 1:
            return by_ring(embeddings, cluster_id)
        return by_home(embeddings, cluster_id, rooms[1:])

    return lax.switch(flag[0, 0], [lambda: result.reshape(-1), again])


def local(embeddings, cluster_id):
    return by_home(embeddings, cluster_id, ROOMS)


def solution(mesh):
    in_specs = (P(("parts", "blk"), None), P(("parts", "blk")))
    out_specs = P(("parts", "blk"))
    return jax.shard_map(local, mesh=mesh, in_specs=in_specs, out_specs=out_specs, check_vma=False)
```

```python
import functools

import jax
import jax.numpy as jnp
from jax import lax
from jax.experimental import pallas as pl
from jax.experimental.pallas import tpu as pltpu
from jax.sharding import PartitionSpec as P

SPAN = 8
HOME = 4
GROUP = 4
ROOMS = (160, 256)
LANES = 128
EMPTY = 2.0
PACK_VMEM = 24 * 1024 * 1024
SCORE_VMEM = 20 * 1024 * 1024


def shifted(block, axis, distance):
    if distance == 0:
        return block
    size = lax.axis_size(axis)
    route = [(i, (i + distance) % size) for i in range(size)]
    return lax.ppermute(block, axis, route)


def block_max(left, left_id, right, right_id, same_block):
    scores = lax.dot_general(
        left, right, (((1,), (1,)), ((), ())), preferred_element_type=jnp.float32
    )
    match = (left_id[:, None] == right_id[None, :]) & (left_id[:, None] >= 0)
    if same_block:
        count = left.shape[0]
        match = match & (jnp.arange(count)[:, None] != jnp.arange(count)[None, :])
    masked = jnp.where(match, scores, jnp.float32(-1.0))
    return (jnp.max(masked, axis=1), jnp.max(masked, axis=0))


def by_ring(embeddings, cluster_id):
    scale = lax.rsqrt(jnp.sum(embeddings * embeddings, axis=1, keepdims=True) + 1e-06)
    normed = (embeddings * scale).astype(jnp.bfloat16)
    best, unused_cols = block_max(normed, cluster_id, normed, cluster_id, True)
    visitor = (normed, cluster_id)
    for offset in range(1, SPAN):
        visitor = (shifted(visitor[0], "blk", 1), shifted(visitor[1], "blk", 1))
        row_best, col_best = block_max(normed, cluster_id, visitor[0], visitor[1], False)
        returned = shifted(col_best, "blk", -offset)
        best = jnp.maximum(best, jnp.maximum(row_best, returned))
    return best


OWN = GROUP
PACKED = ((0, 6), (7, 2, 5, OWN), (1, 3))
STEPS = ((OWN, 0, 6), (7, 2, 5), (1, 3))


def target(block, m, blocks):
    q = block % GROUP
    r = q ^ (m % GROUP)
    step = 0 if m >= GROUP else GROUP if r <= q else -GROUP
    return (block - q + r + step) % blocks


def partner(me, m, blocks, sender):
    q = lax.rem(me, GROUP)
    r = lax.bitwise_xor(q, m % GROUP)
    if m >= GROUP:
        return me - q + r
    back = (q <= r) if sender else (r > q)
    step = jnp.where(back, blocks - GROUP, GROUP)
    return lax.rem(me - q + r + step, blocks)


def send(rows, m):
    if m == OWN:
        return rows
    blocks = lax.axis_size("blk")
    return lax.ppermute(rows, "blk", [(i, target(i, m, blocks)) for i in range(blocks)])


def dot(a, b):
    return jnp.dot(a, b, preferred_element_type=jnp.float32)


def dot_rows(a, b):
    return lax.dot_general(a, b, (((1,), (1,)), ((), ())), preferred_element_type=jnp.float32)


def selection(messages, label, rank, room):
    slot = lax.broadcasted_iota(jnp.int32, (room, LANES), 0)
    rows = []
    for m in messages:
        key = jnp.where(label == m, rank, -1)
        here = [jnp.where(slot == key[s : s + 1], 1.0, 0.0) for s in range(label.shape[0])]
        rows.append(jnp.concatenate([h.astype(jnp.bfloat16) for h in here], axis=1))
    return jnp.concatenate(rows, axis=0)


def pick_rows(messages, selected, count, normed, out_refs):
    room = out_refs[0].shape[0]
    slot = lax.broadcasted_iota(jnp.int32, (room, LANES), 0)
    lane = lax.broadcasted_iota(jnp.int32, (room, LANES), 1)
    picked = dot(selected, normed)
    for i, (m, out_ref) in enumerate(zip(messages, out_refs)):
        rows = picked[i * room : (i + 1) * room]
        empty = (slot >= count[m : m + 1]) & (lane == 0)
        first = jnp.where(empty, EMPTY, rows[:, :LANES])
        out_ref[:, :LANES] = first.astype(jnp.bfloat16)
        out_ref[:, LANES:] = rows[:, LANES:].astype(jnp.bfloat16)


def pack_first_kernel(blocks, emb_ref, id_ref, *refs):
    first_refs, refs = refs[: len(PACKED[0])], refs[len(PACKED[0]) :]
    normed, label_ref, rank_ref, count_ref, over_ref, raw, selected_ref, arrived = refs
    rows, width = normed.shape
    segments = rows // LANES
    copies = []
    for s in range(segments):
        part = pl.ds(s * LANES, LANES)
        copies.append(pltpu.make_async_copy(emb_ref.at[part], raw.at[part], arrived.at[s]))
        copies[-1].start()

    me = lax.axis_index("blk")
    ids = id_ref[...]
    q = lax.rem(me, GROUP)
    offset = lax.rem(me - ids + 2 * blocks, blocks)
    turn = lax.bitwise_and(q - offset + SPAN, SPAN - 1)
    label = jnp.where(ids >= 0, lax.bitwise_xor(turn, q), SPAN)
    member = [jnp.where(label == m, 1.0, 0.0) for m in range(SPAN)]
    stacked = jnp.concatenate(member, axis=0).astype(jnp.bfloat16)
    before = lax.broadcasted_iota(jnp.int32, (LANES, LANES), 0) < lax.broadcasted_iota(
        jnp.int32, (LANES, LANES), 1
    )
    before = jnp.where(before, 1.0, 0.0).astype(jnp.bfloat16)
    ones = jnp.ones((LANES, LANES), jnp.bfloat16)
    size = SPAN * segments
    r = lax.broadcasted_iota(jnp.int32, (size, size), 0)
    c = lax.broadcasted_iota(jnp.int32, (size, size), 1)
    earlier = (lax.div(r, segments) == lax.div(c, segments)) & (c < r)
    earlier = jnp.where(earlier, 1.0, 0.0).astype(jnp.bfloat16)
    r = lax.broadcasted_iota(jnp.int32, (SPAN, size), 0)
    c = lax.broadcasted_iota(jnp.int32, (SPAN, size), 1)
    same = jnp.where(r == lax.div(c, segments), 1.0, 0.0).astype(jnp.bfloat16)
    within = dot(stacked, before)
    start = dot(dot(earlier, stacked).astype(jnp.bfloat16), ones)
    count = dot(dot(same, stacked).astype(jnp.bfloat16), ones).astype(jnp.int32)
    place = (within + start).astype(jnp.int32)
    rank = jnp.zeros_like(ids)
    for m in range(SPAN):
        rank = jnp.where(label == m, place[m * segments : (m + 1) * segments], rank)
    label_ref[...] = label
    rank_ref[...] = rank
    count_ref[...] = count
    over_ref[...] = jnp.max(jnp.where(count > first_refs[0].shape[0], 1, 0), axis=0, keepdims=True)

    selected_ref[...] = selection(PACKED[0], label, rank, first_refs[0].shape[0])
    for s in range(segments):
        part = pl.ds(s * LANES, LANES)
        copies[s].wait()
        x = raw[part]
        scale = lax.rsqrt(jnp.sum(x * x, axis=1, keepdims=True) + 1e-06)
        normed[part] = (x * scale).astype(jnp.bfloat16)

    pick_rows(PACKED[0], selected_ref[...], count, normed[...], first_refs)


def pack_first(embeddings, ids, blocks, room):
    rows, width = embeddings.shape
    segments = rows // LANES
    vmem = pl.BlockSpec(memory_space=pltpu.VMEM)
    shapes = [jax.ShapeDtypeStruct((room, width), jnp.bfloat16)] * len(PACKED[0])
    shapes += [jax.ShapeDtypeStruct((rows, width), jnp.bfloat16)]
    shapes += [jax.ShapeDtypeStruct((segments, LANES), jnp.int32)] * 2
    shapes += [jax.ShapeDtypeStruct((SPAN, LANES), jnp.int32)]
    shapes += [jax.ShapeDtypeStruct((1, LANES), jnp.int32)]
    return pl.pallas_call(
        functools.partial(pack_first_kernel, blocks),
        out_shape=shapes,
        in_specs=[pl.BlockSpec(memory_space=pl.ANY), vmem],
        out_specs=[vmem] * len(shapes),
        scratch_shapes=[
            pltpu.VMEM((rows, width), jnp.float32),
            pltpu.VMEM((len(PACKED[0]) * room, rows), jnp.bfloat16),
            pltpu.SemaphoreType.DMA((segments,)),
        ],
        compiler_params=pltpu.CompilerParams(vmem_limit_bytes=PACK_VMEM),
        cost_estimate=pl.CostEstimate(
            flops=2 * GROUP * room * rows * width, bytes_accessed=rows * width * 4, transcendentals=rows
        ),
        name="pack_first",
    )(embeddings, ids)


def pack_more_kernel(messages, normed, label_ref, rank_ref, count_ref, *out_refs):
    label, rank, count = label_ref[...], rank_ref[...], count_ref[...]
    selected = selection(messages, label, rank, out_refs[0].shape[0])
    pick_rows(messages, selected, count, normed[...], out_refs)


def pack_more(messages, room, normed, label, rank, count):
    rows, width = normed.shape
    vmem = pl.BlockSpec(memory_space=pltpu.VMEM)
    return pl.pallas_call(
        functools.partial(pack_more_kernel, messages),
        out_shape=[jax.ShapeDtypeStruct((room, width), jnp.bfloat16)] * len(messages),
        in_specs=[vmem] * 4,
        out_specs=[vmem] * len(messages),
        compiler_params=pltpu.CompilerParams(vmem_limit_bytes=PACK_VMEM),
        cost_estimate=pl.CostEstimate(
            flops=2 * len(messages) * room * rows * width, bytes_accessed=rows * width * 4, transcendentals=0
        ),
        name=f"pack_{len(messages)}",
    )(normed, label, rank, count)


def same_place(count):
    i = lax.broadcasted_iota(jnp.int32, (count, count), 0)
    j = lax.broadcasted_iota(jnp.int32, (count, count), 1)
    return i == j


def stacked(refs):
    return jnp.concatenate([ref[...] for ref in refs], axis=0)


def join(old, new, before):
    count, width = new.shape
    diagonal = same_place(count)
    unused = jnp.where(new[:, :LANES].astype(jnp.float32)[:, :1] > 1.5, -4.0, 0.0)
    scores = jnp.where(diagonal, -1.0, dot_rows(new, new) + unused)
    best = jnp.max(scores, axis=0, keepdims=True)
    if old is None:
        return None, best
    i = lax.broadcasted_iota(jnp.int32, (16, width), 0)
    j = lax.broadcasted_iota(jnp.int32, (16, width), 1)
    first = jnp.where((i == 0) & (j == 0), 1.0, 0.0).astype(jnp.bfloat16)
    scores = dot_rows(jnp.concatenate([new, first], axis=0), old)
    markers, scores = scores[count : count + 1], scores[:count]
    best_old = jnp.maximum(before, jnp.max(scores + unused, axis=0, keepdims=True))
    best_new = jnp.max(scores + jnp.where(markers > 1.5, -4.0, 0.0), axis=1, keepdims=True)
    best_new = jnp.max(jnp.where(diagonal, best_new, -4.0), axis=0, keepdims=True)
    return best_old, jnp.maximum(best, best_new)


def score_first_kernel(*refs):
    new, (over_ref, best_ref, rows_ref, passed_ref) = refs[:-4], refs[-4:]
    rows_ref[...] = stacked(new)
    best_ref[...] = join(None, rows_ref[...], None)[1]
    passed_ref[...] = over_ref[...]


def score_step_kernel(old_ref, *refs):
    new, (before_ref, best_ref, rows_ref) = refs[:-3], refs[-3:]
    olds = old_ref.shape[0]
    rows_ref[:olds] = old_ref[...]
    rows_ref[olds:] = stacked(new)
    best_old, best_new = join(old_ref[...], rows_ref[olds:], before_ref[...])
    best_ref[...] = jnp.concatenate([best_old, best_new], axis=1)


def score_step(old, new, before):
    room, width = new[0].shape
    vmem = pl.BlockSpec(memory_space=pltpu.VMEM)
    rows = len(new) * room + (0 if old is None else old.shape[0])
    args = (*new, before) if old is None else (old, *new, before)
    shapes = [jax.ShapeDtypeStruct((1, rows), jnp.float32), jax.ShapeDtypeStruct((rows, width), jnp.bfloat16)]
    if old is None:
        shapes += [jax.ShapeDtypeStruct(before.shape, before.dtype)]
    return pl.pallas_call(
        score_first_kernel if old is None else score_step_kernel,
        out_shape=shapes,
        in_specs=[vmem] * len(args),
        out_specs=[vmem] * len(shapes),
        compiler_params=pltpu.CompilerParams(vmem_limit_bytes=SCORE_VMEM),
        cost_estimate=pl.CostEstimate(
            flops=4 * len(new) * room * rows * width, bytes_accessed=rows * width * 2, transcendentals=0
        ),
        name=f"score_{rows // room}",
    )(*args)


def score_last_kernel(blocks, room, old_ref, *refs):
    new, (before_ref, over_ref, other_ref, best_ref) = refs[:-4], refs[-4:]
    me = lax.axis_index("blk")
    flag = jnp.maximum(over_ref[...], other_ref[...]).astype(jnp.float32)
    padded = best_ref.shape[2]
    best_ref[...] = jnp.concatenate([flag[None]] * (padded // LANES), axis=2) + jnp.zeros_like(best_ref)
    bests = []
    for best in join(old_ref[...], stacked(new), before_ref[...]):
        bests += [best[:, i : i + room] for i in range(0, best.shape[1], room)]
    for m, best in zip(sum(STEPS, ()), bests):
        best_ref[blocks - 1 - partner(me, m, blocks, True), :, :room] = jnp.maximum(best, -1.0)


def score_last(old, new, before, over, other, blocks):
    room, width = new[0].shape
    padded = (pl.cdiv(room, LANES) if room % LANES else room // LANES + 1) * LANES
    vmem = pl.BlockSpec(memory_space=pltpu.VMEM)
    return pl.pallas_call(
        functools.partial(score_last_kernel, blocks, room),
        out_shape=jax.ShapeDtypeStruct((blocks, 1, padded), jnp.float32),
        in_specs=[vmem] * (len(new) + 4),
        out_specs=vmem,
        compiler_params=pltpu.CompilerParams(vmem_limit_bytes=SCORE_VMEM),
        name="score_last",
    )(old, *new, before, over, other)


def unpack_kernel(blocks, best_ref, label_ref, rank_ref, out_ref, over_ref):
    label, rank = label_ref[...], rank_ref[...]
    padded = best_ref.shape[2]
    me = lax.axis_index("blk")
    inner = lax.bitwise_and(rank, LANES - 1)
    result = jnp.full(label.shape, -1.0, jnp.float32)
    for m in range(SPAN):
        best = best_ref[blocks - 1 - partner(me, m, blocks, False)]
        for start in range(0, padded, LANES):
            table = jnp.broadcast_to(best[:, start : start + LANES], label.shape)
            value = jnp.take_along_axis(table, inner, axis=1)
            here = (label == m) & (rank >= start) & (rank < start + LANES)
            result = jnp.where(here, value, result)
    out_ref[...] = result
    flags = jnp.max(best_ref[:, :, padded - LANES :], axis=0)
    over_ref[...] = jnp.roll(flags, 1, axis=1).astype(jnp.int32)


def unpack(best, label, rank):
    vmem = pl.BlockSpec(memory_space=pltpu.VMEM)
    return pl.pallas_call(
        functools.partial(unpack_kernel, best.shape[0]),
        out_shape=[
            jax.ShapeDtypeStruct(label.shape, jnp.float32),
            jax.ShapeDtypeStruct((1, LANES), jnp.int32),
        ],
        in_specs=[vmem] * 3,
        out_specs=[vmem] * 2,
        compiler_params=pltpu.CompilerParams(vmem_limit_bytes=4 * 1024 * 1024),
        name="unpack",
    )(best, label, rank)


def by_home(embeddings, cluster_id, rooms):
    blocks = lax.axis_size("blk")
    room = rooms[0]
    ids = cluster_id.reshape(-1, LANES)
    *packed, normed, label, rank, count, over = pack_first(embeddings, ids, blocks, room)
    rows = {m: send(p, m) for m, p in zip(PACKED[0], packed)}
    for messages in PACKED[1:]:
        packed = pack_more(messages, room, normed, label, rank, count)
        rows |= {m: send(p, m) for m, p in zip(messages, packed)}
    best, old, over = score_step(None, [rows[m] for m in STEPS[0]], over)
    other = over
    for distance in range(1, lax.axis_size("parts")):
        other = jnp.maximum(other, shifted(over, "parts", distance))
    for step in STEPS[1:-1]:
        best, old = score_step(old, [rows[m] for m in step], best)
    best = score_last(old, [rows[m] for m in STEPS[-1]], best, over, other, blocks)
    backward = [list(reversed(range(blocks)))]
    returned = lax.all_to_all(best, "blk", 0, 0, axis_index_groups=backward, tiled=True)
    result, flag = unpack(returned, label, rank)

    def again():
        if len(rooms) == 1:
            return by_ring(embeddings, cluster_id)
        return by_home(embeddings, cluster_id, rooms[1:])

    return lax.switch(flag[0, 0], [lambda: result.reshape(-1), again])


def local(embeddings, cluster_id):
    return by_home(embeddings, cluster_id, ROOMS)


def solution(mesh):
    in_specs = (P(("parts", "blk"), None), P(("parts", "blk")))
    out_specs = P(("parts", "blk"))
    return jax.shard_map(local, mesh=mesh, in_specs=in_specs, out_specs=out_specs, check_vma=False)
```

```python
import functools

import jax
import jax.numpy as jnp
from jax import lax
from jax.experimental import pallas as pl
from jax.experimental.pallas import tpu as pltpu
from jax.sharding import PartitionSpec as P

SPAN = 8
HOME = 4
GROUP = 4
ROOMS = (160, 256)
LANES = 128
EMPTY = 2.0
PACK_VMEM = 24 * 1024 * 1024
SCORE_VMEM = 20 * 1024 * 1024


def shifted(block, axis, distance):
    if distance == 0:
        return block
    size = lax.axis_size(axis)
    route = [(i, (i + distance) % size) for i in range(size)]
    return lax.ppermute(block, axis, route)


def block_max(left, left_id, right, right_id, same_block):
    scores = lax.dot_general(
        left, right, (((1,), (1,)), ((), ())), preferred_element_type=jnp.float32
    )
    match = (left_id[:, None] == right_id[None, :]) & (left_id[:, None] >= 0)
    if same_block:
        count = left.shape[0]
        match = match & (jnp.arange(count)[:, None] != jnp.arange(count)[None, :])
    masked = jnp.where(match, scores, jnp.float32(-1.0))
    return (jnp.max(masked, axis=1), jnp.max(masked, axis=0))


def by_ring(embeddings, cluster_id):
    scale = lax.rsqrt(jnp.sum(embeddings * embeddings, axis=1, keepdims=True) + 1e-06)
    normed = (embeddings * scale).astype(jnp.bfloat16)
    best, unused_cols = block_max(normed, cluster_id, normed, cluster_id, True)
    visitor = (normed, cluster_id)
    for offset in range(1, SPAN):
        visitor = (shifted(visitor[0], "blk", 1), shifted(visitor[1], "blk", 1))
        row_best, col_best = block_max(normed, cluster_id, visitor[0], visitor[1], False)
        returned = shifted(col_best, "blk", -offset)
        best = jnp.maximum(best, jnp.maximum(row_best, returned))
    return best


OWN = GROUP
PACKED = ((6, 0), (7, 2, 5, OWN), (3, 1))
STEPS = ((OWN, 6, 0), (7, 2, 5), (3, 1))


def target(block, m, blocks):
    q = block % GROUP
    r = q ^ (m % GROUP)
    step = 0 if m >= GROUP else GROUP if r <= q else -GROUP
    return (block - q + r + step) % blocks


def partner(me, m, blocks, sender):
    q = lax.rem(me, GROUP)
    r = lax.bitwise_xor(q, m % GROUP)
    if m >= GROUP:
        return me - q + r
    back = (q <= r) if sender else (r > q)
    step = jnp.where(back, blocks - GROUP, GROUP)
    return lax.rem(me - q + r + step, blocks)


def send(rows, m):
    if m == OWN:
        return rows
    blocks = lax.axis_size("blk")
    return lax.ppermute(rows, "blk", [(i, target(i, m, blocks)) for i in range(blocks)])


def dot(a, b):
    return jnp.dot(a, b, preferred_element_type=jnp.float32)


def dot_rows(a, b):
    return lax.dot_general(a, b, (((1,), (1,)), ((), ())), preferred_element_type=jnp.float32)


def selection(messages, label, rank, room):
    slot = lax.broadcasted_iota(jnp.int32, (room, LANES), 0)
    rows = []
    for m in messages:
        key = jnp.where(label == m, rank, -1)
        here = [jnp.where(slot == key[s : s + 1], 1.0, 0.0) for s in range(label.shape[0])]
        rows.append(jnp.concatenate([h.astype(jnp.bfloat16) for h in here], axis=1))
    return jnp.concatenate(rows, axis=0)


def pick_rows(messages, selected, count, normed, out_refs):
    room = out_refs[0].shape[0]
    slot = lax.broadcasted_iota(jnp.int32, (room, LANES), 0)
    lane = lax.broadcasted_iota(jnp.int32, (room, LANES), 1)
    picked = dot(selected, normed)
    for i, (m, out_ref) in enumerate(zip(messages, out_refs)):
        rows = picked[i * room : (i + 1) * room]
        empty = (slot >= count[m : m + 1]) & (lane == 0)
        first = jnp.where(empty, EMPTY, rows[:, :LANES])
        out_ref[:, :LANES] = first.astype(jnp.bfloat16)
        out_ref[:, LANES:] = rows[:, LANES:].astype(jnp.bfloat16)


def pack_first_kernel(blocks, emb_ref, id_ref, *refs):
    first_refs, refs = refs[: len(PACKED[0])], refs[len(PACKED[0]) :]
    normed, label_ref, rank_ref, count_ref, over_ref, raw, selected_ref, arrived = refs
    rows, width = normed.shape
    segments = rows // LANES
    copies = []
    for s in range(segments):
        part = pl.ds(s * LANES, LANES)
        copies.append(pltpu.make_async_copy(emb_ref.at[part], raw.at[part], arrived.at[s]))
        copies[-1].start()

    me = lax.axis_index("blk")
    ids = id_ref[...]
    q = lax.rem(me, GROUP)
    offset = lax.rem(me - ids + 2 * blocks, blocks)
    turn = lax.bitwise_and(q - offset + SPAN, SPAN - 1)
    label = jnp.where(ids >= 0, lax.bitwise_xor(turn, q), SPAN)
    member = [jnp.where(label == m, 1.0, 0.0) for m in range(SPAN)]
    stacked = jnp.concatenate(member, axis=0).astype(jnp.bfloat16)
    before = lax.broadcasted_iota(jnp.int32, (LANES, LANES), 0) < lax.broadcasted_iota(
        jnp.int32, (LANES, LANES), 1
    )
    before = jnp.where(before, 1.0, 0.0).astype(jnp.bfloat16)
    ones = jnp.ones((LANES, LANES), jnp.bfloat16)
    size = SPAN * segments
    r = lax.broadcasted_iota(jnp.int32, (size, size), 0)
    c = lax.broadcasted_iota(jnp.int32, (size, size), 1)
    earlier = (lax.div(r, segments) == lax.div(c, segments)) & (c < r)
    earlier = jnp.where(earlier, 1.0, 0.0).astype(jnp.bfloat16)
    r = lax.broadcasted_iota(jnp.int32, (SPAN, size), 0)
    c = lax.broadcasted_iota(jnp.int32, (SPAN, size), 1)
    same = jnp.where(r == lax.div(c, segments), 1.0, 0.0).astype(jnp.bfloat16)
    within = dot(stacked, before)
    start = dot(dot(earlier, stacked).astype(jnp.bfloat16), ones)
    count = dot(dot(same, stacked).astype(jnp.bfloat16), ones).astype(jnp.int32)
    place = (within + start).astype(jnp.int32)
    rank = jnp.zeros_like(ids)
    for m in range(SPAN):
        rank = jnp.where(label == m, place[m * segments : (m + 1) * segments], rank)
    label_ref[...] = label
    rank_ref[...] = rank
    count_ref[...] = count
    over_ref[...] = jnp.max(jnp.where(count > first_refs[0].shape[0], 1, 0), axis=0, keepdims=True)

    selected_ref[...] = selection(PACKED[0], label, rank, first_refs[0].shape[0])
    for s in range(segments):
        part = pl.ds(s * LANES, LANES)
        copies[s].wait()
        x = raw[part]
        scale = lax.rsqrt(jnp.sum(x * x, axis=1, keepdims=True) + 1e-06)
        normed[part] = (x * scale).astype(jnp.bfloat16)

    pick_rows(PACKED[0], selected_ref[...], count, normed[...], first_refs)


def pack_first(embeddings, ids, blocks, room):
    rows, width = embeddings.shape
    segments = rows // LANES
    vmem = pl.BlockSpec(memory_space=pltpu.VMEM)
    shapes = [jax.ShapeDtypeStruct((room, width), jnp.bfloat16)] * len(PACKED[0])
    shapes += [jax.ShapeDtypeStruct((rows, width), jnp.bfloat16)]
    shapes += [jax.ShapeDtypeStruct((segments, LANES), jnp.int32)] * 2
    shapes += [jax.ShapeDtypeStruct((SPAN, LANES), jnp.int32)]
    shapes += [jax.ShapeDtypeStruct((1, LANES), jnp.int32)]
    return pl.pallas_call(
        functools.partial(pack_first_kernel, blocks),
        out_shape=shapes,
        in_specs=[pl.BlockSpec(memory_space=pl.ANY), vmem],
        out_specs=[vmem] * len(shapes),
        scratch_shapes=[
            pltpu.VMEM((rows, width), jnp.float32),
            pltpu.VMEM((len(PACKED[0]) * room, rows), jnp.bfloat16),
            pltpu.SemaphoreType.DMA((segments,)),
        ],
        compiler_params=pltpu.CompilerParams(vmem_limit_bytes=PACK_VMEM),
        cost_estimate=pl.CostEstimate(
            flops=2 * GROUP * room * rows * width, bytes_accessed=rows * width * 4, transcendentals=rows
        ),
        name="pack_first",
    )(embeddings, ids)


def pack_more_kernel(messages, normed, label_ref, rank_ref, count_ref, *out_refs):
    label, rank, count = label_ref[...], rank_ref[...], count_ref[...]
    selected = selection(messages, label, rank, out_refs[0].shape[0])
    pick_rows(messages, selected, count, normed[...], out_refs)


def pack_more(messages, room, normed, label, rank, count):
    rows, width = normed.shape
    vmem = pl.BlockSpec(memory_space=pltpu.VMEM)
    return pl.pallas_call(
        functools.partial(pack_more_kernel, messages),
        out_shape=[jax.ShapeDtypeStruct((room, width), jnp.bfloat16)] * len(messages),
        in_specs=[vmem] * 4,
        out_specs=[vmem] * len(messages),
        compiler_params=pltpu.CompilerParams(vmem_limit_bytes=PACK_VMEM),
        cost_estimate=pl.CostEstimate(
            flops=2 * len(messages) * room * rows * width, bytes_accessed=rows * width * 4, transcendentals=0
        ),
        name=f"pack_{len(messages)}",
    )(normed, label, rank, count)


def same_place(count):
    i = lax.broadcasted_iota(jnp.int32, (count, count), 0)
    j = lax.broadcasted_iota(jnp.int32, (count, count), 1)
    return i == j


def stacked(refs):
    return jnp.concatenate([ref[...] for ref in refs], axis=0)


def join(old, new, before):
    count, width = new.shape
    diagonal = same_place(count)
    unused = jnp.where(new[:, :LANES].astype(jnp.float32)[:, :1] > 1.5, -4.0, 0.0)
    scores = jnp.where(diagonal, -1.0, dot_rows(new, new) + unused)
    best = jnp.max(scores, axis=0, keepdims=True)
    if old is None:
        return None, best
    i = lax.broadcasted_iota(jnp.int32, (16, width), 0)
    j = lax.broadcasted_iota(jnp.int32, (16, width), 1)
    first = jnp.where((i == 0) & (j == 0), 1.0, 0.0).astype(jnp.bfloat16)
    scores = dot_rows(jnp.concatenate([new, first], axis=0), old)
    markers, scores = scores[count : count + 1], scores[:count]
    best_old = jnp.maximum(before, jnp.max(scores + unused, axis=0, keepdims=True))
    best_new = jnp.max(scores + jnp.where(markers > 1.5, -4.0, 0.0), axis=1, keepdims=True)
    best_new = jnp.max(jnp.where(diagonal, best_new, -4.0), axis=0, keepdims=True)
    return best_old, jnp.maximum(best, best_new)


def score_first_kernel(*refs):
    new, (over_ref, best_ref, rows_ref, passed_ref) = refs[:-4], refs[-4:]
    rows_ref[...] = stacked(new)
    best_ref[...] = join(None, rows_ref[...], None)[1]
    passed_ref[...] = over_ref[...]


def score_step_kernel(old_ref, *refs):
    new, (before_ref, best_ref, rows_ref) = refs[:-3], refs[-3:]
    olds = old_ref.shape[0]
    rows_ref[:olds] = old_ref[...]
    rows_ref[olds:] = stacked(new)
    best_old, best_new = join(old_ref[...], rows_ref[olds:], before_ref[...])
    best_ref[...] = jnp.concatenate([best_old, best_new], axis=1)


def score_step(old, new, before):
    room, width = new[0].shape
    vmem = pl.BlockSpec(memory_space=pltpu.VMEM)
    rows = len(new) * room + (0 if old is None else old.shape[0])
    args = (*new, before) if old is None else (old, *new, before)
    shapes = [jax.ShapeDtypeStruct((1, rows), jnp.float32), jax.ShapeDtypeStruct((rows, width), jnp.bfloat16)]
    if old is None:
        shapes += [jax.ShapeDtypeStruct(before.shape, before.dtype)]
    return pl.pallas_call(
        score_first_kernel if old is None else score_step_kernel,
        out_shape=shapes,
        in_specs=[vmem] * len(args),
        out_specs=[vmem] * len(shapes),
        compiler_params=pltpu.CompilerParams(vmem_limit_bytes=SCORE_VMEM),
        cost_estimate=pl.CostEstimate(
            flops=4 * len(new) * room * rows * width, bytes_accessed=rows * width * 2, transcendentals=0
        ),
        name=f"score_{rows // room}",
    )(*args)


def score_last_kernel(blocks, room, old_ref, *refs):
    new, (before_ref, over_ref, other_ref, best_ref) = refs[:-4], refs[-4:]
    me = lax.axis_index("blk")
    flag = jnp.maximum(over_ref[...], other_ref[...]).astype(jnp.float32)
    padded = best_ref.shape[2]
    best_ref[...] = jnp.concatenate([flag[None]] * (padded // LANES), axis=2) + jnp.zeros_like(best_ref)
    bests = []
    for best in join(old_ref[...], stacked(new), before_ref[...]):
        bests += [best[:, i : i + room] for i in range(0, best.shape[1], room)]
    for m, best in zip(sum(STEPS, ()), bests):
        best_ref[blocks - 1 - partner(me, m, blocks, True), :, :room] = jnp.maximum(best, -1.0)


def score_last(old, new, before, over, other, blocks):
    room, width = new[0].shape
    padded = (pl.cdiv(room, LANES) if room % LANES else room // LANES + 1) * LANES
    vmem = pl.BlockSpec(memory_space=pltpu.VMEM)
    return pl.pallas_call(
        functools.partial(score_last_kernel, blocks, room),
        out_shape=jax.ShapeDtypeStruct((blocks, 1, padded), jnp.float32),
        in_specs=[vmem] * (len(new) + 4),
        out_specs=vmem,
        compiler_params=pltpu.CompilerParams(vmem_limit_bytes=SCORE_VMEM),
        name="score_last",
    )(old, *new, before, over, other)


def unpack_kernel(blocks, best_ref, label_ref, rank_ref, out_ref, over_ref):
    label, rank = label_ref[...], rank_ref[...]
    padded = best_ref.shape[2]
    me = lax.axis_index("blk")
    inner = lax.bitwise_and(rank, LANES - 1)
    result = jnp.full(label.shape, -1.0, jnp.float32)
    for m in range(SPAN):
        best = best_ref[blocks - 1 - partner(me, m, blocks, False)]
        for start in range(0, padded, LANES):
            table = jnp.broadcast_to(best[:, start : start + LANES], label.shape)
            value = jnp.take_along_axis(table, inner, axis=1)
            here = (label == m) & (rank >= start) & (rank < start + LANES)
            result = jnp.where(here, value, result)
    out_ref[...] = result
    flags = jnp.max(best_ref[:, :, padded - LANES :], axis=0)
    over_ref[...] = jnp.roll(flags, 1, axis=1).astype(jnp.int32)


def unpack(best, label, rank):
    vmem = pl.BlockSpec(memory_space=pltpu.VMEM)
    return pl.pallas_call(
        functools.partial(unpack_kernel, best.shape[0]),
        out_shape=[
            jax.ShapeDtypeStruct(label.shape, jnp.float32),
            jax.ShapeDtypeStruct((1, LANES), jnp.int32),
        ],
        in_specs=[vmem] * 3,
        out_specs=[vmem] * 2,
        compiler_params=pltpu.CompilerParams(vmem_limit_bytes=4 * 1024 * 1024),
        name="unpack",
    )(best, label, rank)


def by_home(embeddings, cluster_id, rooms):
    blocks = lax.axis_size("blk")
    room = rooms[0]
    ids = cluster_id.reshape(-1, LANES)
    *packed, normed, label, rank, count, over = pack_first(embeddings, ids, blocks, room)
    rows = {m: send(p, m) for m, p in zip(PACKED[0], packed)}
    for messages in PACKED[1:]:
        packed = pack_more(messages, room, normed, label, rank, count)
        rows |= {m: send(p, m) for m, p in zip(messages, packed)}
    best, old, over = score_step(None, [rows[m] for m in STEPS[0]], over)
    other = over
    for distance in range(1, lax.axis_size("parts")):
        other = jnp.maximum(other, shifted(over, "parts", distance))
    for step in STEPS[1:-1]:
        best, old = score_step(old, [rows[m] for m in step], best)
    best = score_last(old, [rows[m] for m in STEPS[-1]], best, over, other, blocks)
    backward = [list(reversed(range(blocks)))]
    returned = lax.all_to_all(best, "blk", 0, 0, axis_index_groups=backward, tiled=True)
    result, flag = unpack(returned, label, rank)

    def again():
        if len(rooms) == 1:
            return by_ring(embeddings, cluster_id)
        return by_home(embeddings, cluster_id, rooms[1:])

    return lax.switch(flag[0, 0], [lambda: result.reshape(-1), again])


def local(embeddings, cluster_id):
    return by_home(embeddings, cluster_id, ROOMS)


def solution(mesh):
    in_specs = (P(("parts", "blk"), None), P(("parts", "blk")))
    out_specs = P(("parts", "blk"))
    return jax.shard_map(local, mesh=mesh, in_specs=in_specs, out_specs=out_specs, check_vma=False)
```

```python
import functools

import jax
import jax.numpy as jnp
from jax import lax
from jax.experimental import pallas as pl
from jax.experimental.pallas import tpu as pltpu
from jax.sharding import PartitionSpec as P

SPAN = 8
HOME = 4
GROUP = 4
ROOMS = (160, 256)
LANES = 128
EMPTY = 2.0
PACK_VMEM = 24 * 1024 * 1024
SCORE_VMEM = 20 * 1024 * 1024


def shifted(block, axis, distance):
    if distance == 0:
        return block
    size = lax.axis_size(axis)
    route = [(i, (i + distance) % size) for i in range(size)]
    return lax.ppermute(block, axis, route)


def block_max(left, left_id, right, right_id, same_block):
    scores = lax.dot_general(
        left, right, (((1,), (1,)), ((), ())), preferred_element_type=jnp.float32
    )
    match = (left_id[:, None] == right_id[None, :]) & (left_id[:, None] >= 0)
    if same_block:
        count = left.shape[0]
        match = match & (jnp.arange(count)[:, None] != jnp.arange(count)[None, :])
    masked = jnp.where(match, scores, jnp.float32(-1.0))
    return (jnp.max(masked, axis=1), jnp.max(masked, axis=0))


def by_ring(embeddings, cluster_id):
    scale = lax.rsqrt(jnp.sum(embeddings * embeddings, axis=1, keepdims=True) + 1e-06)
    normed = (embeddings * scale).astype(jnp.bfloat16)
    best, unused_cols = block_max(normed, cluster_id, normed, cluster_id, True)
    visitor = (normed, cluster_id)
    for offset in range(1, SPAN):
        visitor = (shifted(visitor[0], "blk", 1), shifted(visitor[1], "blk", 1))
        row_best, col_best = block_max(normed, cluster_id, visitor[0], visitor[1], False)
        returned = shifted(col_best, "blk", -offset)
        best = jnp.maximum(best, jnp.maximum(row_best, returned))
    return best


OWN = GROUP
PACKED = ((6, 0), (7, 1, 5, OWN), (2, 3))
STEPS = ((OWN, 6, 0), (7, 1, 5), (2, 3))


def target(block, m, blocks):
    q = block % GROUP
    r = q ^ (m % GROUP)
    step = 0 if m >= GROUP else GROUP if r <= q else -GROUP
    return (block - q + r + step) % blocks


def partner(me, m, blocks, sender):
    q = lax.rem(me, GROUP)
    r = lax.bitwise_xor(q, m % GROUP)
    if m >= GROUP:
        return me - q + r
    back = (q <= r) if sender else (r > q)
    step = jnp.where(back, blocks - GROUP, GROUP)
    return lax.rem(me - q + r + step, blocks)


def send(rows, m):
    if m == OWN:
        return rows
    blocks = lax.axis_size("blk")
    return lax.ppermute(rows, "blk", [(i, target(i, m, blocks)) for i in range(blocks)])


def dot(a, b):
    return jnp.dot(a, b, preferred_element_type=jnp.float32)


def dot_rows(a, b):
    return lax.dot_general(a, b, (((1,), (1,)), ((), ())), preferred_element_type=jnp.float32)


def selection(messages, label, rank, room):
    slot = lax.broadcasted_iota(jnp.int32, (room, LANES), 0)
    rows = []
    for m in messages:
        key = jnp.where(label == m, rank, -1)
        here = [jnp.where(slot == key[s : s + 1], 1.0, 0.0) for s in range(label.shape[0])]
        rows.append(jnp.concatenate([h.astype(jnp.bfloat16) for h in here], axis=1))
    return jnp.concatenate(rows, axis=0)


def pick_rows(messages, selected, count, normed, out_refs):
    room = out_refs[0].shape[0]
    slot = lax.broadcasted_iota(jnp.int32, (room, LANES), 0)
    lane = lax.broadcasted_iota(jnp.int32, (room, LANES), 1)
    picked = dot(selected, normed)
    for i, (m, out_ref) in enumerate(zip(messages, out_refs)):
        rows = picked[i * room : (i + 1) * room]
        empty = (slot >= count[m : m + 1]) & (lane == 0)
        first = jnp.where(empty, EMPTY, rows[:, :LANES])
        out_ref[:, :LANES] = first.astype(jnp.bfloat16)
        out_ref[:, LANES:] = rows[:, LANES:].astype(jnp.bfloat16)


def pack_first_kernel(blocks, emb_ref, id_ref, *refs):
    first_refs, refs = refs[: len(PACKED[0])], refs[len(PACKED[0]) :]
    normed, label_ref, rank_ref, count_ref, over_ref, raw, selected_ref, arrived = refs
    rows, width = normed.shape
    segments = rows // LANES
    copies = []
    for s in range(segments):
        part = pl.ds(s * LANES, LANES)
        copies.append(pltpu.make_async_copy(emb_ref.at[part], raw.at[part], arrived.at[s]))
        copies[-1].start()

    me = lax.axis_index("blk")
    ids = id_ref[...]
    q = lax.rem(me, GROUP)
    offset = lax.rem(me - ids + 2 * blocks, blocks)
    turn = lax.bitwise_and(q - offset + SPAN, SPAN - 1)
    label = jnp.where(ids >= 0, lax.bitwise_xor(turn, q), SPAN)
    member = [jnp.where(label == m, 1.0, 0.0) for m in range(SPAN)]
    stacked = jnp.concatenate(member, axis=0).astype(jnp.bfloat16)
    before = lax.broadcasted_iota(jnp.int32, (LANES, LANES), 0) < lax.broadcasted_iota(
        jnp.int32, (LANES, LANES), 1
    )
    before = jnp.where(before, 1.0, 0.0).astype(jnp.bfloat16)
    ones = jnp.ones((LANES, LANES), jnp.bfloat16)
    size = SPAN * segments
    r = lax.broadcasted_iota(jnp.int32, (size, size), 0)
    c = lax.broadcasted_iota(jnp.int32, (size, size), 1)
    earlier = (lax.div(r, segments) == lax.div(c, segments)) & (c < r)
    earlier = jnp.where(earlier, 1.0, 0.0).astype(jnp.bfloat16)
    r = lax.broadcasted_iota(jnp.int32, (SPAN, size), 0)
    c = lax.broadcasted_iota(jnp.int32, (SPAN, size), 1)
    same = jnp.where(r == lax.div(c, segments), 1.0, 0.0).astype(jnp.bfloat16)
    within = dot(stacked, before)
    start = dot(dot(earlier, stacked).astype(jnp.bfloat16), ones)
    count = dot(dot(same, stacked).astype(jnp.bfloat16), ones).astype(jnp.int32)
    place = (within + start).astype(jnp.int32)
    rank = jnp.zeros_like(ids)
    for m in range(SPAN):
        rank = jnp.where(label == m, place[m * segments : (m + 1) * segments], rank)
    label_ref[...] = label
    rank_ref[...] = rank
    count_ref[...] = count
    over_ref[...] = jnp.max(jnp.where(count > first_refs[0].shape[0], 1, 0), axis=0, keepdims=True)

    selected_ref[...] = selection(PACKED[0], label, rank, first_refs[0].shape[0])
    for s in range(segments):
        part = pl.ds(s * LANES, LANES)
        copies[s].wait()
        x = raw[part]
        scale = lax.rsqrt(jnp.sum(x * x, axis=1, keepdims=True) + 1e-06)
        normed[part] = (x * scale).astype(jnp.bfloat16)

    pick_rows(PACKED[0], selected_ref[...], count, normed[...], first_refs)


def pack_first(embeddings, ids, blocks, room):
    rows, width = embeddings.shape
    segments = rows // LANES
    vmem = pl.BlockSpec(memory_space=pltpu.VMEM)
    shapes = [jax.ShapeDtypeStruct((room, width), jnp.bfloat16)] * len(PACKED[0])
    shapes += [jax.ShapeDtypeStruct((rows, width), jnp.bfloat16)]
    shapes += [jax.ShapeDtypeStruct((segments, LANES), jnp.int32)] * 2
    shapes += [jax.ShapeDtypeStruct((SPAN, LANES), jnp.int32)]
    shapes += [jax.ShapeDtypeStruct((1, LANES), jnp.int32)]
    return pl.pallas_call(
        functools.partial(pack_first_kernel, blocks),
        out_shape=shapes,
        in_specs=[pl.BlockSpec(memory_space=pl.ANY), vmem],
        out_specs=[vmem] * len(shapes),
        scratch_shapes=[
            pltpu.VMEM((rows, width), jnp.float32),
            pltpu.VMEM((len(PACKED[0]) * room, rows), jnp.bfloat16),
            pltpu.SemaphoreType.DMA((segments,)),
        ],
        compiler_params=pltpu.CompilerParams(vmem_limit_bytes=PACK_VMEM),
        cost_estimate=pl.CostEstimate(
            flops=2 * GROUP * room * rows * width, bytes_accessed=rows * width * 4, transcendentals=rows
        ),
        name="pack_first",
    )(embeddings, ids)


def pack_more_kernel(messages, normed, label_ref, rank_ref, count_ref, *out_refs):
    label, rank, count = label_ref[...], rank_ref[...], count_ref[...]
    selected = selection(messages, label, rank, out_refs[0].shape[0])
    pick_rows(messages, selected, count, normed[...], out_refs)


def pack_more(messages, room, normed, label, rank, count):
    rows, width = normed.shape
    vmem = pl.BlockSpec(memory_space=pltpu.VMEM)
    return pl.pallas_call(
        functools.partial(pack_more_kernel, messages),
        out_shape=[jax.ShapeDtypeStruct((room, width), jnp.bfloat16)] * len(messages),
        in_specs=[vmem] * 4,
        out_specs=[vmem] * len(messages),
        compiler_params=pltpu.CompilerParams(vmem_limit_bytes=PACK_VMEM),
        cost_estimate=pl.CostEstimate(
            flops=2 * len(messages) * room * rows * width, bytes_accessed=rows * width * 4, transcendentals=0
        ),
        name=f"pack_{len(messages)}",
    )(normed, label, rank, count)


def same_place(count):
    i = lax.broadcasted_iota(jnp.int32, (count, count), 0)
    j = lax.broadcasted_iota(jnp.int32, (count, count), 1)
    return i == j


def stacked(refs):
    return jnp.concatenate([ref[...] for ref in refs], axis=0)


def join(old, new, before):
    count, width = new.shape
    diagonal = same_place(count)
    unused = jnp.where(new[:, :LANES].astype(jnp.float32)[:, :1] > 1.5, -4.0, 0.0)
    scores = jnp.where(diagonal, -1.0, dot_rows(new, new) + unused)
    best = jnp.max(scores, axis=0, keepdims=True)
    if old is None:
        return None, best
    i = lax.broadcasted_iota(jnp.int32, (16, width), 0)
    j = lax.broadcasted_iota(jnp.int32, (16, width), 1)
    first = jnp.where((i == 0) & (j == 0), 1.0, 0.0).astype(jnp.bfloat16)
    scores = dot_rows(jnp.concatenate([new, first], axis=0), old)
    markers, scores = scores[count : count + 1], scores[:count]
    best_old = jnp.maximum(before, jnp.max(scores + unused, axis=0, keepdims=True))
    best_new = jnp.max(scores + jnp.where(markers > 1.5, -4.0, 0.0), axis=1, keepdims=True)
    best_new = jnp.max(jnp.where(diagonal, best_new, -4.0), axis=0, keepdims=True)
    return best_old, jnp.maximum(best, best_new)


def score_first_kernel(*refs):
    new, (over_ref, best_ref, rows_ref, passed_ref) = refs[:-4], refs[-4:]
    rows_ref[...] = stacked(new)
    best_ref[...] = join(None, rows_ref[...], None)[1]
    passed_ref[...] = over_ref[...]


def score_step_kernel(old_ref, *refs):
    new, (before_ref, best_ref, rows_ref) = refs[:-3], refs[-3:]
    olds = old_ref.shape[0]
    rows_ref[:olds] = old_ref[...]
    rows_ref[olds:] = stacked(new)
    best_old, best_new = join(old_ref[...], rows_ref[olds:], before_ref[...])
    best_ref[...] = jnp.concatenate([best_old, best_new], axis=1)


def score_step(old, new, before):
    room, width = new[0].shape
    vmem = pl.BlockSpec(memory_space=pltpu.VMEM)
    rows = len(new) * room + (0 if old is None else old.shape[0])
    args = (*new, before) if old is None else (old, *new, before)
    shapes = [jax.ShapeDtypeStruct((1, rows), jnp.float32), jax.ShapeDtypeStruct((rows, width), jnp.bfloat16)]
    if old is None:
        shapes += [jax.ShapeDtypeStruct(before.shape, before.dtype)]
    return pl.pallas_call(
        score_first_kernel if old is None else score_step_kernel,
        out_shape=shapes,
        in_specs=[vmem] * len(args),
        out_specs=[vmem] * len(shapes),
        compiler_params=pltpu.CompilerParams(vmem_limit_bytes=SCORE_VMEM),
        cost_estimate=pl.CostEstimate(
            flops=4 * len(new) * room * rows * width, bytes_accessed=rows * width * 2, transcendentals=0
        ),
        name=f"score_{rows // room}",
    )(*args)


def score_last_kernel(blocks, room, old_ref, *refs):
    new, (before_ref, over_ref, other_ref, best_ref) = refs[:-4], refs[-4:]
    me = lax.axis_index("blk")
    flag = jnp.maximum(over_ref[...], other_ref[...]).astype(jnp.float32)
    padded = best_ref.shape[2]
    best_ref[...] = jnp.concatenate([flag[None]] * (padded // LANES), axis=2) + jnp.zeros_like(best_ref)
    bests = []
    for best in join(old_ref[...], stacked(new), before_ref[...]):
        bests += [best[:, i : i + room] for i in range(0, best.shape[1], room)]
    for m, best in zip(sum(STEPS, ()), bests):
        best_ref[blocks - 1 - partner(me, m, blocks, True), :, :room] = jnp.maximum(best, -1.0)


def score_last(old, new, before, over, other, blocks):
    room, width = new[0].shape
    padded = (pl.cdiv(room, LANES) if room % LANES else room // LANES + 1) * LANES
    vmem = pl.BlockSpec(memory_space=pltpu.VMEM)
    return pl.pallas_call(
        functools.partial(score_last_kernel, blocks, room),
        out_shape=jax.ShapeDtypeStruct((blocks, 1, padded), jnp.float32),
        in_specs=[vmem] * (len(new) + 4),
        out_specs=vmem,
        compiler_params=pltpu.CompilerParams(vmem_limit_bytes=SCORE_VMEM),
        name="score_last",
    )(old, *new, before, over, other)


def unpack_kernel(blocks, best_ref, label_ref, rank_ref, out_ref, over_ref):
    label, rank = label_ref[...], rank_ref[...]
    padded = best_ref.shape[2]
    me = lax.axis_index("blk")
    inner = lax.bitwise_and(rank, LANES - 1)
    result = jnp.full(label.shape, -1.0, jnp.float32)
    for m in range(SPAN):
        best = best_ref[blocks - 1 - partner(me, m, blocks, False)]
        for start in range(0, padded, LANES):
            table = jnp.broadcast_to(best[:, start : start + LANES], label.shape)
            value = jnp.take_along_axis(table, inner, axis=1)
            here = (label == m) & (rank >= start) & (rank < start + LANES)
            result = jnp.where(here, value, result)
    out_ref[...] = result
    flags = jnp.max(best_ref[:, :, padded - LANES :], axis=0)
    over_ref[...] = jnp.roll(flags, 1, axis=1).astype(jnp.int32)


def unpack(best, label, rank):
    vmem = pl.BlockSpec(memory_space=pltpu.VMEM)
    return pl.pallas_call(
        functools.partial(unpack_kernel, best.shape[0]),
        out_shape=[
            jax.ShapeDtypeStruct(label.shape, jnp.float32),
            jax.ShapeDtypeStruct((1, LANES), jnp.int32),
        ],
        in_specs=[vmem] * 3,
        out_specs=[vmem] * 2,
        compiler_params=pltpu.CompilerParams(vmem_limit_bytes=4 * 1024 * 1024),
        name="unpack",
    )(best, label, rank)


def by_home(embeddings, cluster_id, rooms):
    blocks = lax.axis_size("blk")
    room = rooms[0]
    ids = cluster_id.reshape(-1, LANES)
    *packed, normed, label, rank, count, over = pack_first(embeddings, ids, blocks, room)
    rows = {m: send(p, m) for m, p in zip(PACKED[0], packed)}
    for messages in PACKED[1:]:
        packed = pack_more(messages, room, normed, label, rank, count)
        rows |= {m: send(p, m) for m, p in zip(messages, packed)}
    best, old, over = score_step(None, [rows[m] for m in STEPS[0]], over)
    other = over
    for distance in range(1, lax.axis_size("parts")):
        other = jnp.maximum(other, shifted(over, "parts", distance))
    for step in STEPS[1:-1]:
        best, old = score_step(old, [rows[m] for m in step], best)
    best = score_last(old, [rows[m] for m in STEPS[-1]], best, over, other, blocks)
    backward = [list(reversed(range(blocks)))]
    returned = lax.all_to_all(best, "blk", 0, 0, axis_index_groups=backward, tiled=True)
    result, flag = unpack(returned, label, rank)

    def again():
        if len(rooms) == 1:
            return by_ring(embeddings, cluster_id)
        return by_home(embeddings, cluster_id, rooms[1:])

    return lax.switch(flag[0, 0], [lambda: result.reshape(-1), again])


def local(embeddings, cluster_id):
    return by_home(embeddings, cluster_id, ROOMS)


def solution(mesh):
    in_specs = (P(("parts", "blk"), None), P(("parts", "blk")))
    out_specs = P(("parts", "blk"))
    return jax.shard_map(local, mesh=mesh, in_specs=in_specs, out_specs=out_specs, check_vma=False)
```

```python
import functools

import jax
import jax.numpy as jnp
from jax import lax
from jax.experimental import pallas as pl
from jax.experimental.pallas import tpu as pltpu
from jax.sharding import PartitionSpec as P

SPAN = 8
HOME = 4
GROUP = 4
ROOMS = (160, 256)
LANES = 128
EMPTY = 2.0
PACK_VMEM = 24 * 1024 * 1024
SCORE_VMEM = 20 * 1024 * 1024


def shifted(block, axis, distance):
    if distance == 0:
        return block
    size = lax.axis_size(axis)
    route = [(i, (i + distance) % size) for i in range(size)]
    return lax.ppermute(block, axis, route)


def block_max(left, left_id, right, right_id, same_block):
    scores = lax.dot_general(
        left, right, (((1,), (1,)), ((), ())), preferred_element_type=jnp.float32
    )
    match = (left_id[:, None] == right_id[None, :]) & (left_id[:, None] >= 0)
    if same_block:
        count = left.shape[0]
        match = match & (jnp.arange(count)[:, None] != jnp.arange(count)[None, :])
    masked = jnp.where(match, scores, jnp.float32(-1.0))
    return (jnp.max(masked, axis=1), jnp.max(masked, axis=0))


def by_ring(embeddings, cluster_id):
    scale = lax.rsqrt(jnp.sum(embeddings * embeddings, axis=1, keepdims=True) + 1e-06)
    normed = (embeddings * scale).astype(jnp.bfloat16)
    best, unused_cols = block_max(normed, cluster_id, normed, cluster_id, True)
    visitor = (normed, cluster_id)
    for offset in range(1, SPAN):
        visitor = (shifted(visitor[0], "blk", 1), shifted(visitor[1], "blk", 1))
        row_best, col_best = block_max(normed, cluster_id, visitor[0], visitor[1], False)
        returned = shifted(col_best, "blk", -offset)
        best = jnp.maximum(best, jnp.maximum(row_best, returned))
    return best


OWN = GROUP
PACKED = ((6, 0), (7, 2, 5), (1, 3, OWN))
STEPS = ((OWN, 6, 0), (7, 2, 5), (1, 3))


def target(block, m, blocks):
    q = block % GROUP
    r = q ^ (m % GROUP)
    step = 0 if m >= GROUP else GROUP if r <= q else -GROUP
    return (block - q + r + step) % blocks


def partner(me, m, blocks, sender):
    q = lax.rem(me, GROUP)
    r = lax.bitwise_xor(q, m % GROUP)
    if m >= GROUP:
        return me - q + r
    back = (q <= r) if sender else (r > q)
    step = jnp.where(back, blocks - GROUP, GROUP)
    return lax.rem(me - q + r + step, blocks)


def send(rows, m):
    if m == OWN:
        return rows
    blocks = lax.axis_size("blk")
    return lax.ppermute(rows, "blk", [(i, target(i, m, blocks)) for i in range(blocks)])


def dot(a, b):
    return jnp.dot(a, b, preferred_element_type=jnp.float32)


def dot_rows(a, b):
    return lax.dot_general(a, b, (((1,), (1,)), ((), ())), preferred_element_type=jnp.float32)


def selection(messages, label, rank, room):
    slot = lax.broadcasted_iota(jnp.int32, (room, LANES), 0)
    rows = []
    for m in messages:
        key = jnp.where(label == m, rank, -1)
        here = [jnp.where(slot == key[s : s + 1], 1.0, 0.0) for s in range(label.shape[0])]
        rows.append(jnp.concatenate([h.astype(jnp.bfloat16) for h in here], axis=1))
    return jnp.concatenate(rows, axis=0)


def pick_rows(messages, selected, count, normed, out_refs):
    room = out_refs[0].shape[0]
    slot = lax.broadcasted_iota(jnp.int32, (room, LANES), 0)
    lane = lax.broadcasted_iota(jnp.int32, (room, LANES), 1)
    picked = dot(selected, normed)
    for i, (m, out_ref) in enumerate(zip(messages, out_refs)):
        rows = picked[i * room : (i + 1) * room]
        empty = (slot >= count[m : m + 1]) & (lane == 0)
        first = jnp.where(empty, EMPTY, rows[:, :LANES])
        out_ref[:, :LANES] = first.astype(jnp.bfloat16)
        out_ref[:, LANES:] = rows[:, LANES:].astype(jnp.bfloat16)


def pack_first_kernel(blocks, emb_ref, id_ref, *refs):
    first_refs, refs = refs[: len(PACKED[0])], refs[len(PACKED[0]) :]
    normed, label_ref, rank_ref, count_ref, over_ref, raw, selected_ref, arrived = refs
    rows, width = normed.shape
    segments = rows // LANES
    copies = []
    for s in range(segments):
        part = pl.ds(s * LANES, LANES)
        copies.append(pltpu.make_async_copy(emb_ref.at[part], raw.at[part], arrived.at[s]))
        copies[-1].start()

    me = lax.axis_index("blk")
    ids = id_ref[...]
    q = lax.rem(me, GROUP)
    offset = lax.rem(me - ids + 2 * blocks, blocks)
    turn = lax.bitwise_and(q - offset + SPAN, SPAN - 1)
    label = jnp.where(ids >= 0, lax.bitwise_xor(turn, q), SPAN)
    member = [jnp.where(label == m, 1.0, 0.0) for m in range(SPAN)]
    stacked = jnp.concatenate(member, axis=0).astype(jnp.bfloat16)
    before = lax.broadcasted_iota(jnp.int32, (LANES, LANES), 0) < lax.broadcasted_iota(
        jnp.int32, (LANES, LANES), 1
    )
    before = jnp.where(before, 1.0, 0.0).astype(jnp.bfloat16)
    ones = jnp.ones((LANES, LANES), jnp.bfloat16)
    size = SPAN * segments
    r = lax.broadcasted_iota(jnp.int32, (size, size), 0)
    c = lax.broadcasted_iota(jnp.int32, (size, size), 1)
    earlier = (lax.div(r, segments) == lax.div(c, segments)) & (c < r)
    earlier = jnp.where(earlier, 1.0, 0.0).astype(jnp.bfloat16)
    r = lax.broadcasted_iota(jnp.int32, (SPAN, size), 0)
    c = lax.broadcasted_iota(jnp.int32, (SPAN, size), 1)
    same = jnp.where(r == lax.div(c, segments), 1.0, 0.0).astype(jnp.bfloat16)
    within = dot(stacked, before)
    start = dot(dot(earlier, stacked).astype(jnp.bfloat16), ones)
    count = dot(dot(same, stacked).astype(jnp.bfloat16), ones).astype(jnp.int32)
    place = (within + start).astype(jnp.int32)
    rank = jnp.zeros_like(ids)
    for m in range(SPAN):
        rank = jnp.where(label == m, place[m * segments : (m + 1) * segments], rank)
    label_ref[...] = label
    rank_ref[...] = rank
    count_ref[...] = count
    over_ref[...] = jnp.max(jnp.where(count > first_refs[0].shape[0], 1, 0), axis=0, keepdims=True)

    selected_ref[...] = selection(PACKED[0], label, rank, first_refs[0].shape[0])
    for s in range(segments):
        part = pl.ds(s * LANES, LANES)
        copies[s].wait()
        x = raw[part]
        scale = lax.rsqrt(jnp.sum(x * x, axis=1, keepdims=True) + 1e-06)
        normed[part] = (x * scale).astype(jnp.bfloat16)

    pick_rows(PACKED[0], selected_ref[...], count, normed[...], first_refs)


def pack_first(embeddings, ids, blocks, room):
    rows, width = embeddings.shape
    segments = rows // LANES
    vmem = pl.BlockSpec(memory_space=pltpu.VMEM)
    shapes = [jax.ShapeDtypeStruct((room, width), jnp.bfloat16)] * len(PACKED[0])
    shapes += [jax.ShapeDtypeStruct((rows, width), jnp.bfloat16)]
    shapes += [jax.ShapeDtypeStruct((segments, LANES), jnp.int32)] * 2
    shapes += [jax.ShapeDtypeStruct((SPAN, LANES), jnp.int32)]
    shapes += [jax.ShapeDtypeStruct((1, LANES), jnp.int32)]
    return pl.pallas_call(
        functools.partial(pack_first_kernel, blocks),
        out_shape=shapes,
        in_specs=[pl.BlockSpec(memory_space=pl.ANY), vmem],
        out_specs=[vmem] * len(shapes),
        scratch_shapes=[
            pltpu.VMEM((rows, width), jnp.float32),
            pltpu.VMEM((len(PACKED[0]) * room, rows), jnp.bfloat16),
            pltpu.SemaphoreType.DMA((segments,)),
        ],
        compiler_params=pltpu.CompilerParams(vmem_limit_bytes=PACK_VMEM),
        cost_estimate=pl.CostEstimate(
            flops=2 * GROUP * room * rows * width, bytes_accessed=rows * width * 4, transcendentals=rows
        ),
        name="pack_first",
    )(embeddings, ids)


def pack_more_kernel(messages, normed, label_ref, rank_ref, count_ref, *out_refs):
    label, rank, count = label_ref[...], rank_ref[...], count_ref[...]
    selected = selection(messages, label, rank, out_refs[0].shape[0])
    pick_rows(messages, selected, count, normed[...], out_refs)


def pack_more(messages, room, normed, label, rank, count):
    rows, width = normed.shape
    vmem = pl.BlockSpec(memory_space=pltpu.VMEM)
    return pl.pallas_call(
        functools.partial(pack_more_kernel, messages),
        out_shape=[jax.ShapeDtypeStruct((room, width), jnp.bfloat16)] * len(messages),
        in_specs=[vmem] * 4,
        out_specs=[vmem] * len(messages),
        compiler_params=pltpu.CompilerParams(vmem_limit_bytes=PACK_VMEM),
        cost_estimate=pl.CostEstimate(
            flops=2 * len(messages) * room * rows * width, bytes_accessed=rows * width * 4, transcendentals=0
        ),
        name=f"pack_{len(messages)}",
    )(normed, label, rank, count)


def same_place(count):
    i = lax.broadcasted_iota(jnp.int32, (count, count), 0)
    j = lax.broadcasted_iota(jnp.int32, (count, count), 1)
    return i == j


def stacked(refs):
    return jnp.concatenate([ref[...] for ref in refs], axis=0)


def join(old, new, before):
    count, width = new.shape
    diagonal = same_place(count)
    unused = jnp.where(new[:, :LANES].astype(jnp.float32)[:, :1] > 1.5, -4.0, 0.0)
    scores = jnp.where(diagonal, -1.0, dot_rows(new, new) + unused)
    best = jnp.max(scores, axis=0, keepdims=True)
    if old is None:
        return None, best
    i = lax.broadcasted_iota(jnp.int32, (16, width), 0)
    j = lax.broadcasted_iota(jnp.int32, (16, width), 1)
    first = jnp.where((i == 0) & (j == 0), 1.0, 0.0).astype(jnp.bfloat16)
    scores = dot_rows(jnp.concatenate([new, first], axis=0), old)
    markers, scores = scores[count : count + 1], scores[:count]
    best_old = jnp.maximum(before, jnp.max(scores + unused, axis=0, keepdims=True))
    best_new = jnp.max(scores + jnp.where(markers > 1.5, -4.0, 0.0), axis=1, keepdims=True)
    best_new = jnp.max(jnp.where(diagonal, best_new, -4.0), axis=0, keepdims=True)
    return best_old, jnp.maximum(best, best_new)


def score_first_kernel(*refs):
    new, (over_ref, best_ref, rows_ref, passed_ref) = refs[:-4], refs[-4:]
    rows_ref[...] = stacked(new)
    best_ref[...] = join(None, rows_ref[...], None)[1]
    passed_ref[...] = over_ref[...]


def score_step_kernel(old_ref, *refs):
    new, (before_ref, best_ref, rows_ref) = refs[:-3], refs[-3:]
    olds = old_ref.shape[0]
    rows_ref[:olds] = old_ref[...]
    rows_ref[olds:] = stacked(new)
    best_old, best_new = join(old_ref[...], rows_ref[olds:], before_ref[...])
    best_ref[...] = jnp.concatenate([best_old, best_new], axis=1)


def score_step(old, new, before):
    room, width = new[0].shape
    vmem = pl.BlockSpec(memory_space=pltpu.VMEM)
    rows = len(new) * room + (0 if old is None else old.shape[0])
    args = (*new, before) if old is None else (old, *new, before)
    shapes = [jax.ShapeDtypeStruct((1, rows), jnp.float32), jax.ShapeDtypeStruct((rows, width), jnp.bfloat16)]
    if old is None:
        shapes += [jax.ShapeDtypeStruct(before.shape, before.dtype)]
    return pl.pallas_call(
        score_first_kernel if old is None else score_step_kernel,
        out_shape=shapes,
        in_specs=[vmem] * len(args),
        out_specs=[vmem] * len(shapes),
        compiler_params=pltpu.CompilerParams(vmem_limit_bytes=SCORE_VMEM),
        cost_estimate=pl.CostEstimate(
            flops=4 * len(new) * room * rows * width, bytes_accessed=rows * width * 2, transcendentals=0
        ),
        name=f"score_{rows // room}",
    )(*args)


def score_last_kernel(blocks, room, old_ref, *refs):
    new, (before_ref, over_ref, other_ref, best_ref) = refs[:-4], refs[-4:]
    me = lax.axis_index("blk")
    flag = jnp.maximum(over_ref[...], other_ref[...]).astype(jnp.float32)
    padded = best_ref.shape[2]
    best_ref[...] = jnp.concatenate([flag[None]] * (padded // LANES), axis=2) + jnp.zeros_like(best_ref)
    bests = []
    for best in join(old_ref[...], stacked(new), before_ref[...]):
        bests += [best[:, i : i + room] for i in range(0, best.shape[1], room)]
    for m, best in zip(sum(STEPS, ()), bests):
        best_ref[blocks - 1 - partner(me, m, blocks, True), :, :room] = jnp.maximum(best, -1.0)


def score_last(old, new, before, over, other, blocks):
    room, width = new[0].shape
    padded = (pl.cdiv(room, LANES) if room % LANES else room // LANES + 1) * LANES
    vmem = pl.BlockSpec(memory_space=pltpu.VMEM)
    return pl.pallas_call(
        functools.partial(score_last_kernel, blocks, room),
        out_shape=jax.ShapeDtypeStruct((blocks, 1, padded), jnp.float32),
        in_specs=[vmem] * (len(new) + 4),
        out_specs=vmem,
        compiler_params=pltpu.CompilerParams(vmem_limit_bytes=SCORE_VMEM),
        name="score_last",
    )(old, *new, before, over, other)


def unpack_kernel(blocks, best_ref, label_ref, rank_ref, out_ref, over_ref):
    label, rank = label_ref[...], rank_ref[...]
    padded = best_ref.shape[2]
    me = lax.axis_index("blk")
    inner = lax.bitwise_and(rank, LANES - 1)
    result = jnp.full(label.shape, -1.0, jnp.float32)
    for m in range(SPAN):
        best = best_ref[blocks - 1 - partner(me, m, blocks, False)]
        for start in range(0, padded, LANES):
            table = jnp.broadcast_to(best[:, start : start + LANES], label.shape)
            value = jnp.take_along_axis(table, inner, axis=1)
            here = (label == m) & (rank >= start) & (rank < start + LANES)
            result = jnp.where(here, value, result)
    out_ref[...] = result
    flags = jnp.max(best_ref[:, :, padded - LANES :], axis=0)
    over_ref[...] = jnp.roll(flags, 1, axis=1).astype(jnp.int32)


def unpack(best, label, rank):
    vmem = pl.BlockSpec(memory_space=pltpu.VMEM)
    return pl.pallas_call(
        functools.partial(unpack_kernel, best.shape[0]),
        out_shape=[
            jax.ShapeDtypeStruct(label.shape, jnp.float32),
            jax.ShapeDtypeStruct((1, LANES), jnp.int32),
        ],
        in_specs=[vmem] * 3,
        out_specs=[vmem] * 2,
        compiler_params=pltpu.CompilerParams(vmem_limit_bytes=4 * 1024 * 1024),
        name="unpack",
    )(best, label, rank)


def by_home(embeddings, cluster_id, rooms):
    blocks = lax.axis_size("blk")
    room = rooms[0]
    ids = cluster_id.reshape(-1, LANES)
    *packed, normed, label, rank, count, over = pack_first(embeddings, ids, blocks, room)
    rows = {m: send(p, m) for m, p in zip(PACKED[0], packed)}
    for messages in PACKED[1:]:
        packed = pack_more(messages, room, normed, label, rank, count)
        rows |= {m: send(p, m) for m, p in zip(messages, packed)}
    best, old, over = score_step(None, [rows[m] for m in STEPS[0]], over)
    other = over
    for distance in range(1, lax.axis_size("parts")):
        other = jnp.maximum(other, shifted(over, "parts", distance))
    for step in STEPS[1:-1]:
        best, old = score_step(old, [rows[m] for m in step], best)
    best = score_last(old, [rows[m] for m in STEPS[-1]], best, over, other, blocks)
    backward = [list(reversed(range(blocks)))]
    returned = lax.all_to_all(best, "blk", 0, 0, axis_index_groups=backward, tiled=True)
    result, flag = unpack(returned, label, rank)

    def again():
        if len(rooms) == 1:
            return by_ring(embeddings, cluster_id)
        return by_home(embeddings, cluster_id, rooms[1:])

    return lax.switch(flag[0, 0], [lambda: result.reshape(-1), again])


def local(embeddings, cluster_id):
    return by_home(embeddings, cluster_id, ROOMS)


def solution(mesh):
    in_specs = (P(("parts", "blk"), None), P(("parts", "blk")))
    out_specs = P(("parts", "blk"))
    return jax.shard_map(local, mesh=mesh, in_specs=in_specs, out_specs=out_specs, check_vma=False)
```
